256 devices in a mesh: gx: 64 (over y, z, x_lo), gy: 4 (over x_hi, core).
Axes of the slice: x: 4 (x_hi: 2, x_lo: 2; x = x_hi * 2 + x_lo), y: 4, z: 8, core: 2. Of those that a mesh axis runs over, the one named last changes fastest.
Arguments:
- features: bfloat16 [524288, 128], P(('gx', 'gy')), may hold values from -6 to 6
- cotangent: bfloat16 [524288, 128], P(('gx', 'gy')), may hold values from -6 to 6
- kernel: bfloat16 [27, 128, 128], replicated, may hold values from -0.109375 to 0.109375
- block_count: int32 [256], P(('gx', 'gy')), may hold values from 8 to 32, as said below
- neighbours: int32 [8192, 27], P(('gx', 'gy')), may hold values from 0 to 72, as said below
- send_face: int32 [256, 4, 8], P(('gx', 'gy')), may hold values from 0 to 31, as said below
- send_corner: int32 [256, 4, 2], P(('gx', 'gy')), may hold values from 0 to 31, as said below
Outputs:
- conv_out: bfloat16 [524288, 128], P(('gx', 'gy'))
- input_grad: bfloat16 [524288, 128], P(('gx', 'gy'))
- kernel_grad: float32 [27, 128, 128], replicated
The draws below stay inside these ranges and needn't reach their ends.
Inputs may be any that keep to these rules, and one draw needn't show every extreme that they name: `block_count`: live blocks of each device; in every draw some device has all 32 live. `neighbours`: entries index the device's extended table (own blocks 0 to 31, the zero block 32, then the face and corner blocks in the order of the steps). Entry 13 of a live block names the block itself; every entry of a block at or past the device's block count is 32; an own block that is named is live. A face block from x-1 (x+1) is named only at offsets with ox = -1 (+1), one from y-1 (y+1) only where oy = -1 (+1), a corner block only where (ox, oy) is its corner. `send_face`: each list holds 8 distinct live blocks of its device. `send_corner`: each list holds 2 distinct live blocks of its device.
All inputs are finite; a program needn't handle non-finite values.
Results may differ from the reference program's by a relative error of at most 0.0025.
Values may be sent and summed in bfloat16 or wider, within the bound.
A program may use at most 64 MiB of HBM per device.

```python
import math
import jax
import jax.numpy as jnp
from jax import lax

C = 128
NB = 32
HF = 8
HC = 2
VOXELS = 524288
N_GX = 64
N_GY = 4


def live_counts(key):
    grid_size = N_GX * N_GY
    counts = jax.random.randint(jax.random.fold_in(key, 101), (grid_size,), NB // 4, NB + 1)
    fullest = jax.random.randint(jax.random.fold_in(key, 102), (), 0, grid_size)
    return jnp.where(jnp.arange(grid_size) == fullest, NB, counts).astype(jnp.int32)


def one_order(subkey):
    return jax.random.permutation(subkey, NB)


def block_lists(key, counts, length):
    grid_size = N_GX * N_GY
    subkeys = jax.random.split(key, grid_size * 4)
    orders = jax.vmap(one_order)(subkeys).reshape(grid_size, 4, NB)
    block_rank = jnp.arange(NB)[None, None, :]
    scores = jnp.where(block_rank < counts[:, None, None], orders, NB + orders)
    chosen = jnp.argsort(scores, axis=-1, stable=True)[:, :, :length]
    return chosen.astype(jnp.int32)


def draw_block_count(key, part):
    return live_counts(key)


def draw_send_face(key, part):
    counts = live_counts(key)
    key = jax.random.fold_in(key, 7)
    return block_lists(key, counts, HF)


def draw_send_corner(key, part):
    counts = live_counts(key)
    key = jax.random.fold_in(key, 8)
    return block_lists(key, counts, HC)


def draw_neighbours(key, part):
    counts = live_counts(key)
    key = jax.random.fold_in(key, 9)
    grid_size = N_GX * N_GY
    full_shape = (grid_size, NB, 27)
    subkeys = jax.random.split(key, 5)
    kind_pick = jax.random.randint(subkeys[0], full_shape, 0, 4)
    own_pick = jax.random.randint(subkeys[1], full_shape, 0, 1 << 20) % counts[:, None, None]
    face_pick = jax.random.randint(subkeys[2], full_shape, 0, HF)
    corner_pick = jax.random.randint(subkeys[3], full_shape, 0, HC)
    side_pick = jax.random.randint(subkeys[4], full_shape, 0, 3)
    offset = jnp.arange(27)
    step_x = offset // 9 - 1
    step_y = offset // 3 % 3 - 1
    face_x = NB + 1 + jnp.where(step_x < 0, 0, 1) * HF + face_pick
    face_y = NB + 1 + (2 + jnp.where(step_y < 0, 0, 1)) * HF + face_pick
    corner_slot = jnp.where(step_x < 0, 0, 2) + jnp.where(step_y < 0, 0, 1)
    corner_entry = NB + 1 + 4 * HF + corner_slot * HC + corner_pick
    corner_site = (step_x != 0) & (step_y != 0)
    diagonal_pick = jnp.where(side_pick == 0, face_x, jnp.where(side_pick == 1, face_y, corner_entry))
    straight_pick = jnp.where(step_x != 0, face_x, jnp.where(step_y != 0, face_y, own_pick))
    halo_pick = jnp.where(corner_site, diagonal_pick, straight_pick)
    entries = jnp.where(kind_pick == 0, NB, jnp.where(kind_pick == 1, own_pick, halo_pick))
    block_ids = jnp.arange(NB)[None, :, None]
    entries = jnp.where(offset == 13, block_ids, entries)
    entries = jnp.where(block_ids < counts[:, None, None], entries, NB)
    return entries.reshape(grid_size * NB, 27).astype(jnp.int32)


def block_levels(own_key, extent, pieces, least, largest):
    gain = 1.0
    for axis_at, blocks in pieces:
        draws = jax.random.uniform(jax.random.fold_in(jax.random.fold_in(own_key, 6), axis_at), (blocks,), jnp.float32, least / len(pieces), largest / len(pieces))
        gain = gain * jnp.repeat(jnp.exp(draws), extent[axis_at] // blocks).reshape((-1,) + (1,) * (len(extent) - 1 - axis_at))
    return gain


def bell_draw(rng, extent, width, most, cuts=(), held_as=jnp.bfloat16):
    drawn = jax.random.normal(rng, extent, jnp.float32) * width
    if len(cuts) > 0:
        drawn = block_levels(rng, extent, cuts, -0.22, 0.18) * drawn
    return jnp.clip(drawn, min=-most, max=most).astype(held_as)


def setup_inputs(seed: int = 0) -> dict:
    arg_keys = jax.random.split(jax.random.key(seed), 8)
    return {
        "features": bell_draw(arg_keys[0], (VOXELS, C), 1.0, 6.0, ((0, 256),)),
        "cotangent": bell_draw(arg_keys[1], (VOXELS, C), 1.0, 6.0, ((0, 256),)),
        "kernel": bell_draw(arg_keys[2], (27, C, C), (27 * C) ** -0.5, 0.109375),
        "block_count": draw_block_count(jax.random.fold_in(arg_keys[7], 71), 0),
        "neighbours": draw_neighbours(jax.random.fold_in(arg_keys[7], 71), 0),
        "send_face": draw_send_face(jax.random.fold_in(arg_keys[7], 71), 0),
        "send_corner": draw_send_corner(jax.random.fold_in(arg_keys[7], 71), 0),
    }


FACE_WAYS = ((-1, 0), (1, 0), (0, -1), (0, 1))
CORNER_WAYS = ((-1, -1), (-1, 1), (1, -1), (1, 1))

def gather_index(block_table):
    positions = jnp.arange(6, dtype=jnp.int32) - 1
    block_step = (positions + 4) // 4 - 1
    local_pos = positions - 4 * block_step
    slot_grid = (block_step[:, None, None] + 1) * 9 + (block_step[None, :, None] + 1) * 3 + (block_step[None, None, :] + 1)
    row_grid = local_pos[:, None, None] * 16 + local_pos[None, :, None] * 4 + local_pos[None, None, :]
    return block_table[:, slot_grid.reshape(-1)] * 64 + row_grid.reshape(-1)[None, :]

def displaced(grid_array, move_x, move_y):
    pad_width = [(1, 1), (1, 1)] + [(0, 0)] * (grid_array.ndim - 2)
    padded = jnp.pad(grid_array, pad_width)
    size_x = grid_array.shape[0]
    size_y = grid_array.shape[1]
    return padded[1 - move_x:1 - move_x + size_x, 1 - move_y:1 - move_y + size_y]

def local_pass(extended, block_table, cot_rows, live_count, kernel):
    num_blocks = block_table.shape[0]
    channels = extended.shape[1]
    row_index = gather_index(block_table)
    gathered = jnp.take(extended, row_index, axis=0).reshape(num_blocks, 6, 6, 6, channels)
    live_flag = (jnp.arange(num_blocks) < live_count).astype(jnp.float32)
    live_rows = jnp.repeat(live_flag, 64)[:, None]
    masked = cot_rows * live_rows.astype(jnp.bfloat16)
    conv_sum = jnp.zeros((num_blocks * 64, channels), jnp.float32)
    hood_grad = jnp.zeros((num_blocks, 6, 6, 6, channels), jnp.float32)
    kernel_terms = []
    for off_x in (-1, 0, 1):
        for off_y in (-1, 0, 1):
            for off_z in (-1, 0, 1):
                offset = (off_x + 1) * 9 + (off_y + 1) * 3 + off_z + 1
                shifted = gathered[:, 1 + off_x:5 + off_x, 1 + off_y:5 + off_y, 1 + off_z:5 + off_z].reshape(-1, channels)
                conv_sum = conv_sum + jnp.dot(shifted, kernel[offset], preferred_element_type=jnp.float32)
                kernel_terms.append(lax.dot_general(shifted, masked, (((0,), (0,)), ((), ())), preferred_element_type=jnp.float32))
                back_term = lax.dot_general(masked, kernel[offset], (((1,), (1,)), ((), ())), preferred_element_type=jnp.float32)
                hood_grad = hood_grad.at[:, 1 + off_x:5 + off_x, 1 + off_y:5 + off_y, 1 + off_z:5 + off_z].add(back_term.reshape(num_blocks, 4, 4, 4, channels))
    conv_rows = (conv_sum * live_rows).astype(jnp.bfloat16)
    ext_grad = jnp.zeros(extended.shape, jnp.float32).at[row_index.reshape(-1)].add(hood_grad.reshape(-1, channels))
    return (conv_rows, jnp.stack(kernel_terms), ext_grad)

def pick_blocks(chosen, owned):
    return owned[chosen]

def reference(features, cotangent, kernel, block_count, neighbours, send_face, send_corner):
    channels = features.shape[1]
    grid_size = N_GX * N_GY
    own_blocks = features.reshape(grid_size, NB, 64, channels)
    face_sent = jax.vmap(pick_blocks)(send_face.reshape(grid_size, 4 * HF), own_blocks).reshape(N_GX, N_GY, 4, HF, 64, channels)
    corner_sent = jax.vmap(pick_blocks)(send_corner.reshape(grid_size, 4 * HC), own_blocks).reshape(N_GX, N_GY, 4, HC, 64, channels)
    face_recv = jnp.stack([displaced(face_sent[:, :, slot_index ^ 1], -FACE_WAYS[slot_index][0], -FACE_WAYS[slot_index][1]) for slot_index in range(4)], axis=2).reshape(grid_size, 4 * HF, 64, channels)
    corner_recv = jnp.stack([displaced(corner_sent[:, :, 3 - slot_index], -CORNER_WAYS[slot_index][0], -CORNER_WAYS[slot_index][1]) for slot_index in range(4)], axis=2).reshape(grid_size, 4 * HC, 64, channels)

    def one_device(kernel_acc, inputs):
        owned, cot_rows, live_count, block_table, from_faces, from_corners = inputs
        zero_block = jnp.zeros((1, 64, channels), owned.dtype)
        extended = jnp.concatenate([owned, zero_block, from_faces, from_corners], 0).reshape(-1, channels)
        conv_rows, kernel_part, ext_grad = local_pass(extended, block_table, cot_rows, live_count, kernel)
        halo_grad = ext_grad[(NB + 1) * 64:].astype(jnp.bfloat16)
        return (kernel_acc + kernel_part, (conv_rows, ext_grad[:NB * 64], halo_grad))
    start_acc = jnp.zeros((27, channels, channels), jnp.float32)
    inputs = (own_blocks, cotangent.reshape(grid_size, NB * 64, channels), block_count, neighbours.reshape(grid_size, NB, 27), face_recv, corner_recv)
    kernel_sum, outputs = lax.scan(one_device, start_acc, inputs)
    conv_rows, own_grad, halo_grad = outputs
    halo_face = halo_grad[:, :4 * HF * 64].reshape(N_GX, N_GY, 4, HF, 64, channels)
    halo_corner = halo_grad[:, 4 * HF * 64:].reshape(N_GX, N_GY, 4, HC, 64, channels)
    back_face = jnp.stack([displaced(halo_face[:, :, slot_index ^ 1], -FACE_WAYS[slot_index][0], -FACE_WAYS[slot_index][1]) for slot_index in range(4)], axis=2).reshape(grid_size, 4 * HF, 64, channels)
    back_corner = jnp.stack([displaced(halo_corner[:, :, 3 - slot_index], -CORNER_WAYS[slot_index][0], -CORNER_WAYS[slot_index][1]) for slot_index in range(4)], axis=2).reshape(grid_size, 4 * HC, 64, channels)

    def assemble(inputs):
        own_part, face_ids, face_back, corner_ids, corner_back = inputs
        grad_sum = own_part.reshape(NB, 64, channels)
        grad_sum = grad_sum.at[face_ids].add(face_back.astype(jnp.float32))
        grad_sum = grad_sum.at[corner_ids].add(corner_back.astype(jnp.float32))
        return grad_sum.reshape(NB * 64, channels).astype(jnp.bfloat16)
    input_grad = lax.map(assemble, (own_grad, send_face.reshape(grid_size, 4 * HF), back_face, send_corner.reshape(grid_size, 4 * HC), back_corner))
    kernel_grad = kernel_sum * (1.0 / math.sqrt(VOXELS))
    return (conv_rows.reshape(-1, channels), input_grad.reshape(-1, channels), kernel_grad)
```

```python
import math

import jax
import jax.numpy as jnp
from jax import lax
from jax.experimental import pallas as pl
from jax.experimental.pallas import tpu as pltpu
from jax.sharding import PartitionSpec as P

MESH = pl.DeviceIdType.MESH
BF = jnp.bfloat16
F32 = jnp.float32

NX, NY, NZ = 4, 4, 8
FACE_WAYS = ((-1, 0), (1, 0), (0, -1), (0, 1))
CORNER_WAYS = ((-1, -1), (-1, 1), (1, -1), (1, 1))
WAYS = FACE_WAYS + CORNER_WAYS


def opposite(channel):
    return channel ^ 1 if channel < 4 else 11 - channel


def side(stride):
    return 0 if stride < 0 else 3


def places(local):
    if local == 0:
        return ((1, 0), (5, 1))
    if local == 3:
        return ((4, 0), (0, -1))
    return ((local + 1, 0),)


def kind(local):
    return 0 if local == 0 else (2 if local == 3 else 1)


def readers(ux, uy, uz):
    found = []
    for px, ox in places(ux):
        for py, oy in places(uy):
            for pz, oz in places(uz):
                found.append((px, py, pz, (ox + 1) * 9 + (oy + 1) * 3 + oz + 1))
    return found


def nn(a, b):
    return lax.dot_general(a, b, (((1,), (0,)), ((), ())), preferred_element_type=F32)


def nt(a, b):
    return lax.dot_general(a, b, (((1,), (1,)), ((), ())), preferred_element_type=F32)


def onehot(mask):
    return jnp.where(mask, 1.0, 0.0).astype(BF)


def iota(shape, dim):
    return lax.broadcasted_iota(jnp.int32, shape, dim)


def body(
    cnt, feat, cot, ker, tab,
    conv, igrad, kgrad,
    et, pz, gz, gt, wt, dp, de, oh, oht, bd, bdt, perm,
    hs, hr, rs, rr,
    wd, rcore, hh, r1, s1, r2, s2, r3, tt, g3, g2,
    hsem, hrem, bsem, brem, csem, crem, asem, arem, lsem,
):
    gx = lax.axis_index("gx")
    gy = lax.axis_index("gy")
    cy = gx // 16
    cz = (gx // 2) % 8
    cx = (gy // 2) * 2 + gx % 2
    core = gy % 2

    def at(x, y, z, c):
        return ((y * 8 + z) * 2 + x % 2, (x // 2) * 2 + c)

    sibling = (gx, gy // 2 * 2 + (1 - core))
    along_x = [at((cx + d) % NX, cy, cz, core) for d in range(1, NX)]
    along_y = [at(cx, (cy + d) % NY, cz, core) for d in range(1, NY)]
    along_z = [at(cx, cy, (cz + d) % NZ, core) for d in range(1, NZ)]
    halo = [(gx + wx, gy + wy) for wx, wy in WAYS]
    there = [
        (gx + wx >= 0) & (gx + wx < 64) & (gy + wy >= 0) & (gy + wy < 4) for wx, wy in WAYS
    ]

    barrier = pltpu.get_barrier_semaphore()
    greet = [sibling] + along_x + along_y + along_z
    greet += [((gx + wx + 64) % 64, (gy + wy + 4) % 4) for wx, wy in WAYS]
    for other in greet:
        pl.semaphore_signal(barrier, inc=1, device_id=other, device_id_type=MESH)

    r256, c256 = iota((256, 256), 0), iota((256, 256), 1)
    perm[...] = onehot(((r256 >> 4) == (c256 & 15)) & ((r256 & 15) == (c256 >> 4)))
    eye = onehot(iota((128, 128), 0) == iota((128, 128), 1))
    eye256 = onehot(r256 == c256)

    def swap16(v):
        return nn(perm[...], v.reshape(256, 128)).reshape(16, 16, 128)

    for hb in range(2):
        for ug in range(4):
            rows = swap16(feat[pl.ds(16 * hb, 16), pl.ds(16 * ug, 16), :])
            et[pl.ds(16 * ug, 16), pl.ds(16 * hb, 16), :] = rows.astype(BF)

    r32, c32 = iota((32, 128), 0), iota((32, 128), 1)
    same_z = (r32 >> 3) == (c32 >> 5)
    for ch in range(8):
        pick = onehot(same_z & (tab[:, 27 + ch : 28 + ch] == (c32 & 31)))
        bd[ch] = pick
        bdt[ch] = nt(eye, pick).astype(BF)

    def rim_base(ch, chunk):
        wx, wy = WAYS[ch]
        ux = side(wx) if wx != 0 else chunk
        uy = side(wy) if wy != 0 else chunk
        return ux * 16 + uy * 4

    def chunks(ch):
        return 4 if ch < 4 else 1

    for ch in range(8):
        for chunk in range(chunks(ch)):
            source = et[pl.ds(rim_base(ch, chunk), 4), pl.ds(0, 32), :].reshape(128, 128)
            hs[ch, chunk] = nn(bd[ch], source).astype(BF)

    pl.semaphore_wait(barrier, len(greet))

    def part(buf, ch):
        return buf.at[ch] if ch < 4 else buf.at[ch, pl.ds(0, 1)]

    def halo_copy(src, dst, ss, rs_, ch):
        return pltpu.make_async_remote_copy(
            src_ref=part(src, ch),
            dst_ref=part(dst, opposite(ch)),
            send_sem=ss.at[ch],
            recv_sem=rs_.at[opposite(ch)],
            device_id=halo[ch],
            device_id_type=MESH,
        )

    def halo_arrived(src, dst, ss, rs_, ch):
        return pltpu.make_async_remote_copy(
            src_ref=part(src, ch),
            dst_ref=part(dst, ch),
            send_sem=ss.at[ch],
            recv_sem=rs_.at[ch],
            device_id=halo[ch],
            device_id_type=MESH,
        )

    for ch in range(8):
        @pl.when(there[ch])
        def _():
            halo_copy(hs, hr, hsem, hrem, ch).start()

    for x in range(4):
        for hb in range(2):
            live = jnp.where(iota((16, 128), 0) + 16 * hb < cnt[0], 1.0, 0.0)
            rows = swap16(cot[pl.ds(16 * hb, 16), pl.ds(16 * x, 16), :]) * live[None]
            rows = rows.reshape(4, 2, 2, 16, 128).astype(BF)
            gz[x, :, :, pl.ds(16 * hb, 16), pl.ds(0, 128)] = rows[:, :, 0]
            gz[x, :, :, pl.ds(16 * hb, 16), pl.ds(128, 128)] = rows[:, :, 1]
        gt[:, pl.ds(256 * x, 256)] = nt(eye256, gz[x].reshape(256, 256)).astype(BF)

    def weights(j, carry):
        low, mid, high = ker[3 * j], ker[3 * j + 1], ker[3 * j + 2]
        none = jnp.zeros((128, 128), BF)
        wt[j, 0, pl.ds(0, 128), pl.ds(0, 128)] = low
        wt[j, 0, pl.ds(0, 128), pl.ds(128, 128)] = none
        wt[j, 0, pl.ds(128, 128), pl.ds(0, 128)] = mid
        wt[j, 0, pl.ds(128, 128), pl.ds(128, 128)] = low
        wt[j, 1, pl.ds(0, 128), pl.ds(0, 128)] = high
        wt[j, 1, pl.ds(0, 128), pl.ds(128, 128)] = mid
        wt[j, 1, pl.ds(128, 128), pl.ds(0, 128)] = none
        wt[j, 1, pl.ds(128, 128), pl.ds(128, 128)] = high
        return carry

    lax.fori_loop(0, 9, weights, 0)

    columns = c32 + jnp.where(c32 >= 32, 1, 0)
    for o in range(27):
        oh[o] = onehot(tab[:, o : o + 1] == columns)

    def offsets_of(tx, ty, tz):
        pick = (0, 1, 3)
        return [r[3] for r in readers(pick[tx], pick[ty], pick[tz])]

    def stacked(offsets):
        if len(offsets) == 1:
            return oh[offsets[0]]
        return jnp.concatenate([oh[o] for o in offsets], axis=0)

    for tx in range(3):
        for ty in range(3):
            for tz in range(3):
                offs = offsets_of(tx, ty, tz)
                flipped = nt(eye[:80], stacked(offs)).astype(BF)
                oht[tx * 9 + ty * 3 + tz, :, pl.ds(0, 32 * len(offs))] = flipped

    def clear(u, carry):
        et[u, pl.ds(32, 96), :] = jnp.zeros((96, 128), BF)
        return carry

    lax.fori_loop(0, 64, clear, 0)

    def clear_dp(x, carry):
        dp[x] = jnp.zeros((6, 3, 32, 256), F32)
        return carry

    lax.fori_loop(0, 6, clear_dp, 0)

    def back(j, carry):
        kx = j // 3
        ky = j % 3
        for x in range(4):
            g = gz[x].reshape(256, 256)
            for w in range(2):
                term = nt(g, wt[j, w]).reshape(4, 2, 32, 256)
                dp[x + kx, pl.ds(ky, 4), pl.ds(w, 2)] += term
        return carry

    lax.fori_loop(0, 9, back, 0)

    for ch in range(8):
        @pl.when(there[ch])
        def _():
            halo_arrived(hs, hr, hsem, hrem, ch).wait_recv()
            wx, wy = WAYS[ch]
            for chunk in range(chunks(ch)):
                ux = side(-wx) if wx != 0 else chunk
                uy = side(-wy) if wy != 0 else chunk
                got = hr[ch, chunk].astype(F32).reshape(4, 8, 128)
                none = jnp.zeros((4, 8, 128), F32)
                pair = (got, none) if ch >= 4 or ch % 2 == 0 else (none, got)
                start = 64 if ch >= 4 else 32 + 16 * (ch // 2)
                et[pl.ds(ux * 16 + uy * 4, 4), pl.ds(start, 16), :] = jnp.concatenate(
                    pair, axis=1
                ).astype(BF)

    for ux in range(4):
        for uy in range(4):
            for uz in range(4):
                found = readers(ux, uy, uz)
                rows = nn(stacked([r[3] for r in found]), et[ux * 16 + uy * 4 + uz]).astype(BF)
                for n, (px, py, p, _) in enumerate(found):
                    pz[px, py, p // 2, :, pl.ds(128 * (p % 2), 128)] = rows[32 * n : 32 * n + 32]

    mine = pl.multiple_of(64 * core, 64)
    other = pl.multiple_of(64 - 64 * core, 64)

    def core_copy(s):
        return pltpu.make_async_remote_copy(
            src_ref=wd.at[pl.ds(9 * s, 9), pl.ds(other, 64), :],
            dst_ref=rcore.at[pl.ds(9 * s, 9)],
            send_sem=csem.at[s],
            recv_sem=crem.at[s],
            device_id=sibling,
            device_id_type=MESH,
        )

    for s in range(3):
        def slab(ky, carry):
            j = 3 * s + ky
            d0 = nn(gt[...], pz[pl.ds(s, 4), pl.ds(ky, 4), pl.ds(0, 2)].reshape(1024, 256))
            d1 = nn(gt[...], pz[pl.ds(s, 4), pl.ds(ky, 4), pl.ds(1, 2)].reshape(1024, 256))
            wd[3 * j] = (d0[:128, :128] + d0[128:, 128:]).T
            wd[3 * j + 1] = (d0[:128, 128:] + d1[128:, :128]).T
            wd[3 * j + 2] = (d1[:128, :128] + d1[128:, 128:]).T
            return carry

        lax.fori_loop(0, 3, slab, 0)
        core_copy(s).start()

    def send(src, dst, n, device):
        return pltpu.make_async_remote_copy(
            src_ref=src,
            dst_ref=dst,
            send_sem=asem.at[n],
            recv_sem=arem.at[n],
            device_id=device,
            device_id_type=MESH,
        )

    for s in range(3):
        core_copy(s).wait()
        hh[pl.ds(9 * s, 9)] = wd[pl.ds(9 * s, 9), pl.ds(mine, 64), :] + rcore[pl.ds(9 * s, 9)]

    def at8(first, index):
        return pl.ds(pl.multiple_of(first + 8 * index, 8), 8)

    first = []
    for d in range(1, 4):
        first.append(send(hh.at[:, at8(0, (cx + d) % 4), :], r1.at[0, d - 1], d - 1, along_x[d - 1]))
        first.append(send(hh.at[:, at8(32, (cy + d) % 4), :], r1.at[1, d - 1], d + 2, along_y[d - 1]))
    for copy in first:
        copy.start()

    for x in range(4):
        total = jnp.zeros((256, 256), F32)
        for kx in range(3):
            for ky in range(3):
                for w in range(2):
                    rows = pz[x + kx, pl.ds(ky, 4), pl.ds(w, 2)].reshape(256, 256)
                    total = total + nn(rows, wt[3 * kx + ky, w])
        total = total.reshape(4, 2, 32, 256)
        for hb in range(2):
            live = jnp.where(iota((16, 128), 0) + 16 * hb < cnt[0], 1.0, 0.0)
            even = total[:, :, 16 * hb : 16 * hb + 16, :128] * live
            odd = total[:, :, 16 * hb : 16 * hb + 16, 128:] * live
            both = jnp.stack([even, odd], axis=2).astype(BF).reshape(16, 16, 128)
            conv[pl.ds(16 * hb, 16), pl.ds(16 * x, 16), :] = swap16(both).astype(BF)

    for copy in first:
        copy.wait()
    s1[0, pl.ds(0, 27)] = hh[:, at8(0, cx), :] + r1[0, 0] + r1[0, 1] + r1[0, 2]
    s1[1, pl.ds(0, 27)] = hh[:, at8(32, cy), :] + r1[1, 0] + r1[1, 1] + r1[1, 2]
    s1[:, pl.ds(27, 1)] = jnp.zeros((2, 1, 8, 128), F32)

    second = []
    for d in range(1, 4):
        second.append(send(s1.at[0, pl.ds(7 * ((cy + d) % 4), 7)], r2.at[0, d - 1], d + 5, along_y[d - 1]))
        second.append(send(s1.at[1, pl.ds(7 * ((cx + d) % 4), 7)], r2.at[1, d - 1], d + 8, along_x[d - 1]))
    for copy in second:
        copy.start()

    for ux in range(4):
        for uy in range(4):
            pieces = []
            for uz in range(4):
                found = readers(ux, uy, uz)
                high, low = [], []
                for px, py, p, _ in found:
                    value = dp[px, py, p // 2, :, pl.ds(128 * (p % 2), 128)]
                    top = value.astype(BF)
                    high.append(top)
                    low.append((value - top.astype(F32)).astype(BF))
                high = jnp.concatenate(high, axis=0) if len(high) > 1 else high[0]
                low = jnp.concatenate(low, axis=0) if len(low) > 1 else low[0]
                group = kind(ux) * 9 + kind(uy) * 3 + kind(uz)
                res = nn(
                    oht[group, :, pl.ds(0, 32 * len(found))],
                    jnp.concatenate([high, low], axis=1),
                )
                res = res[:, :128] + res[:, 128:]
                de[ux * 16 + uy * 4 + uz] = res[:32]
                pieces.append(res)

            def give(slot, chunk, row):
                rs[slot, chunk] = jnp.concatenate(
                    [piece[row : row + 8] for piece in pieces], axis=0
                ).astype(BF)

            for slot in range(8):
                wx, wy = WAYS[slot]
                if (wx != 0 and ux != side(-wx)) or (wy != 0 and uy != side(-wy)):
                    continue
                chunk = 0 if slot >= 4 else (uy if wx != 0 else ux)
                give(slot, chunk, 64 if slot >= 4 else 32 + 8 * slot)

    for ch in range(8):
        @pl.when(there[ch])
        def _():
            halo_copy(rs, rr, bsem, brem, ch).start()

        @pl.when(jnp.logical_not(there[ch]))
        def _():
            rr[ch] = jnp.zeros((4, 32, 128), BF)

    for copy in second:
        copy.wait()
    s2[0, pl.ds(0, 7)] = s1[0, pl.ds(7 * cy, 7)] + r2[0, 0] + r2[0, 1] + r2[0, 2]
    s2[1, pl.ds(0, 7)] = s1[1, pl.ds(7 * cx, 7)] + r2[1, 0] + r2[1, 1] + r2[1, 2]
    s2[:, pl.ds(7, 1)] = jnp.zeros((2, 1, 8, 128), F32)

    third = [
        send(s2.at[:, pl.ds((cz + d) % 8, 1)], r3.at[d - 1], 11 + d, along_z[d - 1])
        for d in range(1, 8)
    ]
    for copy in third:
        copy.start()
    for copy in third:
        copy.wait()
    whole = s2[:, pl.ds(cz, 1)]
    for d in range(7):
        whole = whole + r3[d]
    tt[...] = whole * (1.0 / math.sqrt(256 * 32 * 64))
    g3[:, pl.ds(cz, 1)] = tt[...]

    fourth = [send(tt, g3.at[:, pl.ds(cz, 1)], 18 + d, along_z[d - 1]) for d in range(1, 8)]
    for copy in fourth:
        copy.start()

    for ch in range(8):
        @pl.when(there[ch])
        def _():
            halo_arrived(rs, rr, bsem, brem, ch).wait_recv()

    for ux in range(4):
        parts = []
        for uy in range(4):
            rows = de[pl.ds(ux * 16 + uy * 4, 4)].reshape(128, 128)
            for ch in range(8):
                wx, wy = WAYS[ch]
                if (wx != 0 and ux != side(wx)) or (wy != 0 and uy != side(wy)):
                    continue
                chunk = 0 if ch >= 4 else (uy if wx != 0 else ux)
                rows = rows + nn(bdt[ch], rr[ch, chunk])
            parts.append(rows.astype(BF).reshape(4, 32, 128))
        parts = jnp.concatenate(parts, axis=0)
        for hb in range(2):
            swapped = swap16(parts[:, 16 * hb : 16 * hb + 16])
            igrad[pl.ds(16 * hb, 16), pl.ds(16 * ux, 16), :] = swapped.astype(BF)

    for copy in fourth:
        copy.wait()
    g2[0, pl.ds(7 * cy, 7)] = g3[0, pl.ds(0, 7)]
    g2[1, pl.ds(7 * cx, 7)] = g3[1, pl.ds(0, 7)]
    fifth = []
    for d in range(1, 4):
        fifth.append(send(g3.at[0, pl.ds(0, 7)], g2.at[0, pl.ds(7 * cy, 7)], 25 + d, along_y[d - 1]))
        fifth.append(send(g3.at[1, pl.ds(0, 7)], g2.at[1, pl.ds(7 * cx, 7)], 28 + d, along_x[d - 1]))
    for copy in fifth:
        copy.start()
    for copy in fifth:
        copy.wait()

    def rows_of(base, x):
        return pl.ds(pl.multiple_of(64 * core + base + 8 * x, 8), 8)

    sixth = []
    for d in range(1, 4):
        sixth.append(send(g2.at[0, pl.ds(0, 27)], kgrad.at[:, rows_of(0, cx), :], 31 + d, along_x[d - 1]))
        sixth.append(send(g2.at[1, pl.ds(0, 27)], kgrad.at[:, rows_of(32, cy), :], 34 + d, along_y[d - 1]))
    for copy in sixth:
        copy.start()
    own = []
    for n, (base, index) in enumerate(((0, cx), (32, cy))):
        rows = kgrad.at[:, rows_of(base, index), :]
        local = pltpu.make_async_copy(g2.at[n, pl.ds(0, 27)], rows, lsem.at[n])
        local.start()
        own.append(local)
        twin = send(g2.at[n, pl.ds(0, 27)], rows, 38 + n, sibling)
        twin.start()
        own.append(twin)
    last = []
    for n in range(6):
        sixth[n].wait()
        d = n // 2 + 1
        base, index = ((0, (cx + 4 - d) % 4), (32, (cy + 4 - d) % 4))[n % 2]
        rows = kgrad.at[:, rows_of(base, index), :]
        forward = send(rows, rows, 40 + n, sibling)
        forward.start()
        last.append(forward)
    for copy in own + last:
        copy.wait()

    for ch in range(8):
        @pl.when(there[ch])
        def _():
            halo_copy(hs, hr, hsem, hrem, ch).wait_send()
            halo_copy(rs, rr, bsem, brem, ch).wait_send()


def per_device(features, cotangent, kernel, block_count, neighbours, send_face, send_corner):
    face = jnp.tile(send_face[0].T, (4, 1))
    slot = jnp.arange(8)[:, None] // 2 == 3 - jnp.arange(4)[None, :]
    corner = jnp.where(slot, jnp.tile(send_corner[0].T, (4, 1)), -1)
    table = jnp.concatenate([neighbours, face, jnp.tile(corner, (4, 1))], axis=1)
    vmem = pl.BlockSpec(memory_space=pltpu.VMEM)
    dma = pltpu.SemaphoreType.DMA
    conv, igrad, kgrad = pl.pallas_call(
        body,
        out_shape=(
            jax.ShapeDtypeStruct((32, 64, 128), BF),
            jax.ShapeDtypeStruct((32, 64, 128), BF),
            jax.ShapeDtypeStruct((27, 128, 128), F32),
        ),
        in_specs=[pl.BlockSpec(memory_space=pltpu.SMEM)] + [vmem] * 4,
        out_specs=(vmem, vmem, pl.BlockSpec(memory_space=pl.ANY)),
        scratch_shapes=[
            pltpu.VMEM((64, 128, 128), BF),
            pltpu.VMEM((6, 6, 3, 32, 256), BF),
            pltpu.VMEM((4, 4, 2, 32, 256), BF),
            pltpu.VMEM((256, 1024), BF),
            pltpu.VMEM((9, 2, 256, 256), BF),
            pltpu.VMEM((6, 6, 3, 32, 256), F32),
            pltpu.VMEM((64, 32, 128), F32),
            pltpu.VMEM((27, 32, 128), BF),
            pltpu.VMEM((27, 80, 256), BF),
            pltpu.VMEM((8, 32, 128), BF),
            pltpu.VMEM((8, 128, 32), BF),
            pltpu.VMEM((256, 256), BF),
            pltpu.VMEM((8, 4, 32, 128), BF),
            pltpu.VMEM((8, 4, 32, 128), BF),
            pltpu.VMEM((8, 4, 32, 128), BF),
            pltpu.VMEM((8, 4, 32, 128), BF),
            pltpu.VMEM((27, 128, 128), F32),
            pltpu.VMEM((27, 64, 128), F32),
            pltpu.VMEM((27, 64, 128), F32),
            pltpu.VMEM((2, 3, 27, 8, 128), F32),
            pltpu.VMEM((2, 28, 8, 128), F32),
            pltpu.VMEM((2, 3, 7, 8, 128), F32),
            pltpu.VMEM((2, 8, 8, 128), F32),
            pltpu.VMEM((7, 2, 1, 8, 128), F32),
            pltpu.VMEM((2, 1, 8, 128), F32),
            pltpu.VMEM((2, 8, 8, 128), F32),
            pltpu.VMEM((2, 28, 8, 128), F32),
            dma((8,)), dma((8,)), dma((8,)), dma((8,)),
            dma((3,)), dma((3,)), dma((46,)), dma((46,)), dma((2,)),
        ],
        compiler_params=pltpu.CompilerParams(
            collective_id=0, has_side_effects=True, vmem_limit_bytes=48 * 1024 * 1024
        ),
        cost_estimate=pl.CostEstimate(
            flops=7_000_000_000, bytes_accessed=6_000_000, transcendentals=0
        ),
    )(
        block_count,
        features.reshape(32, 64, 128),
        cotangent.reshape(32, 64, 128),
        kernel,
        table,
    )
    return conv.reshape(2048, 128), igrad.reshape(2048, 128), kgrad


def solution(mesh):
    in_specs = (
        P(("gx", "gy"), None),
        P(("gx", "gy"), None),
        P(),
        P(("gx", "gy")),
        P(("gx", "gy"), None),
        P(("gx", "gy"), None, None),
        P(("gx", "gy"), None, None),
    )
    out_specs = (P(("gx", "gy"), None), P(("gx", "gy"), None), P())
    return jax.shard_map(
        per_device, mesh=mesh, in_specs=in_specs, out_specs=out_specs, check_vma=False
    )
```

```python
import math

import jax
import jax.numpy as jnp
from jax import lax
from jax.experimental import pallas as pl
from jax.experimental.pallas import tpu as pltpu
from jax.sharding import PartitionSpec as P

MESH = pl.DeviceIdType.MESH
BF = jnp.bfloat16
F32 = jnp.float32

NX, NY, NZ = 4, 4, 8
FACE_WAYS = ((-1, 0), (1, 0), (0, -1), (0, 1))
CORNER_WAYS = ((-1, -1), (-1, 1), (1, -1), (1, 1))
WAYS = FACE_WAYS + CORNER_WAYS


RUNS = (
    ((0, 0, 5), (5, 0, 4)),
    ((9, 5, 4), (13, 4, 5)),
    ((18, 9, 5), (23, 9, 4)),
)


def opposite(channel):
    return channel ^ 1 if channel < 4 else 11 - channel


def side(stride):
    return 0 if stride < 0 else 3


def places(local):
    if local == 0:
        return ((1, 0), (5, 1))
    if local == 3:
        return ((4, 0), (0, -1))
    return ((local + 1, 0),)


def kind(local):
    return 0 if local == 0 else (2 if local == 3 else 1)


def readers(ux, uy, uz):
    found = []
    for px, ox in places(ux):
        for py, oy in places(uy):
            for pz, oz in places(uz):
                found.append((px, py, pz, (ox + 1) * 9 + (oy + 1) * 3 + oz + 1))
    return found


def nn(a, b):
    return lax.dot_general(a, b, (((1,), (0,)), ((), ())), preferred_element_type=F32)


def nt(a, b):
    return lax.dot_general(a, b, (((1,), (1,)), ((), ())), preferred_element_type=F32)


def onehot(mask):
    return jnp.where(mask, 1.0, 0.0).astype(BF)


def iota(shape, dim):
    return lax.broadcasted_iota(jnp.int32, shape, dim)


def body(
    cnt, face, corner, feat_in, cot_in, ker_in, near_in,
    conv_out, igrad_out, kg,
    feat, cot, ker, near, conv, igrad,
    et, pz, gz, gt, gty, wt, di, dp, de, oh, oht, bd, bdt, co, perm, pair_perm, part_perm,
    hs, hr, rs, rr,
    wd, rcore, hh, r1, s1, r2, s2, r3, tt, g3, g2,
    isem, osem, hsem, hrem, bsem, brem, csem, crem, asem, arem,
):
    loads = [
        pltpu.make_async_copy(src, dst, isem.at[n])
        for n, (src, dst) in enumerate(
            ((feat_in, feat), (cot_in, cot), (near_in, near), (ker_in, ker))
        )
    ]
    for copy in loads:
        copy.start()
    gx = lax.axis_index("gx")
    gy = lax.axis_index("gy")
    cy = gx // 16
    cz = (gx // 2) % 8
    cx = (gy // 2) * 2 + gx % 2
    core = gy % 2

    def at(x, y, z, c):
        return ((y * 8 + z) * 2 + x % 2, (x // 2) * 2 + c)

    sibling = (gx, gy // 2 * 2 + (1 - core))
    along_x = [at((cx + d) % NX, cy, cz, core) for d in range(1, NX)]
    along_y = [at(cx, (cy + d) % NY, cz, core) for d in range(1, NY)]
    along_z = [at(cx, cy, (cz + d) % NZ, core) for d in range(1, NZ)]
    halo = [(gx + wx, gy + wy) for wx, wy in WAYS]
    there = [
        (gx + wx >= 0) & (gx + wx < 64) & (gy + wy >= 0) & (gy + wy < 4) for wx, wy in WAYS
    ]

    barrier = pltpu.get_barrier_semaphore()
    greet = [sibling] + along_x + along_y + along_z
    greet += [((gx + wx + 64) % 64, (gy + wy + 4) % 4) for wx, wy in WAYS]
    for other in greet:
        pl.semaphore_signal(barrier, inc=1, device_id=other, device_id_type=MESH)

    r256, c256 = iota((256, 256), 0), iota((256, 256), 1)
    perm[...] = onehot(((r256 >> 4) == (c256 & 15)) & ((r256 & 15) == (c256 >> 4)))
    pair_perm[...] = onehot(c256 == (r256 & 15) * 16 + ((r256 >> 4) & 7) * 2 + (r256 >> 7))
    part_perm[...] = onehot(c256 == (r256 & 1) * 128 + ((r256 & 15) >> 1) * 16 + (r256 >> 4))
    eye = onehot(iota((128, 128), 0) == iota((128, 128), 1))
    eye256 = onehot(r256 == c256)

    def swap16(v):
        return nn(perm[...], v.reshape(256, 128)).reshape(16, 16, 128)

    r32, c32 = iota((32, 128), 0), iota((32, 128), 1)
    same_z = (r32 >> 3) == (c32 >> 5)
    for ch in range(8):
        index = jnp.full((32, 128), -1, jnp.int32)
        for n in range(8 if ch < 4 else 2):
            slot = n if ch < 4 else 2 * (opposite(ch) - 4) + n
            block = face[0, ch, n] if ch < 4 else corner[0, n, ch - 4]
            index = jnp.where((r32 & 7) == slot, block, index)
        pick = onehot(same_z & (index == (c32 & 31)))
        bd[ch] = pick
        bdt[ch] = nt(eye, pick).astype(BF)

    loads[0].wait()
    for hb in range(2):
        for ug in range(4):
            rows = swap16(feat[pl.ds(16 * hb, 16), pl.ds(16 * ug, 16), :])
            et[pl.ds(16 * ug, 16), pl.ds(16 * hb, 16), :] = rows.astype(BF)

    def rim_base(ch, chunk):
        wx, wy = WAYS[ch]
        ux = side(wx) if wx != 0 else chunk
        uy = side(wy) if wy != 0 else chunk
        return ux * 16 + uy * 4

    def chunks(ch):
        return 4 if ch < 4 else 1

    for ch in range(8):
        for chunk in range(chunks(ch)):
            source = et[pl.ds(rim_base(ch, chunk), 4), pl.ds(0, 32), :].reshape(128, 128)
            hs[ch, chunk] = nn(bd[ch], source).astype(BF)

    pl.semaphore_wait(barrier, len(greet))

    def part(buf, ch):
        return buf.at[ch] if ch < 4 else buf.at[ch, pl.ds(0, 1)]

    def halo_copy(src, dst, ss, rs_, ch):
        return pltpu.make_async_remote_copy(
            src_ref=part(src, ch),
            dst_ref=part(dst, opposite(ch)),
            send_sem=ss.at[ch],
            recv_sem=rs_.at[opposite(ch)],
            device_id=halo[ch],
            device_id_type=MESH,
        )

    def halo_arrived(src, dst, ss, rs_, ch):
        return pltpu.make_async_remote_copy(
            src_ref=part(src, ch),
            dst_ref=part(dst, ch),
            send_sem=ss.at[ch],
            recv_sem=rs_.at[ch],
            device_id=halo[ch],
            device_id_type=MESH,
        )

    for ch in range(8):
        @pl.when(there[ch])
        def _():
            halo_copy(hs, hr, hsem, hrem, ch).start()

    lives = [jnp.where(iota((16, 128), 0) + 16 * hb < cnt[0], 1.0, 0.0) for hb in range(2)]
    loads[1].wait()
    for x in range(4):
        for hb in range(2):
            rows = cot[pl.ds(16 * hb, 16), pl.ds(16 * x, 16), :].reshape(256, 128)
            rows = nn(pair_perm[...], rows).reshape(2, 4, 2, 16, 128) * lives[hb]
            for n in range(2):
                gz[x, :, :, pl.ds(16 * hb, 16), pl.ds(128 * n, 128)] = rows[n].astype(BF)
        turned = nt(eye256, gz[x].reshape(256, 256))
        place = pl.ds(256 * x, 256)
        gt[0, :, place] = jnp.where(c256 < 64, 0.0, turned).astype(BF)
        gt[1, :, place] = turned.astype(BF)
        gt[2, :, place] = jnp.where(c256 < 192, turned, 0.0).astype(BF)
    for n, y in enumerate((0, 3)):
        gty[n] = nt(eye256, gz[:, y].reshape(256, 256)).astype(BF)

    loads[2].wait()
    columns = c32 + jnp.where(c32 >= 32, 1, 0)
    for o in range(27):
        oh[o] = onehot(near[:, o : o + 1] == columns)

    def offsets_of(tx, ty, tz):
        pick = (0, 1, 3)
        return [r[3] for r in readers(pick[tx], pick[ty], pick[tz])]

    def stacked(offsets):
        if len(offsets) == 1:
            return oh[offsets[0]]
        return jnp.concatenate([oh[o] for o in offsets], axis=0)

    def clear(u, carry):
        et[u, pl.ds(32, 96), :] = jnp.zeros((96, 128), BF)
        return carry

    lax.fori_loop(0, 64, clear, 0)

    def inner(found):
        return [r for r in found if 1 <= r[0] <= 4 and 1 <= r[1] <= 4]

    def outer(found):
        return [r for r in found if not (1 <= r[0] <= 4 and 1 <= r[1] <= 4)]

    def keep(rows, found):
        for n, (px, py, p, _) in enumerate(found):
            pz[px, py, p // 2, :, pl.ds(128 * (p % 2), 128)] = rows[32 * n : 32 * n + 32]

    for py in (0, 5):
        pz[pl.ds(1, 4), py] = jnp.zeros((4, 3, 32, 256), BF)
    for ux in range(4):
        for uy in range(4):
            for uz in range(4):
                found = inner(readers(ux, uy, uz))
                picks = stacked([r[3] for r in found])[:, :32]
                keep(nn(picks, et[ux * 16 + uy * 4 + uz, pl.ds(0, 32)]).astype(BF), found)

    def blocks_of(d0, d1):
        return (
            d0[:128, :128] + d0[128:, 128:],
            d0[:128, 128:] + d1[128:, :128],
            d1[:128, :128] + d1[128:, 128:],
        )

    for kx in range(3):
        x0, x1 = ((1, 4), (0, 4), (0, 3))[kx]
        for ky in range(3):
            left = gt[ky, :, pl.ds(256 * x0, 256 * (x1 - x0))]
            sums = [
                nn(
                    left,
                    pz[pl.ds(x0 + kx, x1 - x0), pl.ds(ky, 4), pl.ds(w, 2)].reshape(-1, 256),
                )
                for w in range(2)
            ]
            for n, value in enumerate(blocks_of(*sums)):
                if kx == 1 and ky == 1:
                    wd[9 * kx + 3 * ky + n] = value.T
                else:
                    di[9 * kx + 3 * ky + n] = value

    for ch in range(8):
        @pl.when(there[ch])
        def _():
            halo_arrived(hs, hr, hsem, hrem, ch).wait_recv()
            wx, wy = WAYS[ch]
            for chunk in range(chunks(ch)):
                ux = side(-wx) if wx != 0 else chunk
                uy = side(-wy) if wy != 0 else chunk
                got = hr[ch, chunk].astype(F32).reshape(4, 8, 128)
                none = jnp.zeros((4, 8, 128), F32)
                pair = (got, none) if ch >= 4 or ch % 2 == 0 else (none, got)
                start = 64 if ch >= 4 else 32 + 16 * (ch // 2)
                et[pl.ds(ux * 16 + uy * 4, 4), pl.ds(start, 16), :] = jnp.concatenate(
                    pair, axis=1
                ).astype(BF)

    for ux in range(4):
        for uy in range(4):
            for uz in range(4):
                found = outer(readers(ux, uy, uz))
                if found:
                    picks = stacked([r[3] for r in found])
                    keep(nn(picks, et[ux * 16 + uy * 4 + uz]).astype(BF), found)

    mine = pl.multiple_of(64 * core, 64)
    other = pl.multiple_of(64 - 64 * core, 64)

    def core_copy(s):
        return pltpu.make_async_remote_copy(
            src_ref=wd.at[pl.ds(9 * s, 9), pl.ds(other, 64), :],
            dst_ref=rcore.at[pl.ds(9 * s, 9)],
            send_sem=csem.at[s],
            recv_sem=crem.at[s],
            device_id=sibling,
            device_id_type=MESH,
        )

    def send(src, dst, n, device):
        return pltpu.make_async_remote_copy(
            src_ref=src,
            dst_ref=dst,
            send_sem=asem.at[n],
            recv_sem=arem.at[n],
            device_id=device,
            device_id_type=MESH,
        )

    def sixteen(first, index):
        return pl.ds(pl.multiple_of(first + 16 * index, 16), 16)

    def quarter(index):
        return pl.ds(4 * index, 4)

    first = []

    def core_sum(s):
        core_copy(s).wait()
        hh[pl.ds(9 * s, 9)] = wd[pl.ds(9 * s, 9), pl.ds(mine, 64), :] + rcore[pl.ds(9 * s, 9)]
        for n, (matrix, slot, count) in enumerate(RUNS[s]):
            for d in range(1, 4):
                place = (cx, cy)[n]
                copy = send(
                    hh.at[pl.ds(matrix, count), sixteen(0, (place + d) % 4), :],
                    r1.at[n, d - 1, pl.ds(slot, count)],
                    6 * s + 3 * n + d - 1,
                    (along_x, along_y)[n][d - 1],
                )
                copy.start()
                first.append(copy)

    def outer_sums(kx, ky, w):
        total = None
        if ky != 1:
            rows = pz[pl.ds(kx, 4), (0, None, 5)[ky], pl.ds(w, 2)].reshape(256, 256)
            total = nn(gty[ky // 2], rows)
        if kx != 1:
            x, px = ((0, 0), None, (3, 5))[kx]
            rows = pz[px, pl.ds(ky, 4), pl.ds(w, 2)].reshape(256, 256)
            term = nn(gt[ky, :, pl.ds(256 * x, 256)], rows)
            total = term if total is None else total + term
        return total

    for s in (1, 0, 2):
        for ky in range(3):
            if s == 1 and ky == 1:
                continue
            value = blocks_of(outer_sums(s, ky, 0), outer_sums(s, ky, 1))
            for n in range(3):
                j = 9 * s + 3 * ky + n
                wd[j] = (di[j] + value[n]).T
        core_copy(s).start()
    for s in (1, 0, 2):
        core_sum(s)

    def weights(j, carry):
        low, mid, high = ker[3 * j], ker[3 * j + 1], ker[3 * j + 2]
        none = jnp.zeros((128, 128), BF)
        wt[j, 0, pl.ds(0, 128), pl.ds(0, 128)] = low
        wt[j, 0, pl.ds(0, 128), pl.ds(128, 128)] = none
        wt[j, 0, pl.ds(128, 128), pl.ds(0, 128)] = mid
        wt[j, 0, pl.ds(128, 128), pl.ds(128, 128)] = low
        wt[j, 1, pl.ds(0, 128), pl.ds(0, 128)] = high
        wt[j, 1, pl.ds(0, 128), pl.ds(128, 128)] = mid
        wt[j, 1, pl.ds(128, 128), pl.ds(0, 128)] = none
        wt[j, 1, pl.ds(128, 128), pl.ds(128, 128)] = high
        return carry

    loads[3].wait()
    lax.fori_loop(0, 9, weights, 0)

    for tx in range(3):
        for ty in range(3):
            for tz in range(3):
                offs = offsets_of(tx, ty, tz)
                flipped = nt(eye[:80], stacked(offs)).astype(BF)
                oht[tx * 9 + ty * 3 + tz, :, pl.ds(0, 32 * len(offs))] = flipped

    def clear_dp(x, carry):
        dp[x] = jnp.zeros((6, 3, 32, 256), F32)
        return carry

    lax.fori_loop(0, 6, clear_dp, 0)

    for px in range(6):
        for ky in range(3):
            for w in range(2):
                term = None
                for kx in range(3):
                    if 0 <= px - kx < 4:
                        one = nt(gz[px - kx].reshape(256, 256), wt[3 * kx + ky, w])
                        term = one if term is None else term + one
                dp[px, pl.ds(ky, 4), pl.ds(w, 2)] += term.reshape(4, 2, 32, 256)

    for ux in range(4):
        for uy in range(4):
            pieces = []
            for uz in range(4):
                found = readers(ux, uy, uz)
                high, low = [], []
                for px, py, p, _ in found:
                    value = dp[px, py, p // 2, :, pl.ds(128 * (p % 2), 128)]
                    top = value.astype(BF)
                    high.append(top)
                    low.append((value - top.astype(F32)).astype(BF))
                high = jnp.concatenate(high, axis=0) if len(high) > 1 else high[0]
                low = jnp.concatenate(low, axis=0) if len(low) > 1 else low[0]
                group = kind(ux) * 9 + kind(uy) * 3 + kind(uz)
                res = nn(
                    oht[group, :, pl.ds(0, 32 * len(found))],
                    jnp.concatenate([high, low], axis=1),
                )
                res = res[:, :128] + res[:, 128:]
                de[ux * 16 + uy * 4 + uz] = res[:32]
                pieces.append(res)

            def give(slot, chunk, row):
                rs[slot, chunk] = jnp.concatenate(
                    [piece[row : row + 8] for piece in pieces], axis=0
                ).astype(BF)

            for slot in range(8):
                wx, wy = WAYS[slot]
                if (wx != 0 and ux != side(-wx)) or (wy != 0 and uy != side(-wy)):
                    continue
                chunk = 0 if slot >= 4 else (uy if wx != 0 else ux)
                give(slot, chunk, 64 if slot >= 4 else 32 + 8 * slot)

    for ch in range(8):
        @pl.when(there[ch])
        def _():
            halo_copy(rs, rr, bsem, brem, ch).start()

        @pl.when(jnp.logical_not(there[ch]))
        def _():
            rr[ch] = jnp.zeros((4, 32, 128), BF)

    for copy in first:
        copy.wait()
    for s in range(3):
        for n, (matrix, slot, count) in enumerate(RUNS[s]):
            kept = hh[pl.ds(matrix, count), sixteen(0, (cx, cy)[n]), :]
            got = [r1[n, d, pl.ds(slot, count)] for d in range(3)]
            s1[n, pl.ds(slot, count)] = kept + got[0] + got[1] + got[2]
    s1[0, pl.ds(14, 2)] = jnp.zeros((2, 16, 128), F32)
    s1[1, pl.ds(13, 3)] = jnp.zeros((3, 16, 128), F32)

    second = []
    for d in range(1, 4):
        for n in range(2):
            place = (cy, cx)[n]
            second.append(
                send(
                    s1.at[n, quarter((place + d) % 4)],
                    r2.at[n, d - 1],
                    17 + 2 * d - 1 + n,
                    (along_y, along_x)[n][d - 1],
                )
            )
    for copy in second:
        copy.start()

    for x in range(4):
        total = jnp.zeros((256, 256), F32)
        for kx in range(3):
            for ky in range(3):
                for w in range(2):
                    rows = pz[x + kx, pl.ds(ky, 4), pl.ds(w, 2)].reshape(256, 256)
                    total = total + nn(rows, wt[3 * kx + ky, w])
        co[x] = total.astype(BF).reshape(4, 2, 32, 256)
    for x in range(4):
        for hb in range(2):
            parts = [
                co[x, :, :, pl.ds(16 * hb, 16), pl.ds(128 * n, 128)].reshape(128, 128)
                for n in range(2)
            ]
            rows = nn(part_perm[...], jnp.concatenate(parts, axis=0)).reshape(16, 16, 128)
            block = iota((16, 16, 128), 0) + 16 * hb
            rows = rows * jnp.where(block < cnt[0], 1.0, 0.0)
            conv[pl.ds(16 * hb, 16), pl.ds(16 * x, 16), :] = rows.astype(BF)

    conv_copy = pltpu.make_async_copy(conv, conv_out, osem.at[0])
    conv_copy.start()

    for copy in second:
        copy.wait()
    for n in range(2):
        total = s1[n, quarter((cy, cx)[n])] + r2[n, 0] + r2[n, 1] + r2[n, 2]
        s2[n] = total.reshape(8, 8, 128)

    third = [
        send(s2.at[:, pl.ds((cz + d) % 8, 1)], r3.at[d - 1], 23 + d, along_z[d - 1])
        for d in range(1, 8)
    ]
    for copy in third:
        copy.start()

    for ch in range(8):
        @pl.when(there[ch])
        def _():
            halo_arrived(rs, rr, bsem, brem, ch).wait_recv()

    for ux in range(4):
        parts = []
        for uy in range(4):
            rows = de[pl.ds(ux * 16 + uy * 4, 4)].reshape(128, 128)
            for ch in range(8):
                wx, wy = WAYS[ch]
                if (wx != 0 and ux != side(wx)) or (wy != 0 and uy != side(wy)):
                    continue
                chunk = 0 if ch >= 4 else (uy if wx != 0 else ux)
                rows = rows + nn(bdt[ch], rr[ch, chunk])
            parts.append(rows.astype(BF).reshape(4, 32, 128))
        parts = jnp.concatenate(parts, axis=0)
        for hb in range(2):
            swapped = swap16(parts[:, 16 * hb : 16 * hb + 16])
            igrad[pl.ds(16 * hb, 16), pl.ds(16 * ux, 16), :] = swapped.astype(BF)

    igrad_copy = pltpu.make_async_copy(igrad, igrad_out, osem.at[1])
    igrad_copy.start()

    for copy in third:
        copy.wait()
    whole = s2[:, pl.ds(cz, 1)]
    for d in range(7):
        whole = whole + r3[d]
    tt[...] = (whole * (1.0 / math.sqrt(256 * 32 * 64))).reshape(16, 128).astype(BF)
    g3[pl.ds(cz, 1)] = tt[...][None]

    fourth = [send(tt, g3.at[cz], 30 + d, along_z[d - 1]) for d in range(1, 8)]
    for copy in fourth:
        copy.start()
    for copy in fourth:
        copy.wait()
    sums = g3[...].astype(F32)
    g2[0, quarter(cy)] = sums[:, :8].reshape(4, 16, 128).astype(BF)
    g2[1, quarter(cx)] = sums[:, 8:].reshape(4, 16, 128).astype(BF)

    def across(n, away):
        piece = g2.at[n, quarter(((cy, cx)[n] + 4 - away) % 4)]
        rows = sixteen(64 * core, (cx, cy)[n])
        copies = []
        for d in range(1, 4):
            copy = send(
                piece,
                kg.at[n, quarter(((cy, cx)[n] + 4 - away) % 4), rows, :],
                44 + 12 * n + 3 * away + d - 1,
                (along_x, along_y)[n][d - 1],
            )
            copy.start()
            copies.append(copy)
        return copies

    fifth = []
    for d in (1, 3, 2):
        for n in range(2):
            piece = g2.at[n, quarter((cy, cx)[n])]
            fifth.append(send(piece, piece, 36 + 2 * d + n, (along_y, along_x)[n][d - 1]))
    for copy in fifth:
        copy.start()
    sixth = [across(n, 0) for n in range(2)]
    for order, d in enumerate((1, 3, 2)):
        for n in range(2):
            fifth[2 * order + n].wait()
            sixth.append(across(n, d))

    last = []
    for n in range(2):
        rows = sixteen(64 * core, (cx, cy)[n])
        last.append(pltpu.make_async_copy(g2.at[n], kg.at[n, :, rows, :], osem.at[2 + n]))
        last.append(send(g2.at[n], kg.at[n, :, rows, :], 68 + n, sibling))
    for copy in last:
        copy.start()
    for d in (1, 3, 2):
        for n in range(2):
            for group in sixth[n::2]:
                group[d - 1].wait()
            rows = kg.at[n, :, sixteen(64 * core, ((cx, cy)[n] + 4 - d) % 4), :]
            forward = send(rows, rows, 68 + 2 * d + n, sibling)
            forward.start()
            last.append(forward)
    for copy in last + [conv_copy, igrad_copy]:
        copy.wait()

    for ch in range(8):
        @pl.when(there[ch])
        def _():
            halo_copy(hs, hr, hsem, hrem, ch).wait_send()
            halo_copy(rs, rr, bsem, brem, ch).wait_send()


def finish(conv, igrad, kg, conv_out, igrad_out, kgrad_out, conv_v, igrad_v, held, wide, sem):
    loads = []
    for s in range(3):
        slots = pl.ds(*((0, 5), (5, 5), (10, 4))[s])
        loads.append(pltpu.make_async_copy(kg.at[:, slots], held.at[:, slots], sem.at[s]))
    loads.append(pltpu.make_async_copy(conv, conv_v, sem.at[3]))
    loads.append(pltpu.make_async_copy(igrad, igrad_v, sem.at[4]))
    for copy in loads:
        copy.start()
    stores = []
    for s in range(3):
        loads[s].wait()
        for n, (matrix, slot, count) in enumerate(RUNS[s]):
            wide[pl.ds(matrix, count)] = held[n, pl.ds(slot, count)].astype(F32)
        part = pl.ds(9 * s, 9)
        stores.append(pltpu.make_async_copy(wide.at[part], kgrad_out.at[part], sem.at[5 + s]))
        stores[-1].start()
    for n, (src, dst) in enumerate(((conv_v, conv_out), (igrad_v, igrad_out))):
        loads[3 + n].wait()
        stores.append(pltpu.make_async_copy(src, dst, sem.at[8 + n]))
        stores[-1].start()
    for copy in stores:
        copy.wait()


def per_device(features, cotangent, kernel, block_count, neighbours, send_face, send_corner):
    vmem = pl.BlockSpec(memory_space=pltpu.VMEM)
    smem = pl.BlockSpec(memory_space=pltpu.SMEM)
    hbm = pl.BlockSpec(memory_space=pltpu.HBM)
    dma = pltpu.SemaphoreType.DMA
    blocks = (32, 64, 128)
    conv, igrad, kg = pl.pallas_call(
        body,
        out_shape=(
            jax.ShapeDtypeStruct(blocks, BF),
            jax.ShapeDtypeStruct(blocks, BF),
            jax.ShapeDtypeStruct((2, 16, 128, 128), BF),
        ),
        in_specs=[smem] * 3 + [hbm] * 4,
        out_specs=(hbm, hbm, hbm),
        scratch_shapes=[
            pltpu.VMEM(blocks, BF),
            pltpu.VMEM(blocks, BF),
            pltpu.VMEM((27, 128, 128), BF),
            pltpu.VMEM((32, 27), jnp.int32),
            pltpu.VMEM(blocks, BF),
            pltpu.VMEM(blocks, BF),
            pltpu.VMEM((64, 128, 128), BF),
            pltpu.VMEM((6, 6, 3, 32, 256), BF),
            pltpu.VMEM((4, 4, 2, 32, 256), BF),
            pltpu.VMEM((3, 256, 1024), BF),
            pltpu.VMEM((2, 256, 256), BF),
            pltpu.VMEM((9, 2, 256, 256), BF),
            pltpu.VMEM((27, 128, 128), F32),
            pltpu.VMEM((6, 6, 3, 32, 256), F32),
            pltpu.VMEM((64, 32, 128), F32),
            pltpu.VMEM((27, 32, 128), BF),
            pltpu.VMEM((27, 80, 256), BF),
            pltpu.VMEM((8, 32, 128), BF),
            pltpu.VMEM((8, 128, 32), BF),
            pltpu.VMEM((4, 4, 2, 32, 256), BF),
            pltpu.VMEM((256, 256), BF),
            pltpu.VMEM((256, 256), BF),
            pltpu.VMEM((256, 256), BF),
            pltpu.VMEM((8, 4, 32, 128), BF),
            pltpu.VMEM((8, 4, 32, 128), BF),
            pltpu.VMEM((8, 4, 32, 128), BF),
            pltpu.VMEM((8, 4, 32, 128), BF),
            pltpu.VMEM((27, 128, 128), F32),
            pltpu.VMEM((27, 64, 128), F32),
            pltpu.VMEM((27, 64, 128), F32),
            pltpu.VMEM((2, 3, 14, 16, 128), F32),
            pltpu.VMEM((2, 16, 16, 128), F32),
            pltpu.VMEM((2, 3, 4, 16, 128), F32),
            pltpu.VMEM((2, 8, 8, 128), F32),
            pltpu.VMEM((7, 2, 1, 8, 128), F32),
            pltpu.VMEM((16, 128), BF),
            pltpu.VMEM((8, 16, 128), BF),
            pltpu.VMEM((2, 16, 16, 128), BF),
            dma((4,)), dma((4,)), dma((8,)), dma((8,)), dma((8,)), dma((8,)),
            dma((3,)), dma((3,)), dma((76,)), dma((76,)),
        ],
        compiler_params=pltpu.CompilerParams(
            collective_id=0, has_side_effects=True, vmem_limit_bytes=62 * 1024 * 1024
        ),
        cost_estimate=pl.CostEstimate(
            flops=7_000_000_000, bytes_accessed=6_000_000, transcendentals=0
        ),
    )(
        block_count,
        send_face,
        jnp.swapaxes(send_corner, 1, 2),
        features.reshape(blocks),
        cotangent.reshape(blocks),
        kernel,
        neighbours,
    )
    conv, igrad, kgrad = pl.pallas_call(
        finish,
        out_shape=(
            jax.ShapeDtypeStruct(blocks, BF),
            jax.ShapeDtypeStruct(blocks, BF),
            jax.ShapeDtypeStruct((27, 128, 128), F32),
        ),
        in_specs=[hbm] * 3,
        out_specs=(hbm, hbm, hbm),
        scratch_shapes=[
            pltpu.VMEM(blocks, BF),
            pltpu.VMEM(blocks, BF),
            pltpu.VMEM((2, 16, 128, 128), BF),
            pltpu.VMEM((27, 128, 128), F32),
            dma((10,)),
        ],
        compiler_params=pltpu.CompilerParams(vmem_limit_bytes=62 * 1024 * 1024),
    )(conv, igrad, kg)
    return conv.reshape(2048, 128), igrad.reshape(2048, 128), kgrad


def solution(mesh):
    in_specs = (
        P(("gx", "gy"), None),
        P(("gx", "gy"), None),
        P(),
        P(("gx", "gy")),
        P(("gx", "gy"), None),
        P(("gx", "gy"), None, None),
        P(("gx", "gy"), None, None),
    )
    out_specs = (P(("gx", "gy"), None), P(("gx", "gy"), None), P())
    return jax.shard_map(
        per_device, mesh=mesh, in_specs=in_specs, out_specs=out_specs, check_vma=False
    )
```

```python
import math

import jax
import jax.numpy as jnp
from jax import lax
from jax.experimental import pallas as pl
from jax.experimental.pallas import tpu as pltpu
from jax.sharding import PartitionSpec as P

MESH = pl.DeviceIdType.MESH
BF = jnp.bfloat16
F32 = jnp.float32

NX, NY, NZ = 4, 4, 8
FACE_WAYS = ((-1, 0), (1, 0), (0, -1), (0, 1))
CORNER_WAYS = ((-1, -1), (-1, 1), (1, -1), (1, 1))
WAYS = FACE_WAYS + CORNER_WAYS


RUNS = (
    ((0, 0, 5), (5, 0, 4)),
    ((9, 5, 4), (13, 4, 5)),
    ((18, 9, 5), (23, 9, 4)),
)


def opposite(channel):
    return channel ^ 1 if channel < 4 else 11 - channel


def side(stride):
    return 0 if stride < 0 else 3


def places(local):
    if local == 0:
        return ((1, 0), (5, 1))
    if local == 3:
        return ((4, 0), (0, -1))
    return ((local + 1, 0),)


def kind(local):
    return 0 if local == 0 else (2 if local == 3 else 1)


def readers(ux, uy, uz):
    found = []
    for px, ox in places(ux):
        for py, oy in places(uy):
            for pz, oz in places(uz):
                found.append((px, py, pz, (ox + 1) * 9 + (oy + 1) * 3 + oz + 1))
    return found


def nn(a, b):
    return lax.dot_general(a, b, (((1,), (0,)), ((), ())), preferred_element_type=F32)


def nt(a, b):
    return lax.dot_general(a, b, (((1,), (1,)), ((), ())), preferred_element_type=F32)


def onehot(mask):
    return jnp.where(mask, 1.0, 0.0).astype(BF)


def iota(shape, dim):
    return lax.broadcasted_iota(jnp.int32, shape, dim)


def encode(rows):
    largest = jnp.max(jnp.abs(rows.reshape(-1, 8, 128)), axis=0)
    for step in (4, 2, 1):
        largest = jnp.maximum(largest, pltpu.roll(largest, step, 0))
    largest = jnp.maximum(largest, 1e-33)
    scale = largest * (1.0 / 32000.0)
    inverse = 32000.0 / largest
    coded = jnp.round(rows.reshape(-1, 8, 128) * inverse[None]).reshape(-1, 128)
    return coded.astype(jnp.int32).astype(jnp.int16), scale


def decode(coded, scale):
    rows = coded.astype(jnp.int32).astype(F32).reshape(-1, 8, 128)
    return (rows * scale[None]).reshape(-1, 128)


def body(
    cnt_in, face_in, corner_in, feat_in, cot_in, ker_in, near_in,
    conv_out, igrad_out, kg,
    cnt, face, corner, feat, cot, ker, near, conv, igrad,
    et, pz, gz, gt, gty, wt, di, dp, de, oh, oht, bd, bdt, co, perm, pair_perm, part_perm,
    hs, hr, rs, rr,
    wd, rcore, hh, q1, r1, s1, q2, r2, qs, rscale, s2, r3, tt, g3, g2,
    isem, osem, hsem, hrem, bsem, brem, csem, crem, asem, arem,
):
    loads = [
        pltpu.make_async_copy(src, dst, isem.at[n])
        for n, (src, dst) in enumerate(
            (
                (feat_in, feat),
                (cot_in, cot),
                (near_in, near),
                (ker_in, ker),
                (face_in, face),
                (corner_in, corner),
                (cnt_in, cnt),
            )
        )
    ]
    for copy in loads:
        copy.start()
    gx = lax.axis_index("gx")
    gy = lax.axis_index("gy")
    cy = gx // 16
    cz = (gx // 2) % 8
    cx = (gy // 2) * 2 + gx % 2
    core = gy % 2

    def at(x, y, z, c):
        return ((y * 8 + z) * 2 + x % 2, (x // 2) * 2 + c)

    sibling = (gx, gy // 2 * 2 + (1 - core))
    along_x = [at((cx + d) % NX, cy, cz, core) for d in range(1, NX)]
    along_y = [at(cx, (cy + d) % NY, cz, core) for d in range(1, NY)]
    along_z = [at(cx, cy, (cz + d) % NZ, core) for d in range(1, NZ)]
    halo = [(gx + wx, gy + wy) for wx, wy in WAYS]
    there = [
        (gx + wx >= 0) & (gx + wx < 64) & (gy + wy >= 0) & (gy + wy < 4) for wx, wy in WAYS
    ]

    barrier = pltpu.get_barrier_semaphore()
    greet = [sibling] + along_x + along_y + along_z
    greet += [((gx + wx + 64) % 64, (gy + wy + 4) % 4) for wx, wy in WAYS]
    for other in greet:
        pl.semaphore_signal(barrier, inc=1, device_id=other, device_id_type=MESH)

    r256, c256 = iota((256, 256), 0), iota((256, 256), 1)
    perm[...] = onehot(((r256 >> 4) == (c256 & 15)) & ((r256 & 15) == (c256 >> 4)))
    pair_perm[...] = onehot(c256 == (r256 & 15) * 16 + ((r256 >> 4) & 7) * 2 + (r256 >> 7))
    part_perm[...] = onehot(c256 == (r256 & 1) * 128 + ((r256 & 15) >> 1) * 16 + (r256 >> 4))
    eye = onehot(iota((128, 128), 0) == iota((128, 128), 1))
    eye256 = onehot(r256 == c256)

    def swap16(v):
        return nn(perm[...], v.reshape(256, 128)).reshape(16, 16, 128)

    r32, c32 = iota((32, 128), 0), iota((32, 128), 1)
    same_z = (r32 >> 3) == (c32 >> 5)
    loads[4].wait()
    loads[5].wait()
    for ch in range(8):
        index = jnp.full((32, 128), -1, jnp.int32)
        for n in range(8 if ch < 4 else 2):
            slot = n if ch < 4 else 2 * (opposite(ch) - 4) + n
            block = face[0, ch, n] if ch < 4 else corner[0, n, ch - 4]
            index = jnp.where((r32 & 7) == slot, block, index)
        pick = onehot(same_z & (index == (c32 & 31)))
        bd[ch] = pick
        bdt[ch] = nt(eye, pick).astype(BF)

    loads[0].wait()
    for hb in range(2):
        for ug in range(4):
            rows = swap16(feat[pl.ds(16 * hb, 16), pl.ds(16 * ug, 16), :])
            et[pl.ds(16 * ug, 16), pl.ds(16 * hb, 16), :] = rows.astype(BF)

    def rim_base(ch, chunk):
        wx, wy = WAYS[ch]
        ux = side(wx) if wx != 0 else chunk
        uy = side(wy) if wy != 0 else chunk
        return ux * 16 + uy * 4

    def chunks(ch):
        return 4 if ch < 4 else 1

    for ch in range(8):
        for chunk in range(chunks(ch)):
            source = et[pl.ds(rim_base(ch, chunk), 4), pl.ds(0, 32), :].reshape(128, 128)
            hs[ch, chunk] = nn(bd[ch], source).astype(BF)

    pl.semaphore_wait(barrier, len(greet))

    def part(buf, ch):
        return buf.at[ch] if ch < 4 else buf.at[ch, pl.ds(0, 1)]

    def halo_copy(src, dst, ss, rs_, ch):
        return pltpu.make_async_remote_copy(
            src_ref=part(src, ch),
            dst_ref=part(dst, opposite(ch)),
            send_sem=ss.at[ch],
            recv_sem=rs_.at[opposite(ch)],
            device_id=halo[ch],
            device_id_type=MESH,
        )

    def halo_arrived(src, dst, ss, rs_, ch):
        return pltpu.make_async_remote_copy(
            src_ref=part(src, ch),
            dst_ref=part(dst, ch),
            send_sem=ss.at[ch],
            recv_sem=rs_.at[ch],
            device_id=halo[ch],
            device_id_type=MESH,
        )

    for ch in range(8):
        @pl.when(there[ch])
        def _():
            halo_copy(hs, hr, hsem, hrem, ch).start()

    loads[6].wait()
    lives = [jnp.where(iota((16, 128), 0) + 16 * hb < cnt[0], 1.0, 0.0) for hb in range(2)]
    loads[1].wait()
    for x in range(4):
        for hb in range(2):
            rows = cot[pl.ds(16 * hb, 16), pl.ds(16 * x, 16), :].reshape(256, 128)
            rows = nn(pair_perm[...], rows).reshape(2, 4, 2, 16, 128) * lives[hb]
            for n in range(2):
                gz[x, :, :, pl.ds(16 * hb, 16), pl.ds(128 * n, 128)] = rows[n].astype(BF)
        turned = nt(eye256, gz[x].reshape(256, 256))
        place = pl.ds(256 * x, 256)
        gt[0, :, place] = jnp.where(c256 < 64, 0.0, turned).astype(BF)
        gt[1, :, place] = turned.astype(BF)
        gt[2, :, place] = jnp.where(c256 < 192, turned, 0.0).astype(BF)
    for n, y in enumerate((0, 3)):
        gty[n] = nt(eye256, gz[:, y].reshape(256, 256)).astype(BF)

    loads[2].wait()
    columns = c32 + jnp.where(c32 >= 32, 1, 0)
    for o in range(27):
        oh[o] = onehot(near[:, o : o + 1] == columns)

    def offsets_of(tx, ty, tz):
        pick = (0, 1, 3)
        return [r[3] for r in readers(pick[tx], pick[ty], pick[tz])]

    def stacked(offsets):
        if len(offsets) == 1:
            return oh[offsets[0]]
        return jnp.concatenate([oh[o] for o in offsets], axis=0)

    def clear(u, carry):
        et[u, pl.ds(32, 96), :] = jnp.zeros((96, 128), BF)
        return carry

    lax.fori_loop(0, 64, clear, 0)

    def inner(found):
        return [r for r in found if 1 <= r[0] <= 4 and 1 <= r[1] <= 4]

    def outer(found):
        return [r for r in found if not (1 <= r[0] <= 4 and 1 <= r[1] <= 4)]

    def keep(rows, found):
        for n, (px, py, p, _) in enumerate(found):
            pz[px, py, p // 2, :, pl.ds(128 * (p % 2), 128)] = rows[32 * n : 32 * n + 32]

    for py in (0, 5):
        pz[pl.ds(1, 4), py] = jnp.zeros((4, 3, 32, 256), BF)
    for ux in range(4):
        for uy in range(4):
            for uz in range(4):
                found = inner(readers(ux, uy, uz))
                picks = stacked([r[3] for r in found])[:, :32]
                keep(nn(picks, et[ux * 16 + uy * 4 + uz, pl.ds(0, 32)]).astype(BF), found)

    def blocks_of(d0, d1):
        return (
            d0[:128, :128] + d0[128:, 128:],
            d0[:128, 128:] + d1[128:, :128],
            d1[:128, :128] + d1[128:, 128:],
        )

    for kx in range(3):
        x0, x1 = ((1, 4), (0, 4), (0, 3))[kx]
        for ky in range(3):
            left = gt[ky, :, pl.ds(256 * x0, 256 * (x1 - x0))]
            sums = [
                nn(
                    left,
                    pz[pl.ds(x0 + kx, x1 - x0), pl.ds(ky, 4), pl.ds(w, 2)].reshape(-1, 256),
                )
                for w in range(2)
            ]
            for n, value in enumerate(blocks_of(*sums)):
                if kx == 1 and ky == 1:
                    wd[9 * kx + 3 * ky + n] = value
                else:
                    di[9 * kx + 3 * ky + n] = value

    for ch in range(8):
        @pl.when(there[ch])
        def _():
            halo_arrived(hs, hr, hsem, hrem, ch).wait_recv()
            wx, wy = WAYS[ch]
            for chunk in range(chunks(ch)):
                ux = side(-wx) if wx != 0 else chunk
                uy = side(-wy) if wy != 0 else chunk
                got = hr[ch, chunk].astype(F32).reshape(4, 8, 128)
                none = jnp.zeros((4, 8, 128), F32)
                pair = (got, none) if ch >= 4 or ch % 2 == 0 else (none, got)
                start = 64 if ch >= 4 else 32 + 16 * (ch // 2)
                et[pl.ds(ux * 16 + uy * 4, 4), pl.ds(start, 16), :] = jnp.concatenate(
                    pair, axis=1
                ).astype(BF)

    for ux in range(4):
        for uy in range(4):
            for uz in range(4):
                found = outer(readers(ux, uy, uz))
                if found:
                    picks = stacked([r[3] for r in found])
                    keep(nn(picks, et[ux * 16 + uy * 4 + uz]).astype(BF), found)

    mine = pl.multiple_of(64 * core, 64)
    other = pl.multiple_of(64 - 64 * core, 64)

    def core_copy(s):
        return pltpu.make_async_remote_copy(
            src_ref=wd.at[pl.ds(9 * s, 9), pl.ds(other, 64), :],
            dst_ref=rcore.at[pl.ds(9 * s, 9)],
            send_sem=csem.at[s],
            recv_sem=crem.at[s],
            device_id=sibling,
            device_id_type=MESH,
        )

    def send(src, dst, n, device):
        return pltpu.make_async_remote_copy(
            src_ref=src,
            dst_ref=dst,
            send_sem=asem.at[n],
            recv_sem=arem.at[n],
            device_id=device,
            device_id_type=MESH,
        )

    def sixteen(first, index):
        return pl.ds(pl.multiple_of(first + 16 * index, 16), 16)

    def quarter(index):
        return pl.ds(4 * index, 4)

    def core_sum(s):
        core_copy(s).wait()
        for n, (matrix, slot, count) in enumerate(RUNS[s]):
            kept = wd[pl.ds(matrix, count), pl.ds(mine, 64), :]
            hh[n, pl.ds(slot, count)] = kept + rcore[pl.ds(matrix, count)]

    def outer_sums(kx, ky, w):
        total = None
        if ky != 1:
            rows = pz[pl.ds(kx, 4), (0, None, 5)[ky], pl.ds(w, 2)].reshape(256, 256)
            total = nn(gty[ky // 2], rows)
        if kx != 1:
            x, px = ((0, 0), None, (3, 5))[kx]
            rows = pz[px, pl.ds(ky, 4), pl.ds(w, 2)].reshape(256, 256)
            term = nn(gt[ky, :, pl.ds(256 * x, 256)], rows)
            total = term if total is None else total + term
        return total

    for s in (1, 0, 2):
        for ky in range(3):
            if s == 1 and ky == 1:
                continue
            value = blocks_of(outer_sums(s, ky, 0), outer_sums(s, ky, 1))
            for n in range(3):
                j = 9 * s + 3 * ky + n
                wd[j] = di[j] + value[n]
        core_copy(s).start()
    for s in (1, 0, 2):
        core_sum(s)

    far_first = (2, 1, 3)
    first = []
    for n in range(2):
        size = (14, 13)[n]
        for d in far_first:
            rows = sixteen(0, ((cx, cy)[n] + d) % 4)
            coded, scale = encode(hh[n, pl.ds(0, size), rows, :].reshape(-1, 128))
            q1[n, d - 1, pl.ds(0, size)] = coded.reshape(size, 16, 128)
            qs[0, n, d - 1] = scale
            device = (along_x, along_y)[n][d - 1]
            first.append(
                send(
                    q1.at[n, d - 1, pl.ds(0, size)],
                    r1.at[n, d - 1, pl.ds(0, size)],
                    3 * n + d - 1,
                    device,
                )
            )
            first.append(send(qs.at[0, n, d - 1], rscale.at[0, n, d - 1], 6 + 3 * n + d - 1, device))
            first[-2].start()
            first[-1].start()

    def weights(j, carry):
        low, mid, high = ker[3 * j], ker[3 * j + 1], ker[3 * j + 2]
        none = jnp.zeros((128, 128), BF)
        wt[j, 0, pl.ds(0, 128), pl.ds(0, 128)] = low
        wt[j, 0, pl.ds(0, 128), pl.ds(128, 128)] = none
        wt[j, 0, pl.ds(128, 128), pl.ds(0, 128)] = mid
        wt[j, 0, pl.ds(128, 128), pl.ds(128, 128)] = low
        wt[j, 1, pl.ds(0, 128), pl.ds(0, 128)] = high
        wt[j, 1, pl.ds(0, 128), pl.ds(128, 128)] = mid
        wt[j, 1, pl.ds(128, 128), pl.ds(0, 128)] = none
        wt[j, 1, pl.ds(128, 128), pl.ds(128, 128)] = high
        return carry

    loads[3].wait()
    lax.fori_loop(0, 9, weights, 0)

    for tx in range(3):
        for ty in range(3):
            for tz in range(3):
                offs = offsets_of(tx, ty, tz)
                flipped = nt(eye[:80], stacked(offs)).astype(BF)
                oht[tx * 9 + ty * 3 + tz, :, pl.ds(0, 32 * len(offs))] = flipped

    def clear_dp(x, carry):
        dp[x] = jnp.zeros((6, 3, 32, 256), F32)
        return carry

    lax.fori_loop(0, 6, clear_dp, 0)

    for px in range(6):
        for ky in range(3):
            for w in range(2):
                term = None
                for kx in range(3):
                    if 0 <= px - kx < 4:
                        one = nt(gz[px - kx].reshape(256, 256), wt[3 * kx + ky, w])
                        term = one if term is None else term + one
                dp[px, pl.ds(ky, 4), pl.ds(w, 2)] += term.reshape(4, 2, 32, 256)

    for ux in range(4):
        for uy in range(4):
            pieces = []
            for uz in range(4):
                found = readers(ux, uy, uz)
                high, low = [], []
                for px, py, p, _ in found:
                    value = dp[px, py, p // 2, :, pl.ds(128 * (p % 2), 128)]
                    top = value.astype(BF)
                    high.append(top)
                    low.append((value - top.astype(F32)).astype(BF))
                high = jnp.concatenate(high, axis=0) if len(high) > 1 else high[0]
                low = jnp.concatenate(low, axis=0) if len(low) > 1 else low[0]
                group = kind(ux) * 9 + kind(uy) * 3 + kind(uz)
                res = nn(
                    oht[group, :, pl.ds(0, 32 * len(found))],
                    jnp.concatenate([high, low], axis=1),
                )
                res = res[:, :128] + res[:, 128:]
                de[ux * 16 + uy * 4 + uz] = res[:32]
                pieces.append(res)

            def give(slot, chunk, row):
                rs[slot, chunk] = jnp.concatenate(
                    [piece[row : row + 8] for piece in pieces], axis=0
                ).astype(BF)

            for slot in range(8):
                wx, wy = WAYS[slot]
                if (wx != 0 and ux != side(-wx)) or (wy != 0 and uy != side(-wy)):
                    continue
                chunk = 0 if slot >= 4 else (uy if wx != 0 else ux)
                give(slot, chunk, 64 if slot >= 4 else 32 + 8 * slot)

    for ch in range(8):
        @pl.when(there[ch])
        def _():
            halo_copy(rs, rr, bsem, brem, ch).start()

        @pl.when(jnp.logical_not(there[ch]))
        def _():
            rr[ch] = jnp.zeros((4, 32, 128), BF)

    for copy in first:
        copy.wait()
    for n in range(2):
        size = (14, 13)[n]
        total = hh[n, pl.ds(0, size), sixteen(0, (cx, cy)[n]), :]
        for d in range(3):
            got = decode(r1[n, d, pl.ds(0, size)].reshape(-1, 128), rscale[0, n, d])
            total = total + got.reshape(size, 16, 128)
        s1[n, pl.ds(0, size)] = total
        s1[n, pl.ds(size, 16 - size)] = jnp.zeros((16 - size, 16, 128), F32)

    second = []
    for n in range(2):
        for d in far_first:
            coded, scale = encode(s1[n, quarter(((cy, cx)[n] + d) % 4)].reshape(64, 128))
            q2[n, d - 1] = coded.reshape(4, 16, 128)
            qs[1, n, d - 1] = scale
            device = (along_y, along_x)[n][d - 1]
            second.append(send(q2.at[n, d - 1], r2.at[n, d - 1], 12 + 3 * n + d - 1, device))
            second.append(send(qs.at[1, n, d - 1], rscale.at[1, n, d - 1], 18 + 3 * n + d - 1, device))
            second[-2].start()
            second[-1].start()

    for x in range(4):
        total = jnp.zeros((256, 256), F32)
        for kx in range(3):
            for ky in range(3):
                for w in range(2):
                    rows = pz[x + kx, pl.ds(ky, 4), pl.ds(w, 2)].reshape(256, 256)
                    total = total + nn(rows, wt[3 * kx + ky, w])
        co[x] = total.astype(BF).reshape(4, 2, 32, 256)
    for x in range(4):
        for hb in range(2):
            parts = [
                co[x, :, :, pl.ds(16 * hb, 16), pl.ds(128 * n, 128)].reshape(128, 128)
                for n in range(2)
            ]
            rows = nn(part_perm[...], jnp.concatenate(parts, axis=0)).reshape(16, 16, 128)
            block = iota((16, 16, 128), 0) + 16 * hb
            rows = rows * jnp.where(block < cnt[0], 1.0, 0.0)
            conv[pl.ds(16 * hb, 16), pl.ds(16 * x, 16), :] = rows.astype(BF)

    conv_copy = pltpu.make_async_copy(conv, conv_out, osem.at[0])
    conv_copy.start()

    for copy in second:
        copy.wait()
    for n in range(2):
        total = s1[n, quarter((cy, cx)[n])].reshape(64, 128)
        for d in range(3):
            total = total + decode(r2[n, d].reshape(64, 128), rscale[1, n, d])
        s2[n] = total.reshape(8, 8, 128)

    third = [
        send(s2.at[:, pl.ds((cz + d) % 8, 1)], r3.at[d - 1], 23 + d, along_z[d - 1])
        for d in (4, 3, 5, 2, 6, 1, 7)
    ]
    for copy in third:
        copy.start()

    for ch in range(8):
        @pl.when(there[ch])
        def _():
            halo_arrived(rs, rr, bsem, brem, ch).wait_recv()

    for ux in range(4):
        parts = []
        for uy in range(4):
            rows = de[pl.ds(ux * 16 + uy * 4, 4)].reshape(128, 128)
            for ch in range(8):
                wx, wy = WAYS[ch]
                if (wx != 0 and ux != side(wx)) or (wy != 0 and uy != side(wy)):
                    continue
                chunk = 0 if ch >= 4 else (uy if wx != 0 else ux)
                rows = rows + nn(bdt[ch], rr[ch, chunk])
            parts.append(rows.astype(BF).reshape(4, 32, 128))
        parts = jnp.concatenate(parts, axis=0)
        for hb in range(2):
            swapped = swap16(parts[:, 16 * hb : 16 * hb + 16])
            igrad[pl.ds(16 * hb, 16), pl.ds(16 * ux, 16), :] = swapped.astype(BF)

    igrad_copy = pltpu.make_async_copy(igrad, igrad_out, osem.at[1])
    igrad_copy.start()

    for copy in third:
        copy.wait()
    whole = s2[:, pl.ds(cz, 1)]
    for d in range(7):
        whole = whole + r3[d]
    tt[...] = (whole * (1.0 / math.sqrt(256 * 32 * 64))).reshape(16, 128).astype(BF)
    g3[pl.ds(cz, 1)] = tt[...][None]

    fourth = [
        send(tt, g3.at[cz], 30 + d, along_z[d - 1]) for d in (4, 3, 5, 2, 6, 1, 7)
    ]
    for copy in fourth:
        copy.start()
    for copy in fourth:
        copy.wait()
    sums = g3[...].astype(F32)
    g2[0, quarter(cy)] = sums[:, :8].reshape(4, 16, 128).astype(BF)
    g2[1, quarter(cx)] = sums[:, 8:].reshape(4, 16, 128).astype(BF)

    def across(n, away):
        piece = g2.at[n, quarter(((cy, cx)[n] + 4 - away) % 4)]
        rows = sixteen(64 * core, (cx, cy)[n])
        copies = {}
        for d in far_first:
            copy = send(
                piece,
                kg.at[n, quarter(((cy, cx)[n] + 4 - away) % 4), rows, :],
                44 + 12 * n + 3 * away + d - 1,
                (along_x, along_y)[n][d - 1],
            )
            copy.start()
            copies[d] = copy
        return copies

    fifth = {}
    for d in far_first:
        for n in range(2):
            piece = g2.at[n, quarter((cy, cx)[n])]
            fifth[d, n] = send(piece, piece, 36 + 2 * d + n, (along_y, along_x)[n][d - 1])
            fifth[d, n].start()
    sixth = [across(n, 0) for n in range(2)]
    for d in (1, 3, 2):
        for n in range(2):
            fifth[d, n].wait()
            sixth.append(across(n, d))

    last = []
    for n in range(2):
        rows = sixteen(64 * core, (cx, cy)[n])
        last.append(pltpu.make_async_copy(g2.at[n], kg.at[n, :, rows, :], osem.at[2 + n]))
        last.append(send(g2.at[n], kg.at[n, :, rows, :], 68 + n, sibling))
    for copy in last:
        copy.start()
    for d in (1, 3, 2):
        for n in range(2):
            for group in sixth[n::2]:
                group[d].wait()
            rows = kg.at[n, :, sixteen(64 * core, ((cx, cy)[n] + 4 - d) % 4), :]
            forward = send(rows, rows, 68 + 2 * d + n, sibling)
            forward.start()
            last.append(forward)
    for copy in last + [conv_copy, igrad_copy]:
        copy.wait()

    for ch in range(8):
        @pl.when(there[ch])
        def _():
            halo_copy(hs, hr, hsem, hrem, ch).wait_send()
            halo_copy(rs, rr, bsem, brem, ch).wait_send()


def finish(conv, igrad, kg, conv_out, igrad_out, kgrad_out, conv_v, igrad_v, held, wide, sem):
    loads = []
    for s in range(3):
        slots = pl.ds(*((0, 5), (5, 5), (10, 4))[s])
        loads.append(pltpu.make_async_copy(kg.at[:, slots], held.at[:, slots], sem.at[s]))
    loads.append(pltpu.make_async_copy(conv, conv_v, sem.at[3]))
    loads.append(pltpu.make_async_copy(igrad, igrad_v, sem.at[4]))
    for copy in loads:
        copy.start()
    stores = []
    for s in range(3):
        loads[s].wait()
        for n, (matrix, slot, count) in enumerate(RUNS[s]):
            for m in range(count):
                wide[matrix + m] = held[n, slot + m].astype(F32).T
        part = pl.ds(9 * s, 9)
        stores.append(pltpu.make_async_copy(wide.at[part], kgrad_out.at[part], sem.at[5 + s]))
        stores[-1].start()
    for n, (src, dst) in enumerate(((conv_v, conv_out), (igrad_v, igrad_out))):
        loads[3 + n].wait()
        stores.append(pltpu.make_async_copy(src, dst, sem.at[8 + n]))
        stores[-1].start()
    for copy in stores:
        copy.wait()


def per_device(features, cotangent, kernel, block_count, neighbours, send_face, send_corner):
    vmem = pl.BlockSpec(memory_space=pltpu.VMEM)
    hbm = pl.BlockSpec(memory_space=pltpu.HBM)
    dma = pltpu.SemaphoreType.DMA
    blocks = (32, 64, 128)
    conv, igrad, kg = pl.pallas_call(
        body,
        out_shape=(
            jax.ShapeDtypeStruct(blocks, BF),
            jax.ShapeDtypeStruct(blocks, BF),
            jax.ShapeDtypeStruct((2, 16, 128, 128), BF),
        ),
        in_specs=[hbm] * 7,
        out_specs=(hbm,) * 3,
        scratch_shapes=[
            pltpu.SMEM((1,), jnp.int32),
            pltpu.SMEM((1, 4, 8), jnp.int32),
            pltpu.SMEM((1, 2, 4), jnp.int32),
            pltpu.VMEM(blocks, BF),
            pltpu.VMEM(blocks, BF),
            pltpu.VMEM((27, 128, 128), BF),
            pltpu.VMEM((32, 27), jnp.int32),
            pltpu.VMEM(blocks, BF),
            pltpu.VMEM(blocks, BF),
            pltpu.VMEM((64, 128, 128), BF),
            pltpu.VMEM((6, 6, 3, 32, 256), BF),
            pltpu.VMEM((4, 4, 2, 32, 256), BF),
            pltpu.VMEM((3, 256, 1024), BF),
            pltpu.VMEM((2, 256, 256), BF),
            pltpu.VMEM((9, 2, 256, 256), BF),
            pltpu.VMEM((27, 128, 128), F32),
            pltpu.VMEM((6, 6, 3, 32, 256), F32),
            pltpu.VMEM((64, 32, 128), F32),
            pltpu.VMEM((27, 32, 128), BF),
            pltpu.VMEM((27, 80, 256), BF),
            pltpu.VMEM((8, 32, 128), BF),
            pltpu.VMEM((8, 128, 32), BF),
            pltpu.VMEM((4, 4, 2, 32, 256), BF),
            pltpu.VMEM((256, 256), BF),
            pltpu.VMEM((256, 256), BF),
            pltpu.VMEM((256, 256), BF),
            pltpu.VMEM((8, 4, 32, 128), BF),
            pltpu.VMEM((8, 4, 32, 128), BF),
            pltpu.VMEM((8, 4, 32, 128), BF),
            pltpu.VMEM((8, 4, 32, 128), BF),
            pltpu.VMEM((27, 128, 128), F32),
            pltpu.VMEM((27, 64, 128), F32),
            pltpu.VMEM((2, 14, 64, 128), F32),
            pltpu.VMEM((2, 3, 14, 16, 128), jnp.int16),
            pltpu.VMEM((2, 3, 14, 16, 128), jnp.int16),
            pltpu.VMEM((2, 16, 16, 128), F32),
            pltpu.VMEM((2, 3, 4, 16, 128), jnp.int16),
            pltpu.VMEM((2, 3, 4, 16, 128), jnp.int16),
            pltpu.VMEM((2, 2, 3, 8, 128), F32),
            pltpu.VMEM((2, 2, 3, 8, 128), F32),
            pltpu.VMEM((2, 8, 8, 128), F32),
            pltpu.VMEM((7, 2, 1, 8, 128), F32),
            pltpu.VMEM((16, 128), BF),
            pltpu.VMEM((8, 16, 128), BF),
            pltpu.VMEM((2, 16, 16, 128), BF),
            dma((7,)), dma((4,)), dma((8,)), dma((8,)), dma((8,)), dma((8,)),
            dma((3,)), dma((3,)), dma((76,)), dma((76,)),
        ],
        compiler_params=pltpu.CompilerParams(
            collective_id=0, has_side_effects=True, vmem_limit_bytes=62 * 1024 * 1024
        ),
        cost_estimate=pl.CostEstimate(
            flops=7_000_000_000, bytes_accessed=6_000_000, transcendentals=0
        ),
    )(
        block_count,
        send_face,
        jnp.swapaxes(send_corner, 1, 2),
        features.reshape(blocks),
        cotangent.reshape(blocks),
        kernel,
        neighbours,
    )
    conv, igrad, kgrad = pl.pallas_call(
        finish,
        out_shape=(
            jax.ShapeDtypeStruct(blocks, BF),
            jax.ShapeDtypeStruct(blocks, BF),
            jax.ShapeDtypeStruct((27, 128, 128), F32),
        ),
        in_specs=[hbm] * 3,
        out_specs=(hbm, hbm, hbm),
        scratch_shapes=[
            pltpu.VMEM(blocks, BF),
            pltpu.VMEM(blocks, BF),
            pltpu.VMEM((2, 16, 128, 128), BF),
            pltpu.VMEM((27, 128, 128), F32),
            dma((10,)),
        ],
        compiler_params=pltpu.CompilerParams(vmem_limit_bytes=62 * 1024 * 1024),
    )(conv, igrad, kg)
    return conv.reshape(2048, 128), igrad.reshape(2048, 128), kgrad


def solution(mesh):
    in_specs = (
        P(("gx", "gy"), None),
        P(("gx", "gy"), None),
        P(),
        P(("gx", "gy")),
        P(("gx", "gy"), None),
        P(("gx", "gy"), None, None),
        P(("gx", "gy"), None, None),
    )
    out_specs = (P(("gx", "gy"), None), P(("gx", "gy"), None), P())
    return jax.shard_map(
        per_device, mesh=mesh, in_specs=in_specs, out_specs=out_specs, check_vma=False
    )
```

```python
import math

import jax
import jax.numpy as jnp
from jax import lax
from jax.experimental import pallas as pl
from jax.experimental.pallas import tpu as pltpu
from jax.sharding import PartitionSpec as P

MESH = pl.DeviceIdType.MESH
BF = jnp.bfloat16
F32 = jnp.float32

NX, NY, NZ = 4, 4, 8
FACE_WAYS = ((-1, 0), (1, 0), (0, -1), (0, 1))
CORNER_WAYS = ((-1, -1), (-1, 1), (1, -1), (1, 1))
WAYS = FACE_WAYS + CORNER_WAYS


RUNS = (
    ((0, 0, 5), (5, 0, 4)),
    ((9, 5, 4), (13, 4, 5)),
    ((18, 9, 5), (23, 9, 4)),
)


def opposite(channel):
    return channel ^ 1 if channel < 4 else 11 - channel


def side(stride):
    return 0 if stride < 0 else 3


def places(local):
    if local == 0:
        return ((1, 0), (5, 1))
    if local == 3:
        return ((4, 0), (0, -1))
    return ((local + 1, 0),)


def kind(local):
    return 0 if local == 0 else (2 if local == 3 else 1)


def readers(ux, uy, uz):
    found = []
    for px, ox in places(ux):
        for py, oy in places(uy):
            for pz, oz in places(uz):
                found.append((px, py, pz, (ox + 1) * 9 + (oy + 1) * 3 + oz + 1))
    return found


def nn(a, b):
    return lax.dot_general(a, b, (((1,), (0,)), ((), ())), preferred_element_type=F32)


def nt(a, b):
    return lax.dot_general(a, b, (((1,), (1,)), ((), ())), preferred_element_type=F32)


def onehot(mask):
    return jnp.where(mask, 1.0, 0.0).astype(BF)


def iota(shape, dim):
    return lax.broadcasted_iota(jnp.int32, shape, dim)


def encode(rows):
    largest = jnp.max(jnp.abs(rows.reshape(-1, 8, 128)), axis=0)
    for step in (4, 2, 1):
        largest = jnp.maximum(largest, pltpu.roll(largest, step, 0))
    largest = jnp.maximum(largest, 1e-33)
    scale = largest * (1.0 / 32000.0)
    inverse = 32000.0 / largest
    coded = jnp.round(rows.reshape(-1, 8, 128) * inverse[None]).reshape(-1, 128)
    return coded.astype(jnp.int32).astype(jnp.int16), scale


def decode(coded, scale):
    rows = coded.astype(jnp.int32).astype(F32).reshape(-1, 8, 128)
    return (rows * scale[None]).reshape(-1, 128)


def body(
    face_in, corner_in, feat_in, cot_in, ker_in, near_in,
    conv_out, igrad_out, kg,
    face, corner, feat, cot, ker, near, live, conv, igrad,
    et, pz, gz, gt, gty, wt, di, dp, de, oh, oht, bd, bdt, co, perm, pair_perm, part_perm,
    hs, hr, rs, rr,
    wd, rcore, hh, q1, r1, s1, q2, r2, qs, rscale, s2, q3, qs3, r3, rscale3, g2,
    isem, osem, hsem, hrem, bsem, brem, csem, crem, asem, arem,
):
    loads = [
        pltpu.make_async_copy(src, dst, isem.at[n])
        for n, (src, dst) in enumerate(
            (
                (face_in, face),
                (corner_in, corner),
                (feat_in, feat),
                (near_in, near),
                (cot_in, cot),
                (ker_in, ker),
            )
        )
    ]
    for copy in loads:
        copy.start()
    gx = lax.axis_index("gx")
    gy = lax.axis_index("gy")
    cy = gx // 16
    cz = (gx // 2) % 8
    cx = (gy // 2) * 2 + gx % 2
    core = gy % 2

    def at(x, y, z, c):
        return ((y * 8 + z) * 2 + x % 2, (x // 2) * 2 + c)

    sibling = (gx, gy // 2 * 2 + (1 - core))
    along_x = [at((cx + d) % NX, cy, cz, core) for d in range(1, NX)]
    along_y = [at(cx, (cy + d) % NY, cz, core) for d in range(1, NY)]
    along_z = [at(cx, cy, (cz + d) % NZ, core) for d in range(1, NZ)]
    halo = [(gx + wx, gy + wy) for wx, wy in WAYS]
    there = [
        (gx + wx >= 0) & (gx + wx < 64) & (gy + wy >= 0) & (gy + wy < 4) for wx, wy in WAYS
    ]

    barrier = pltpu.get_barrier_semaphore()
    greet = [along_z[n] for n in (3, 2, 4, 1, 5, 0, 6)] + along_x + along_y + [sibling]
    greet += [((gx + wx + 64) % 64, (gy + wy + 4) % 4) for wx, wy in WAYS]
    for other in greet:
        pl.semaphore_signal(barrier, inc=1, device_id=other, device_id_type=MESH)

    r256, c256 = iota((256, 256), 0), iota((256, 256), 1)
    perm[...] = onehot(((r256 >> 4) == (c256 & 15)) & ((r256 & 15) == (c256 >> 4)))
    pair_perm[...] = onehot(c256 == (r256 & 15) * 16 + ((r256 >> 4) & 7) * 2 + (r256 >> 7))
    part_perm[...] = onehot(c256 == (r256 & 1) * 128 + ((r256 & 15) >> 1) * 16 + (r256 >> 4))
    eye = onehot(iota((128, 128), 0) == iota((128, 128), 1))
    eye256 = onehot(r256 == c256)

    def swap16(v):
        return nn(perm[...], v.reshape(256, 128)).reshape(16, 16, 128)

    def clear(u, carry):
        et[u, pl.ds(32, 96), :] = jnp.zeros((96, 128), BF)
        return carry

    lax.fori_loop(0, 64, clear, 0)

    r32, c32 = iota((32, 128), 0), iota((32, 128), 1)
    same_z = (r32 >> 3) == (c32 >> 5)
    loads[0].wait()
    loads[1].wait()
    for ch in range(8):
        index = jnp.full((32, 128), -1, jnp.int32)
        for n in range(8 if ch < 4 else 2):
            slot = n if ch < 4 else 2 * (opposite(ch) - 4) + n
            block = face[0, ch, n] if ch < 4 else corner[0, n, ch - 4]
            index = jnp.where((r32 & 7) == slot, block, index)
        pick = onehot(same_z & (index == (c32 & 31)))
        bd[ch] = pick
        bdt[ch] = nt(eye, pick).astype(BF)

    loads[2].wait()
    for hb in range(2):
        for ug in range(4):
            rows = swap16(feat[pl.ds(16 * hb, 16), pl.ds(16 * ug, 16), :])
            et[pl.ds(16 * ug, 16), pl.ds(16 * hb, 16), :] = rows.astype(BF)

    def rim_base(ch, chunk):
        wx, wy = WAYS[ch]
        ux = side(wx) if wx != 0 else chunk
        uy = side(wy) if wy != 0 else chunk
        return ux * 16 + uy * 4

    def chunks(ch):
        return 4 if ch < 4 else 1

    for ch in range(8):
        for chunk in range(chunks(ch)):
            source = et[pl.ds(rim_base(ch, chunk), 4), pl.ds(0, 32), :].reshape(128, 128)
            hs[ch, chunk] = nn(bd[ch], source).astype(BF)

    pl.semaphore_wait(barrier, len(greet))

    def part(buf, ch):
        return buf.at[ch] if ch < 4 else buf.at[ch, pl.ds(0, 1)]

    def halo_copy(src, dst, ss, rs_, ch):
        return pltpu.make_async_remote_copy(
            src_ref=part(src, ch),
            dst_ref=part(dst, opposite(ch)),
            send_sem=ss.at[ch],
            recv_sem=rs_.at[opposite(ch)],
            device_id=halo[ch],
            device_id_type=MESH,
        )

    def halo_arrived(src, dst, ss, rs_, ch):
        return pltpu.make_async_remote_copy(
            src_ref=part(src, ch),
            dst_ref=part(dst, ch),
            send_sem=ss.at[ch],
            recv_sem=rs_.at[ch],
            device_id=halo[ch],
            device_id_type=MESH,
        )

    for ch in range(8):
        @pl.when(there[ch])
        def _():
            halo_copy(hs, hr, hsem, hrem, ch).start()

    loads[3].wait()
    live[...] = jnp.where(near[:, 13:14] == r32, 1.0, 0.0)
    lives = [live[pl.ds(16 * hb, 16), :] for hb in range(2)]
    loads[4].wait()
    for x in range(4):
        for hb in range(2):
            rows = cot[pl.ds(16 * hb, 16), pl.ds(16 * x, 16), :].reshape(256, 128)
            rows = nn(pair_perm[...], rows).reshape(2, 4, 2, 16, 128) * lives[hb]
            for n in range(2):
                gz[x, :, :, pl.ds(16 * hb, 16), pl.ds(128 * n, 128)] = rows[n].astype(BF)
    for x in range(4):
        turned = nt(eye256, gz[x].reshape(256, 256))
        place = pl.ds(256 * x, 256)
        gt[:, place] = turned.astype(BF)
    for n, y in enumerate((0, 3)):
        turned = nt(eye256, gz[:, y].reshape(256, 256))
        gty[n, 0] = jnp.where(c256 < 64, 0.0, turned).astype(BF)
        gty[n, 1] = turned.astype(BF)
        gty[n, 2] = jnp.where(c256 < 192, turned, 0.0).astype(BF)

    columns = c32 + jnp.where(c32 >= 32, 1, 0)
    for o in range(27):
        oh[o] = onehot(near[:, o : o + 1] == columns)

    def offsets_of(tx, ty, tz):
        pick = (0, 1, 3)
        return [r[3] for r in readers(pick[tx], pick[ty], pick[tz])]

    def stacked(offsets):
        if len(offsets) == 1:
            return oh[offsets[0]]
        return jnp.concatenate([oh[o] for o in offsets], axis=0)

    def inner(found):
        return [r for r in found if 1 <= r[0] <= 4 and 1 <= r[1] <= 4]

    def outer(found):
        return [r for r in found if not (1 <= r[0] <= 4 and 1 <= r[1] <= 4)]

    def keep(rows, found):
        for n, (px, py, p, _) in enumerate(found):
            pz[px, py, p // 2, :, pl.ds(128 * (p % 2), 128)] = rows[32 * n : 32 * n + 32]

    for py in (0, 5):
        pz[pl.ds(1, 4), py] = jnp.zeros((4, 3, 32, 256), BF)
    for ux in range(4):
        for uy in range(4):
            for uz in range(4):
                found = inner(readers(ux, uy, uz))
                picks = stacked([r[3] for r in found])[:, :32]
                keep(nn(picks, et[ux * 16 + uy * 4 + uz, pl.ds(0, 32)]).astype(BF), found)

    mine = pl.multiple_of(64 * core, 64)
    other = pl.multiple_of(64 - 64 * core, 64)

    def core_copy(s):
        return pltpu.make_async_remote_copy(
            src_ref=wd.at[pl.ds(9 * s, 9), pl.ds(other, 64), :],
            dst_ref=rcore.at[pl.ds(9 * s, 9)],
            send_sem=csem.at[s],
            recv_sem=crem.at[s],
            device_id=sibling,
            device_id_type=MESH,
        )

    def blocks_of(d0, d1):
        return (
            d0[:128, :128] + d0[128:, 128:],
            d0[:128, 128:] + d1[128:, :128],
            d1[:128, :128] + d1[128:, 128:],
        )

    for kx in range(3):
        x0, x1 = ((1, 4), (0, 4), (0, 3))[kx]
        for ky in range(3):
            left = gt[:, pl.ds(256 * x0, 256 * (x1 - x0))]
            sums = [
                nn(
                    left,
                    pz[pl.ds(x0 + kx, x1 - x0), pl.ds(ky, 4), pl.ds(w, 2)].reshape(-1, 256),
                )
                for w in range(2)
            ]
            for n, value in enumerate(blocks_of(*sums)):
                if kx == 1 and ky == 1:
                    wd[9 * kx + 3 * ky + n] = value
                else:
                    di[9 * kx + 3 * ky + n] = value

    for ch in range(8):
        @pl.when(there[ch])
        def _():
            halo_arrived(hs, hr, hsem, hrem, ch).wait_recv()
            wx, wy = WAYS[ch]
            for chunk in range(chunks(ch)):
                ux = side(-wx) if wx != 0 else chunk
                uy = side(-wy) if wy != 0 else chunk
                got = hr[ch, chunk].astype(F32).reshape(4, 8, 128)
                none = jnp.zeros((4, 8, 128), F32)
                pair = (got, none) if ch >= 4 or ch % 2 == 0 else (none, got)
                start = 64 if ch >= 4 else 32 + 16 * (ch // 2)
                et[pl.ds(ux * 16 + uy * 4, 4), pl.ds(start, 16), :] = jnp.concatenate(
                    pair, axis=1
                ).astype(BF)

    for ux in range(4):
        for uy in range(4):
            for uz in range(4):
                found = outer(readers(ux, uy, uz))
                if found:
                    picks = stacked([r[3] for r in found])
                    keep(nn(picks, et[ux * 16 + uy * 4 + uz]).astype(BF), found)

    def send(src, dst, n, device):
        return pltpu.make_async_remote_copy(
            src_ref=src,
            dst_ref=dst,
            send_sem=asem.at[n],
            recv_sem=arem.at[n],
            device_id=device,
            device_id_type=MESH,
        )

    def sixteen(first, index):
        return pl.ds(pl.multiple_of(first + 16 * index, 16), 16)

    def quarter(index):
        return pl.ds(4 * index, 4)

    def core_sum(s):
        core_copy(s).wait()
        for n, (matrix, slot, count) in enumerate(RUNS[s]):
            kept = wd[pl.ds(matrix, count), pl.ds(mine, 64), :]
            hh[n, pl.ds(slot, count)] = kept + rcore[pl.ds(matrix, count)]

    def outer_sums(kx, ky, w):
        total = None
        if ky != 1:
            rows = pz[pl.ds(kx, 4), (0, None, 5)[ky], pl.ds(w, 2)].reshape(256, 256)
            total = nn(gty[ky // 2, kx], rows)
        if kx != 1:
            x, px = ((0, 0), None, (3, 5))[kx]
            rows = pz[px, pl.ds(ky, 4), pl.ds(w, 2)].reshape(256, 256)
            term = nn(gt[:, pl.ds(256 * x, 256)], rows)
            total = term if total is None else total + term
        return total

    for s in (1, 0, 2):
        for ky in range(3):
            if s == 1 and ky == 1:
                continue
            value = blocks_of(outer_sums(s, ky, 0), outer_sums(s, ky, 1))
            for n in range(3):
                j = 9 * s + 3 * ky + n
                wd[j] = di[j] + value[n]
        core_copy(s).start()
    for s in (1, 0, 2):
        core_sum(s)

    far_first = (2, 1, 3)
    first = []
    for n in range(2):
        size = (14, 13)[n]
        for d in far_first:
            rows = sixteen(0, ((cx, cy)[n] + d) % 4)
            coded, scale = encode(hh[n, pl.ds(0, size), rows, :].reshape(-1, 128))
            q1[n, d - 1, pl.ds(0, size)] = coded.reshape(size, 16, 128)
            qs[0, n, d - 1] = scale
            device = (along_x, along_y)[n][d - 1]
            first.append(
                send(
                    q1.at[n, d - 1, pl.ds(0, size)],
                    r1.at[n, d - 1, pl.ds(0, size)],
                    3 * n + d - 1,
                    device,
                )
            )
            first.append(send(qs.at[0, n, d - 1], rscale.at[0, n, d - 1], 6 + 3 * n + d - 1, device))
            first[-2].start()
            first[-1].start()

    def weights(j, carry):
        low, mid, high = ker[3 * j], ker[3 * j + 1], ker[3 * j + 2]
        none = jnp.zeros((128, 128), BF)
        wt[j, 0, pl.ds(0, 128), pl.ds(0, 128)] = low
        wt[j, 0, pl.ds(0, 128), pl.ds(128, 128)] = none
        wt[j, 0, pl.ds(128, 128), pl.ds(0, 128)] = mid
        wt[j, 0, pl.ds(128, 128), pl.ds(128, 128)] = low
        wt[j, 1, pl.ds(0, 128), pl.ds(0, 128)] = high
        wt[j, 1, pl.ds(0, 128), pl.ds(128, 128)] = mid
        wt[j, 1, pl.ds(128, 128), pl.ds(0, 128)] = none
        wt[j, 1, pl.ds(128, 128), pl.ds(128, 128)] = high
        return carry

    loads[5].wait()
    lax.fori_loop(0, 9, weights, 0)

    for tx in range(3):
        for ty in range(3):
            for tz in range(3):
                offs = offsets_of(tx, ty, tz)
                flipped = nt(eye[:80], stacked(offs)).astype(BF)
                oht[tx * 9 + ty * 3 + tz, :, pl.ds(0, 32 * len(offs))] = flipped

    def clear_dp(x, carry):
        dp[x] = jnp.zeros((6, 3, 32, 256), F32)
        return carry

    lax.fori_loop(0, 6, clear_dp, 0)

    for px in range(6):
        for ky in range(3):
            for w in range(2):
                term = None
                for kx in range(3):
                    if 0 <= px - kx < 4:
                        one = nt(gz[px - kx].reshape(256, 256), wt[3 * kx + ky, w])
                        term = one if term is None else term + one
                dp[px, pl.ds(ky, 4), pl.ds(w, 2)] += term.reshape(4, 2, 32, 256)

    for copy in first:
        copy.wait()
    for n in range(2):
        size = (14, 13)[n]
        total = hh[n, pl.ds(0, size), sixteen(0, (cx, cy)[n]), :]
        for d in range(3):
            got = decode(r1[n, d, pl.ds(0, size)].reshape(-1, 128), rscale[0, n, d])
            total = total + got.reshape(size, 16, 128)
        s1[n, pl.ds(0, size)] = total
        s1[n, pl.ds(size, 16 - size)] = jnp.zeros((16 - size, 16, 128), F32)

    second = []
    for n in range(2):
        for d in far_first:
            coded, scale = encode(s1[n, quarter(((cy, cx)[n] + d) % 4)].reshape(64, 128))
            q2[n, d - 1] = coded.reshape(4, 16, 128)
            qs[1, n, d - 1] = scale
            device = (along_y, along_x)[n][d - 1]
            second.append(send(q2.at[n, d - 1], r2.at[n, d - 1], 12 + 3 * n + d - 1, device))
            second.append(send(qs.at[1, n, d - 1], rscale.at[1, n, d - 1], 18 + 3 * n + d - 1, device))
            second[-2].start()
            second[-1].start()

    for ux in range(4):
        for uy in range(4):
            pieces = []
            for uz in range(4):
                found = readers(ux, uy, uz)
                high, low = [], []
                for px, py, p, _ in found:
                    value = dp[px, py, p // 2, :, pl.ds(128 * (p % 2), 128)]
                    top = value.astype(BF)
                    high.append(top)
                    low.append((value - top.astype(F32)).astype(BF))
                high = jnp.concatenate(high, axis=0) if len(high) > 1 else high[0]
                low = jnp.concatenate(low, axis=0) if len(low) > 1 else low[0]
                group = kind(ux) * 9 + kind(uy) * 3 + kind(uz)
                res = nn(
                    oht[group, :, pl.ds(0, 32 * len(found))],
                    jnp.concatenate([high, low], axis=1),
                )
                res = res[:, :128] + res[:, 128:]
                de[ux * 16 + uy * 4 + uz] = res[:32]
                pieces.append(res)

            def give(slot, chunk, row):
                rs[slot, chunk] = jnp.concatenate(
                    [piece[row : row + 8] for piece in pieces], axis=0
                ).astype(BF)

            for slot in range(8):
                wx, wy = WAYS[slot]
                if (wx != 0 and ux != side(-wx)) or (wy != 0 and uy != side(-wy)):
                    continue
                chunk = 0 if slot >= 4 else (uy if wx != 0 else ux)
                give(slot, chunk, 64 if slot >= 4 else 32 + 8 * slot)

    for ch in range(8):
        @pl.when(there[ch])
        def _():
            halo_copy(rs, rr, bsem, brem, ch).start()

        @pl.when(jnp.logical_not(there[ch]))
        def _():
            rr[ch] = jnp.zeros((4, 32, 128), BF)

    def convolve(x):
        total = jnp.zeros((256, 256), F32)
        for kx in range(3):
            for ky in range(3):
                for w in range(2):
                    rows = pz[x + kx, pl.ds(ky, 4), pl.ds(w, 2)].reshape(256, 256)
                    total = total + nn(rows, wt[3 * kx + ky, w])
        alive = jnp.concatenate([live[...], live[...]], axis=1)
        co[x] = (total.reshape(4, 2, 32, 256) * alive).astype(BF)
    convolve(0)
    convolve(1)

    for copy in second:
        copy.wait()
    for n in range(2):
        total = s1[n, quarter((cy, cx)[n])].reshape(64, 128)
        for d in range(3):
            total = total + decode(r2[n, d].reshape(64, 128), rscale[1, n, d])
        s2[n] = total

    coded, scale = encode(s2[...].reshape(128, 128))
    q3[...] = coded
    qs3[...] = scale
    r3[pl.ds(cz, 1)] = coded[None]
    rscale3[pl.ds(cz, 1)] = scale[None]
    third = []
    for d in (4, 3, 5, 2, 6, 1, 7):
        third.append(send(q3, r3.at[cz], 23 + d, along_z[d - 1]))
        third.append(send(qs3, rscale3.at[cz], 30 + d, along_z[d - 1]))
    for copy in third:
        copy.start()

    convolve(2)
    convolve(3)
    for x in range(4):
        for hb in range(2):
            parts = [
                co[x, :, :, pl.ds(16 * hb, 16), pl.ds(128 * n, 128)].reshape(128, 128)
                for n in range(2)
            ]
            rows = nn(part_perm[...], jnp.concatenate(parts, axis=0)).reshape(16, 16, 128)
            conv[pl.ds(16 * hb, 16), pl.ds(16 * x, 16), :] = rows.astype(BF)

    conv_copy = pltpu.make_async_copy(conv, conv_out, osem.at[0])
    conv_copy.start()

    for ch in range(8):
        @pl.when(there[ch])
        def _():
            halo_arrived(rs, rr, bsem, brem, ch).wait_recv()

    for ux in range(4):
        parts = []
        for uy in range(4):
            rows = de[pl.ds(ux * 16 + uy * 4, 4)].reshape(128, 128)
            for ch in range(8):
                wx, wy = WAYS[ch]
                if (wx != 0 and ux != side(wx)) or (wy != 0 and uy != side(wy)):
                    continue
                chunk = 0 if ch >= 4 else (uy if wx != 0 else ux)
                rows = rows + nn(bdt[ch], rr[ch, chunk])
            parts.append(rows.astype(BF).reshape(4, 32, 128))
        parts = jnp.concatenate(parts, axis=0)
        for hb in range(2):
            swapped = swap16(parts[:, 16 * hb : 16 * hb + 16])
            igrad[pl.ds(16 * hb, 16), pl.ds(16 * ux, 16), :] = swapped.astype(BF)

    igrad_copy = pltpu.make_async_copy(igrad, igrad_out, osem.at[1])
    igrad_copy.start()

    for copy in third:
        copy.wait()
    whole = decode(r3[0], rscale3[0])
    for z in range(1, 8):
        whole = whole + decode(r3[z], rscale3[z])
    whole = (whole * (1.0 / math.sqrt(256 * 32 * 64))).reshape(2, 4, 16, 128).astype(BF)
    g2[0, quarter(cy)] = whole[0]
    g2[1, quarter(cx)] = whole[1]

    def across(n, away):
        piece = g2.at[n, quarter(((cy, cx)[n] + 4 - away) % 4)]
        rows = sixteen(64 * core, (cx, cy)[n])
        copies = {}
        for d in far_first:
            copy = send(
                piece,
                kg.at[n, quarter(((cy, cx)[n] + 4 - away) % 4), rows, :],
                44 + 12 * n + 3 * away + d - 1,
                (along_x, along_y)[n][d - 1],
            )
            copy.start()
            copies[d] = copy
        return copies

    fifth = {}
    for d in far_first:
        for n in range(2):
            piece = g2.at[n, quarter((cy, cx)[n])]
            fifth[d, n] = send(piece, piece, 36 + 2 * d + n, (along_y, along_x)[n][d - 1])
            fifth[d, n].start()
    sixth = [across(n, 0) for n in range(2)]
    for d in (1, 3, 2):
        for n in range(2):
            fifth[d, n].wait()
            sixth.append(across(n, d))

    last = []
    for n in range(2):
        rows = sixteen(64 * core, (cx, cy)[n])
        last.append(pltpu.make_async_copy(g2.at[n], kg.at[n, :, rows, :], osem.at[2 + n]))
        last.append(send(g2.at[n], kg.at[n, :, rows, :], 68 + n, sibling))
    for copy in last:
        copy.start()
    for d in (1, 3, 2):
        for n in range(2):
            for group in sixth[n::2]:
                group[d].wait()
            rows = kg.at[n, :, sixteen(64 * core, ((cx, cy)[n] + 4 - d) % 4), :]
            forward = send(rows, rows, 68 + 2 * d + n, sibling)
            forward.start()
            last.append(forward)
    for copy in last + [conv_copy, igrad_copy]:
        copy.wait()

    for ch in range(8):
        @pl.when(there[ch])
        def _():
            halo_copy(hs, hr, hsem, hrem, ch).wait_send()
            halo_copy(rs, rr, bsem, brem, ch).wait_send()


def finish(conv, igrad, kg, conv_out, igrad_out, kgrad_out, conv_v, igrad_v, held, wide, sem):
    places = [(conv, conv_v), (igrad, igrad_v)]
    for s in range(3):
        slots = pl.ds(*((0, 5), (5, 5), (10, 4))[s])
        places.append((kg.at[:, slots], held.at[:, slots]))
    loads = [pltpu.make_async_copy(*places[n], sem.at[n]) for n in range(5)]
    for n in (2, 0, 1, 3, 4):
        loads[n].start()
    eye = onehot(iota((128, 128), 0) == iota((128, 128), 1))
    stores = []

    def store(src, dst):
        stores.append(pltpu.make_async_copy(src, dst, sem.at[5 + len(stores)]))
        stores[-1].start()

    for s in range(3):
        loads[2 + s].wait()
        for n, (matrix, slot, count) in enumerate(RUNS[s]):
            for m in range(count):
                wide[matrix + m] = nt(eye, held[n, slot + m])
        part = pl.ds(9 * s, 9)
        store(wide.at[part], kgrad_out.at[part])
        if s == 0:
            loads[0].wait()
            store(conv_v, conv_out)
            loads[1].wait()
            store(igrad_v, igrad_out)
    for copy in stores:
        copy.wait()


def per_device(features, cotangent, kernel, block_count, neighbours, send_face, send_corner):
    vmem = pl.BlockSpec(memory_space=pltpu.VMEM)
    hbm = pl.BlockSpec(memory_space=pltpu.HBM)
    dma = pltpu.SemaphoreType.DMA
    blocks = (32, 64, 128)
    conv, igrad, kg = pl.pallas_call(
        body,
        out_shape=(
            jax.ShapeDtypeStruct(blocks, BF),
            jax.ShapeDtypeStruct(blocks, BF),
            jax.ShapeDtypeStruct((2, 16, 128, 128), BF),
        ),
        in_specs=[hbm] * 6,
        out_specs=(hbm,) * 3,
        scratch_shapes=[
            pltpu.SMEM((1, 4, 8), jnp.int32),
            pltpu.SMEM((1, 2, 4), jnp.int32),
            pltpu.VMEM(blocks, BF),
            pltpu.VMEM(blocks, BF),
            pltpu.VMEM((27, 128, 128), BF),
            pltpu.VMEM((32, 27), jnp.int32),
            pltpu.VMEM((32, 128), F32),
            pltpu.VMEM(blocks, BF),
            pltpu.VMEM(blocks, BF),
            pltpu.VMEM((64, 128, 128), BF),
            pltpu.VMEM((6, 6, 3, 32, 256), BF),
            pltpu.VMEM((4, 4, 2, 32, 256), BF),
            pltpu.VMEM((256, 1024), BF),
            pltpu.VMEM((2, 3, 256, 256), BF),
            pltpu.VMEM((9, 2, 256, 256), BF),
            pltpu.VMEM((27, 128, 128), F32),
            pltpu.VMEM((6, 6, 3, 32, 256), F32),
            pltpu.VMEM((64, 32, 128), F32),
            pltpu.VMEM((27, 32, 128), BF),
            pltpu.VMEM((27, 80, 256), BF),
            pltpu.VMEM((8, 32, 128), BF),
            pltpu.VMEM((8, 128, 32), BF),
            pltpu.VMEM((4, 4, 2, 32, 256), BF),
            pltpu.VMEM((256, 256), BF),
            pltpu.VMEM((256, 256), BF),
            pltpu.VMEM((256, 256), BF),
            pltpu.VMEM((8, 4, 32, 128), BF),
            pltpu.VMEM((8, 4, 32, 128), BF),
            pltpu.VMEM((8, 4, 32, 128), BF),
            pltpu.VMEM((8, 4, 32, 128), BF),
            pltpu.VMEM((27, 128, 128), F32),
            pltpu.VMEM((27, 64, 128), F32),
            pltpu.VMEM((2, 14, 64, 128), F32),
            pltpu.VMEM((2, 3, 14, 16, 128), jnp.int16),
            pltpu.VMEM((2, 3, 14, 16, 128), jnp.int16),
            pltpu.VMEM((2, 16, 16, 128), F32),
            pltpu.VMEM((2, 3, 4, 16, 128), jnp.int16),
            pltpu.VMEM((2, 3, 4, 16, 128), jnp.int16),
            pltpu.VMEM((2, 2, 3, 8, 128), F32),
            pltpu.VMEM((2, 2, 3, 8, 128), F32),
            pltpu.VMEM((2, 64, 128), F32),
            pltpu.VMEM((128, 128), jnp.int16),
            pltpu.VMEM((8, 128), F32),
            pltpu.VMEM((8, 128, 128), jnp.int16),
            pltpu.VMEM((8, 8, 128), F32),
            pltpu.VMEM((2, 16, 16, 128), BF),
            dma((7,)), dma((4,)), dma((8,)), dma((8,)), dma((8,)), dma((8,)),
            dma((3,)), dma((3,)), dma((76,)), dma((76,)),
        ],
        compiler_params=pltpu.CompilerParams(
            collective_id=0, has_side_effects=True, vmem_limit_bytes=62 * 1024 * 1024
        ),
        cost_estimate=pl.CostEstimate(
            flops=7_000_000_000, bytes_accessed=6_000_000, transcendentals=0
        ),
    )(
        send_face,
        jnp.swapaxes(send_corner, 1, 2),
        features.reshape(blocks),
        cotangent.reshape(blocks),
        kernel,
        neighbours,
    )
    conv, igrad, kgrad = pl.pallas_call(
        finish,
        out_shape=(
            jax.ShapeDtypeStruct(blocks, BF),
            jax.ShapeDtypeStruct(blocks, BF),
            jax.ShapeDtypeStruct((27, 128, 128), F32),
        ),
        in_specs=[hbm] * 3,
        out_specs=(hbm, hbm, hbm),
        scratch_shapes=[
            pltpu.VMEM(blocks, BF),
            pltpu.VMEM(blocks, BF),
            pltpu.VMEM((2, 16, 128, 128), BF),
            pltpu.VMEM((27, 128, 128), F32),
            dma((10,)),
        ],
        compiler_params=pltpu.CompilerParams(vmem_limit_bytes=62 * 1024 * 1024),
    )(conv, igrad, kg)
    return conv.reshape(2048, 128), igrad.reshape(2048, 128), kgrad


def solution(mesh):
    in_specs = (
        P(("gx", "gy"), None),
        P(("gx", "gy"), None),
        P(),
        P(("gx", "gy")),
        P(("gx", "gy"), None),
        P(("gx", "gy"), None, None),
        P(("gx", "gy"), None, None),
    )
    out_specs = (P(("gx", "gy"), None), P(("gx", "gy"), None), P())
    return jax.shard_map(
        per_device, mesh=mesh, in_specs=in_specs, out_specs=out_specs, check_vma=False
    )
```

```python
import math

import jax
import jax.numpy as jnp
from jax import lax
from jax.experimental import pallas as pl
from jax.experimental.pallas import tpu as pltpu
from jax.sharding import PartitionSpec as P

MESH = pl.DeviceIdType.MESH
BF = jnp.bfloat16
F32 = jnp.float32

NX, NY, NZ = 4, 4, 8
FACE_WAYS = ((-1, 0), (1, 0), (0, -1), (0, 1))
CORNER_WAYS = ((-1, -1), (-1, 1), (1, -1), (1, 1))
WAYS = FACE_WAYS + CORNER_WAYS


RUNS = (
    ((0, 0, 5), (5, 0, 4)),
    ((9, 5, 4), (13, 4, 5)),
    ((18, 9, 5), (23, 9, 4)),
)


def opposite(channel):
    return channel ^ 1 if channel < 4 else 11 - channel


def side(stride):
    return 0 if stride < 0 else 3


def places(local):
    if local == 0:
        return ((1, 0), (5, 1))
    if local == 3:
        return ((4, 0), (0, -1))
    return ((local + 1, 0),)


def kind(local):
    return 0 if local == 0 else (2 if local == 3 else 1)


def readers(ux, uy, uz):
    found = []
    for px, ox in places(ux):
        for py, oy in places(uy):
            for pz, oz in places(uz):
                found.append((px, py, pz, (ox + 1) * 9 + (oy + 1) * 3 + oz + 1))
    return found


def nn(a, b):
    return lax.dot_general(a, b, (((1,), (0,)), ((), ())), preferred_element_type=F32)


def nt(a, b):
    return lax.dot_general(a, b, (((1,), (1,)), ((), ())), preferred_element_type=F32)


def onehot(mask):
    return jnp.where(mask, 1.0, 0.0).astype(BF)


def iota(shape, dim):
    return lax.broadcasted_iota(jnp.int32, shape, dim)


def encode(rows):
    largest = jnp.max(jnp.abs(rows.reshape(-1, 8, 128)), axis=0)
    for step in (4, 2, 1):
        largest = jnp.maximum(largest, pltpu.roll(largest, step, 0))
    largest = jnp.maximum(largest, 1e-33)
    scale = largest * (1.0 / 32000.0)
    inverse = 32000.0 / largest
    coded = jnp.round(rows.reshape(-1, 8, 128) * inverse[None]).reshape(-1, 128)
    return coded.astype(jnp.int32).astype(jnp.int16), scale


def decode(coded, scale):
    rows = coded.astype(jnp.int32).astype(F32).reshape(-1, 8, 128)
    return (rows * scale[None]).reshape(-1, 128)


def body(
    face_in, corner_in, feat_in, cot_in, ker_in, near_in,
    conv_out, igrad_out, kg,
    face, corner, feat, cot, ker, near, live, conv, igrad,
    et, pz, gz, gt, gty, wt, di, dp, de, oh, oht, bd, bdt, co, perm, pair_perm, part_perm,
    hs, hr, rs, rr,
    wd, rcore, hh, q1, r1, s1, q2, r2, qs, rscale, s2, q3, qs3, r3, rscale3, g2,
    isem, osem, hsem, hrem, brem, csem, crem, asem, arem,
):
    loads = [
        pltpu.make_async_copy(src, dst, isem.at[n])
        for n, (src, dst) in enumerate(
            (
                (face_in, face),
                (corner_in, corner),
                (feat_in, feat),
                (near_in, near),
                (cot_in, cot),
                (ker_in, ker),
            )
        )
    ]
    for copy in loads:
        copy.start()
    gx = lax.axis_index("gx")
    gy = lax.axis_index("gy")
    cy = gx // 16
    cz = (gx // 2) % 8
    cx = (gy // 2) * 2 + gx % 2
    core = gy % 2

    def at(x, y, z, c):
        return ((y * 8 + z) * 2 + x % 2, (x // 2) * 2 + c)

    sibling = (gx, gy // 2 * 2 + (1 - core))
    along_x = [at((cx + d) % NX, cy, cz, core) for d in range(1, NX)]
    along_y = [at(cx, (cy + d) % NY, cz, core) for d in range(1, NY)]
    along_z = [at(cx, cy, (cz + d) % NZ, core) for d in range(1, NZ)]
    halo = [(gx + wx, gy + wy) for wx, wy in WAYS]
    there = [
        (gx + wx >= 0) & (gx + wx < 64) & (gy + wy >= 0) & (gy + wy < 4) for wx, wy in WAYS
    ]

    barrier = pltpu.get_barrier_semaphore()
    greet = [along_z[n] for n in (3, 2, 4, 1, 5, 0, 6)] + along_x + along_y + [sibling]
    greet += [((gx + wx + 64) % 64, (gy + wy + 4) % 4) for wx, wy in WAYS]
    for other in greet:
        pl.semaphore_signal(barrier, inc=1, device_id=other, device_id_type=MESH)

    r256, c256 = iota((256, 256), 0), iota((256, 256), 1)
    perm[...] = onehot(((r256 >> 4) == (c256 & 15)) & ((r256 & 15) == (c256 >> 4)))
    pair_perm[...] = onehot(c256 == (r256 & 15) * 16 + ((r256 >> 4) & 7) * 2 + (r256 >> 7))
    part_perm[...] = onehot(c256 == (r256 & 1) * 128 + ((r256 & 15) >> 1) * 16 + (r256 >> 4))
    eye = onehot(iota((128, 128), 0) == iota((128, 128), 1))
    eye256 = onehot(r256 == c256)

    def swap16(v):
        return nn(perm[...], v.reshape(256, 128)).reshape(16, 16, 128)

    r32, c32 = iota((32, 128), 0), iota((32, 128), 1)
    same_z = (r32 >> 3) == (c32 >> 5)
    loads[0].wait()
    loads[1].wait()
    for ch in range(8):
        index = jnp.full((32, 128), -1, jnp.int32)
        for n in range(8 if ch < 4 else 2):
            slot = n if ch < 4 else 2 * (opposite(ch) - 4) + n
            block = face[0, ch, n] if ch < 4 else corner[0, n, ch - 4]
            index = jnp.where((r32 & 7) == slot, block, index)
        pick = onehot(same_z & (index == (c32 & 31)))
        bd[ch] = pick
        bdt[ch] = nt(eye, pick).astype(BF)

    loads[2].wait()
    for hb in range(2):
        for ug in range(4):
            rows = swap16(feat[pl.ds(16 * hb, 16), pl.ds(16 * ug, 16), :])
            et[pl.ds(16 * ug, 16), pl.ds(16 * hb, 16), :] = rows.astype(BF)

    def rim_base(ch, chunk):
        wx, wy = WAYS[ch]
        ux = side(wx) if wx != 0 else chunk
        uy = side(wy) if wy != 0 else chunk
        return ux * 16 + uy * 4

    def chunks(ch):
        return 4 if ch < 4 else 1

    for ch in range(8):
        for chunk in range(chunks(ch)):
            source = et[pl.ds(rim_base(ch, chunk), 4), pl.ds(0, 32), :].reshape(128, 128)
            hs[ch, chunk] = nn(bd[ch], source).astype(BF)

    pl.semaphore_wait(barrier, len(greet))

    def part(buf, ch):
        return buf.at[ch] if ch < 4 else buf.at[ch, pl.ds(0, 1)]

    def halo_copy(src, dst, ss, rs_, ch):
        return pltpu.make_async_remote_copy(
            src_ref=part(src, ch),
            dst_ref=part(dst, opposite(ch)),
            send_sem=ss.at[ch],
            recv_sem=rs_.at[opposite(ch)],
            device_id=halo[ch],
            device_id_type=MESH,
        )

    def halo_arrived(src, dst, ss, rs_, ch):
        return pltpu.make_async_remote_copy(
            src_ref=part(src, ch),
            dst_ref=part(dst, ch),
            send_sem=ss.at[ch],
            recv_sem=rs_.at[ch],
            device_id=halo[ch],
            device_id_type=MESH,
        )

    for ch in range(8):
        @pl.when(there[ch])
        def _():
            halo_copy(hs, hr, hsem, hrem, ch).start()

    loads[3].wait()
    live[...] = jnp.where(near[:, 13:14] == r32, 1.0, 0.0)
    lives = [live[pl.ds(16 * hb, 16), :] for hb in range(2)]
    loads[4].wait()
    for x in range(4):
        for hb in range(2):
            rows = cot[pl.ds(16 * hb, 16), pl.ds(16 * x, 16), :].reshape(256, 128)
            rows = nn(pair_perm[...], rows).reshape(2, 4, 2, 16, 128) * lives[hb]
            for n in range(2):
                gz[x, :, :, pl.ds(16 * hb, 16), pl.ds(128 * n, 128)] = rows[n].astype(BF)
    for x in range(4):
        turned = nt(eye256, gz[x].reshape(256, 256))
        place = pl.ds(256 * x, 256)
        gt[:, place] = turned.astype(BF)
    for n, y in enumerate((0, 3)):
        turned = nt(eye256, gz[:, y].reshape(256, 256))
        gty[n, 0] = jnp.where(c256 < 64, 0.0, turned).astype(BF)
        gty[n, 1] = turned.astype(BF)
        gty[n, 2] = jnp.where(c256 < 192, turned, 0.0).astype(BF)

    for u in range(64):
        et[u, pl.ds(32, 48), :] = jnp.zeros((48, 128), BF)

    columns = c32 + jnp.where(c32 >= 32, 1, 0)
    for o in range(27):
        oh[o] = onehot(near[:, o : o + 1] == columns)

    def offsets_of(tx, ty, tz):
        pick = (0, 1, 3)
        return [r[3] for r in readers(pick[tx], pick[ty], pick[tz])]

    def stacked(offsets):
        if len(offsets) == 1:
            return oh[offsets[0]]
        return jnp.concatenate([oh[o] for o in offsets], axis=0)

    def inner(found):
        return [r for r in found if 1 <= r[0] <= 4 and 1 <= r[1] <= 4]

    def outer(found):
        return [r for r in found if not (1 <= r[0] <= 4 and 1 <= r[1] <= 4)]

    def keep(rows, found):
        for n, (px, py, p, _) in enumerate(found):
            pz[px, py, p // 2, :, pl.ds(128 * (p % 2), 128)] = rows[32 * n : 32 * n + 32]

    for py in (0, 5):
        pz[pl.ds(1, 4), py] = jnp.zeros((4, 3, 32, 256), BF)
    for ux in range(4):
        for uy in range(4):
            for uz in range(4):
                found = inner(readers(ux, uy, uz))
                picks = stacked([r[3] for r in found])[:, :32]
                keep(nn(picks, et[ux * 16 + uy * 4 + uz, pl.ds(0, 32)]).astype(BF), found)

    mine = pl.multiple_of(64 * core, 64)
    other = pl.multiple_of(64 - 64 * core, 64)

    def core_copy(s):
        return pltpu.make_async_remote_copy(
            src_ref=wd.at[pl.ds(9 * s, 9), pl.ds(other, 64), :],
            dst_ref=rcore.at[pl.ds(9 * s, 9)],
            send_sem=csem.at[s],
            recv_sem=crem.at[s],
            device_id=sibling,
            device_id_type=MESH,
        )

    def blocks_of(d0, d1):
        return (
            d0[:128, :128] + d0[128:, 128:],
            d0[:128, 128:] + d1[128:, :128],
            d1[:128, :128] + d1[128:, 128:],
        )

    for kx in range(3):
        x0, x1 = ((1, 4), (0, 4), (0, 3))[kx]
        for ky in range(3):
            left = gt[:, pl.ds(256 * x0, 256 * (x1 - x0))]
            sums = [
                nn(
                    left,
                    pz[pl.ds(x0 + kx, x1 - x0), pl.ds(ky, 4), pl.ds(w, 2)].reshape(-1, 256),
                )
                for w in range(2)
            ]
            for n, value in enumerate(blocks_of(*sums)):
                if kx == 1 and ky == 1:
                    wd[9 * kx + 3 * ky + n] = value
                else:
                    di[9 * kx + 3 * ky + n] = value

    for ch in range(8):
        @pl.when(there[ch])
        def _():
            halo_arrived(hs, hr, hsem, hrem, ch).wait_recv()
            wx, wy = WAYS[ch]
            for chunk in range(chunks(ch)):
                ux = side(-wx) if wx != 0 else chunk
                uy = side(-wy) if wy != 0 else chunk
                got = hr[ch, chunk].astype(F32).reshape(4, 8, 128)
                none = jnp.zeros((4, 8, 128), F32)
                pair = (got, none) if ch >= 4 or ch % 2 == 0 else (none, got)
                start = 64 if ch >= 4 else 32 + 16 * (ch // 2)
                et[pl.ds(ux * 16 + uy * 4, 4), pl.ds(start, 16), :] = jnp.concatenate(
                    pair, axis=1
                ).astype(BF)

    for ux in range(4):
        for uy in range(4):
            for uz in range(4):
                found = outer(readers(ux, uy, uz))
                if found:
                    picks = stacked([r[3] for r in found])
                    keep(nn(picks[:, :80], et[ux * 16 + uy * 4 + uz]).astype(BF), found)

    def send(src, dst, ns, nr, device):
        pltpu.make_async_remote_copy(
            src_ref=src,
            dst_ref=dst,
            send_sem=asem.at[ns],
            recv_sem=arem.at[nr],
            device_id=device,
            device_id_type=MESH,
        ).start()

    def counted(ref, ns, nr):
        return pltpu.make_async_remote_copy(
            src_ref=ref,
            dst_ref=ref,
            send_sem=asem.at[ns],
            recv_sem=arem.at[nr],
            device_id=sibling,
            device_id_type=MESH,
        )

    def arrived(ref, nr):
        counted(ref, 0, nr).wait_recv()

    def sent(ref, ns):
        counted(ref, ns, 0).wait_send()

    def sixteen(first, index):
        return pl.ds(pl.multiple_of(first + 16 * index, 16), 16)

    def quarter(index):
        return pl.ds(4 * index, 4)

    def core_sum(s):
        core_copy(s).wait()
        for n, (matrix, slot, count) in enumerate(RUNS[s]):
            kept = wd[pl.ds(matrix, count), pl.ds(mine, 64), :]
            hh[n, pl.ds(slot, count)] = kept + rcore[pl.ds(matrix, count)]

    def outer_sums(kx, ky, w):
        total = None
        if ky != 1:
            rows = pz[pl.ds(kx, 4), (0, None, 5)[ky], pl.ds(w, 2)].reshape(256, 256)
            total = nn(gty[ky // 2, kx], rows)
        if kx != 1:
            x, px = ((0, 0), None, (3, 5))[kx]
            rows = pz[px, pl.ds(ky, 4), pl.ds(w, 2)].reshape(256, 256)
            term = nn(gt[:, pl.ds(256 * x, 256)], rows)
            total = term if total is None else total + term
        return total

    for s in (1, 0, 2):
        for ky in range(3):
            if s == 1 and ky == 1:
                continue
            value = blocks_of(outer_sums(s, ky, 0), outer_sums(s, ky, 1))
            for n in range(3):
                j = 9 * s + 3 * ky + n
                wd[j] = di[j] + value[n]
        core_copy(s).start()
    for s in (1, 0, 2):
        core_sum(s)

    far_first = (2, 1, 3)
    for n in range(2):
        size = (14, 13)[n]
        for d in far_first:
            rows = sixteen(0, ((cx, cy)[n] + d) % 4)
            coded, scale = encode(hh[n, pl.ds(0, size), rows, :].reshape(-1, 128))
            q1[n, d - 1, pl.ds(0, size)] = coded.reshape(size, 16, 128)
            qs[0, n, d - 1] = scale
            device = (along_x, along_y)[n][d - 1]
            send(
                q1.at[n, d - 1, pl.ds(0, size)],
                r1.at[n, d - 1, pl.ds(0, size)],
                n,
                n,
                (along_x, along_y)[n][d - 1],
            )
            send(qs.at[0, n, d - 1], rscale.at[0, n, d - 1], 2, 2, (along_x, along_y)[n][d - 1])

    def weights(j, carry):
        low, mid, high = ker[3 * j], ker[3 * j + 1], ker[3 * j + 2]
        none = jnp.zeros((128, 128), BF)
        wt[j, 0, pl.ds(0, 128), pl.ds(0, 128)] = low
        wt[j, 0, pl.ds(0, 128), pl.ds(128, 128)] = none
        wt[j, 0, pl.ds(128, 128), pl.ds(0, 128)] = mid
        wt[j, 0, pl.ds(128, 128), pl.ds(128, 128)] = low
        wt[j, 1, pl.ds(0, 128), pl.ds(0, 128)] = high
        wt[j, 1, pl.ds(0, 128), pl.ds(128, 128)] = mid
        wt[j, 1, pl.ds(128, 128), pl.ds(0, 128)] = none
        wt[j, 1, pl.ds(128, 128), pl.ds(128, 128)] = high
        return carry

    loads[5].wait()
    lax.fori_loop(0, 9, weights, 0)

    for tx in range(3):
        for ty in range(3):
            for tz in range(3):
                offs = offsets_of(tx, ty, tz)
                flipped = nt(eye[:80], stacked(offs)).astype(BF)
                oht[tx * 9 + ty * 3 + tz, :, pl.ds(0, 32 * len(offs))] = flipped

    def clear_dp(x, carry):
        dp[x] = jnp.zeros((6, 3, 32, 256), F32)
        return carry

    lax.fori_loop(0, 6, clear_dp, 0)

    for px in range(6):
        for ky in range(3):
            for w in range(2):
                term = None
                for kx in range(3):
                    if 0 <= px - kx < 4:
                        one = nt(gz[px - kx].reshape(256, 256), wt[3 * kx + ky, w])
                        term = one if term is None else term + one
                dp[px, pl.ds(ky, 4), pl.ds(w, 2)] += term.reshape(4, 2, 32, 256)

    arrived(r1.at[0], 0)
    arrived(r1.at[1, :, pl.ds(0, 13)], 1)
    arrived(rscale.at[0], 2)
    for n in range(2):
        size = (14, 13)[n]
        total = hh[n, pl.ds(0, size), sixteen(0, (cx, cy)[n]), :]
        for d in range(3):
            got = decode(r1[n, d, pl.ds(0, size)].reshape(-1, 128), rscale[0, n, d])
            total = total + got.reshape(size, 16, 128)
        s1[n, pl.ds(0, size)] = total
        s1[n, pl.ds(size, 16 - size)] = jnp.zeros((16 - size, 16, 128), F32)

    for n in range(2):
        for d in far_first:
            coded, scale = encode(s1[n, quarter(((cy, cx)[n] + d) % 4)].reshape(64, 128))
            q2[n, d - 1] = coded.reshape(4, 16, 128)
            qs[1, n, d - 1] = scale
            device = (along_y, along_x)[n][d - 1]
            send(q2.at[n, d - 1], r2.at[n, d - 1], 3, 3, device)
            send(qs.at[1, n, d - 1], rscale.at[1, n, d - 1], 4, 4, device)

    for ux in range(4):
        for uy in range(4):
            pieces = []
            for uz in range(4):
                found = readers(ux, uy, uz)
                high, low = [], []
                for px, py, p, _ in found:
                    value = dp[px, py, p // 2, :, pl.ds(128 * (p % 2), 128)]
                    top = value.astype(BF)
                    high.append(top)
                    low.append((value - top.astype(F32)).astype(BF))
                high = jnp.concatenate(high, axis=0) if len(high) > 1 else high[0]
                low = jnp.concatenate(low, axis=0) if len(low) > 1 else low[0]
                group = kind(ux) * 9 + kind(uy) * 3 + kind(uz)
                res = nn(
                    oht[group, :, pl.ds(0, 32 * len(found))],
                    jnp.concatenate([high, low], axis=1),
                )
                res = res[:, :128] + res[:, 128:]
                de[ux * 16 + uy * 4 + uz] = res[:32]
                pieces.append(res)

            def give(slot, chunk, row):
                rs[slot, chunk] = jnp.concatenate(
                    [piece[row : row + 8] for piece in pieces], axis=0
                ).astype(BF)

            for slot in range(8):
                wx, wy = WAYS[slot]
                if (wx != 0 and ux != side(-wx)) or (wy != 0 and uy != side(-wy)):
                    continue
                chunk = 0 if slot >= 4 else (uy if wx != 0 else ux)
                give(slot, chunk, 64 if slot >= 4 else 32 + 8 * slot)

    for ch in range(8):
        @pl.when(there[ch])
        def _():
            halo_copy(hs, hr, hsem, hrem, ch).wait_send()
            halo_copy(rs, rr, hsem, brem, ch).start()

        @pl.when(jnp.logical_not(there[ch]))
        def _():
            rr[ch] = jnp.zeros((4, 32, 128), BF)

    def convolve(x):
        total = jnp.zeros((256, 256), F32)
        for kx in range(3):
            for ky in range(3):
                for w in range(2):
                    rows = pz[x + kx, pl.ds(ky, 4), pl.ds(w, 2)].reshape(256, 256)
                    total = total + nn(rows, wt[3 * kx + ky, w])
        alive = jnp.concatenate([live[...], live[...]], axis=1)
        co[x] = (total.reshape(4, 2, 32, 256) * alive).astype(BF)
    convolve(0)
    convolve(1)

    arrived(r2, 3)
    arrived(rscale.at[1], 4)
    for n in range(2):
        total = s1[n, quarter((cy, cx)[n])].reshape(64, 128)
        for d in range(3):
            total = total + decode(r2[n, d].reshape(64, 128), rscale[1, n, d])
        s2[n] = total

    coded, scale = encode(s2[...].reshape(128, 128))
    q3[...] = coded
    qs3[...] = scale
    r3[pl.ds(cz, 1)] = coded[None]
    rscale3[pl.ds(cz, 1)] = scale[None]
    for d in (4, 3, 5, 2, 6, 1, 7):
        send(q3, r3.at[cz], 5, 5, along_z[d - 1])
        send(qs3, rscale3.at[cz], 6, 6, along_z[d - 1])

    convolve(2)
    convolve(3)
    for x in range(4):
        for hb in range(2):
            parts = [
                co[x, :, :, pl.ds(16 * hb, 16), pl.ds(128 * n, 128)].reshape(128, 128)
                for n in range(2)
            ]
            rows = nn(part_perm[...], jnp.concatenate(parts, axis=0)).reshape(16, 16, 128)
            conv[pl.ds(16 * hb, 16), pl.ds(16 * x, 16), :] = rows.astype(BF)

    conv_copy = pltpu.make_async_copy(conv, conv_out, osem.at[0])
    conv_copy.start()

    for ch in range(8):
        @pl.when(there[ch])
        def _():
            halo_arrived(rs, rr, hsem, brem, ch).wait_recv()

    for ux in range(4):
        parts = []
        for uy in range(4):
            rows = de[pl.ds(ux * 16 + uy * 4, 4)].reshape(128, 128)
            for ch in range(8):
                wx, wy = WAYS[ch]
                if (wx != 0 and ux != side(wx)) or (wy != 0 and uy != side(wy)):
                    continue
                chunk = 0 if ch >= 4 else (uy if wx != 0 else ux)
                rows = rows + nn(bdt[ch], rr[ch, chunk])
            parts.append(rows.astype(BF).reshape(4, 32, 128))
        parts = jnp.concatenate(parts, axis=0)
        for hb in range(2):
            swapped = swap16(parts[:, 16 * hb : 16 * hb + 16])
            igrad[pl.ds(16 * hb, 16), pl.ds(16 * ux, 16), :] = swapped.astype(BF)

    igrad_copy = pltpu.make_async_copy(igrad, igrad_out, osem.at[1])
    igrad_copy.start()

    arrived(r3.at[pl.ds(0, 7)], 5)
    arrived(rscale3.at[pl.ds(0, 7)], 6)
    whole = decode(r3[0], rscale3[0])
    for z in range(1, 8):
        whole = whole + decode(r3[z], rscale3[z])
    whole = (whole * (1.0 / math.sqrt(256 * 32 * 64))).reshape(2, 4, 16, 128).astype(BF)
    g2[0, quarter(cy)] = whole[0]
    g2[1, quarter(cx)] = whole[1]

    def across(n, away):
        index = ((cy, cx)[n] + 4 - away) % 4
        rows = sixteen(64 * core, (cx, cy)[n])

        def go(slots):
            for d in far_first:
                send(
                    g2.at[n, slots],
                    kg.at[n, slots, rows, :],
                    9 + n,
                    11 + 2 * d + n,
                    (along_x, along_y)[n][d - 1],
                )

        @pl.when(index < 3)
        def _():
            go(quarter(index))

        @pl.when(index == 3)
        def _():
            go(pl.ds(12, (2, 1)[n]))

    for d in far_first:
        for n in range(2):
            piece = g2.at[n, quarter((cy, cx)[n])]
            send(piece, piece, 7 + n, 5 + 2 * d + n, (along_y, along_x)[n][d - 1])
    for n in range(2):
        across(n, 0)
    for d in (1, 3, 2):
        for n in range(2):
            arrived(g2.at[n, quarter(((cy, cx)[n] + 4 - d) % 4)], 5 + 2 * d + n)
            across(n, d)

    own = []
    slots = (pl.ds(0, 14), pl.ds(0, 13))
    for n in range(2):
        rows = kg.at[n, slots[n], sixteen(64 * core, (cx, cy)[n]), :]
        own.append(pltpu.make_async_copy(g2.at[n, slots[n]], rows, osem.at[2 + n]))
        own[n].start()
        send(g2.at[n, slots[n]], rows, 11 + n, 19 + n, sibling)
    for d in (1, 3, 2):
        for n in range(2):
            rows = kg.at[n, slots[n], sixteen(64 * core, ((cx, cy)[n] + 4 - d) % 4), :]
            arrived(rows, 11 + 2 * d + n)
            send(rows, rows, 11 + n, 19 + n, sibling)

    sent(q1.at[0], 0)
    sent(q1.at[1, :, pl.ds(0, 13)], 1)
    sent(qs.at[0], 2)
    sent(q2, 3)
    sent(qs.at[1], 4)
    sent(r3.at[pl.ds(0, 7)], 5)
    sent(rscale3.at[pl.ds(0, 7)], 6)
    for ch in range(8):
        @pl.when(there[ch])
        def _():
            halo_copy(rs, rr, hsem, brem, ch).wait_send()
    for copy in own + [conv_copy, igrad_copy]:
        copy.wait()
    for n in range(2):
        sent(g2.at[n, pl.ds(0, 12)], 7 + n)
        sent(kg.at[n, slots[n], pl.ds(0, 48), :], 9 + n)
        sent(kg.at[n, slots[n], pl.ds(0, 64), :], 11 + n)
        arrived(kg.at[n, slots[n], pl.ds(other, 64), :], 19 + n)


def finish(conv, igrad, kg, conv_out, igrad_out, kgrad_out, conv_v, igrad_v, held, wide, sem):
    places = [(conv, conv_v), (igrad, igrad_v)]
    for s in range(3):
        slots = pl.ds(*((0, 5), (5, 5), (10, 4))[s])
        places.append((kg.at[:, slots], held.at[:, slots]))
    loads = [pltpu.make_async_copy(*places[n], sem.at[n]) for n in range(5)]
    for n in (2, 0, 1, 3, 4):
        loads[n].start()
    stores = []

    def store(src, dst):
        stores.append(pltpu.make_async_copy(src, dst, sem.at[5 + len(stores)]))
        stores[-1].start()

    for s in range(3):
        loads[2 + s].wait()
        for n, (matrix, slot, count) in enumerate(RUNS[s]):
            for m in range(count):
                wide[matrix + m] = held[n, slot + m].astype(F32).T
        part = pl.ds(9 * s, 9)
        store(wide.at[part], kgrad_out.at[part])
        if s == 0:
            loads[0].wait()
            store(conv_v, conv_out)
            loads[1].wait()
            store(igrad_v, igrad_out)
    for copy in stores:
        copy.wait()


def per_device(features, cotangent, kernel, block_count, neighbours, send_face, send_corner):
    vmem = pl.BlockSpec(memory_space=pltpu.VMEM)
    hbm = pl.BlockSpec(memory_space=pltpu.HBM)
    dma = pltpu.SemaphoreType.DMA
    blocks = (32, 64, 128)
    conv, igrad, kg = pl.pallas_call(
        body,
        out_shape=(
            jax.ShapeDtypeStruct(blocks, BF),
            jax.ShapeDtypeStruct(blocks, BF),
            jax.ShapeDtypeStruct((2, 16, 128, 128), BF),
        ),
        in_specs=[hbm] * 6,
        out_specs=(hbm,) * 3,
        scratch_shapes=[
            pltpu.SMEM((1, 4, 8), jnp.int32),
            pltpu.SMEM((1, 2, 4), jnp.int32),
            pltpu.VMEM(blocks, BF),
            pltpu.VMEM(blocks, BF),
            pltpu.VMEM((27, 128, 128), BF),
            pltpu.VMEM((32, 27), jnp.int32),
            pltpu.VMEM((32, 128), F32),
            pltpu.VMEM(blocks, BF),
            pltpu.VMEM(blocks, BF),
            pltpu.VMEM((64, 80, 128), BF),
            pltpu.VMEM((6, 6, 3, 32, 256), BF),
            pltpu.VMEM((4, 4, 2, 32, 256), BF),
            pltpu.VMEM((256, 1024), BF),
            pltpu.VMEM((2, 3, 256, 256), BF),
            pltpu.VMEM((9, 2, 256, 256), BF),
            pltpu.VMEM((27, 128, 128), F32),
            pltpu.VMEM((6, 6, 3, 32, 256), F32),
            pltpu.VMEM((64, 32, 128), F32),
            pltpu.VMEM((27, 32, 128), BF),
            pltpu.VMEM((27, 80, 256), BF),
            pltpu.VMEM((8, 32, 128), BF),
            pltpu.VMEM((8, 128, 32), BF),
            pltpu.VMEM((4, 4, 2, 32, 256), BF),
            pltpu.VMEM((256, 256), BF),
            pltpu.VMEM((256, 256), BF),
            pltpu.VMEM((256, 256), BF),
            pltpu.VMEM((8, 4, 32, 128), BF),
            pltpu.VMEM((8, 4, 32, 128), BF),
            pltpu.VMEM((8, 4, 32, 128), BF),
            pltpu.VMEM((8, 4, 32, 128), BF),
            pltpu.VMEM((27, 128, 128), F32),
            pltpu.VMEM((27, 64, 128), F32),
            pltpu.VMEM((2, 14, 64, 128), F32),
            pltpu.VMEM((2, 3, 14, 16, 128), jnp.int16),
            pltpu.VMEM((2, 3, 14, 16, 128), jnp.int16),
            pltpu.VMEM((2, 16, 16, 128), F32),
            pltpu.VMEM((2, 3, 4, 16, 128), jnp.int16),
            pltpu.VMEM((2, 3, 4, 16, 128), jnp.int16),
            pltpu.VMEM((2, 2, 3, 8, 128), F32),
            pltpu.VMEM((2, 2, 3, 8, 128), F32),
            pltpu.VMEM((2, 64, 128), F32),
            pltpu.VMEM((128, 128), jnp.int16),
            pltpu.VMEM((8, 128), F32),
            pltpu.VMEM((8, 128, 128), jnp.int16),
            pltpu.VMEM((8, 8, 128), F32),
            pltpu.VMEM((2, 16, 16, 128), BF),
            dma((6,)), dma((4,)), dma((8,)), dma((8,)), dma((8,)),
            dma((3,)), dma((3,)), dma((13,)), dma((21,)),
        ],
        compiler_params=pltpu.CompilerParams(
            collective_id=0, has_side_effects=True, vmem_limit_bytes=62 * 1024 * 1024
        ),
        cost_estimate=pl.CostEstimate(
            flops=7_000_000_000, bytes_accessed=6_000_000, transcendentals=0
        ),
    )(
        send_face,
        jnp.swapaxes(send_corner, 1, 2),
        features.reshape(blocks),
        cotangent.reshape(blocks),
        kernel,
        neighbours,
    )
    conv, igrad, kgrad = pl.pallas_call(
        finish,
        out_shape=(
            jax.ShapeDtypeStruct(blocks, BF),
            jax.ShapeDtypeStruct(blocks, BF),
            jax.ShapeDtypeStruct((27, 128, 128), F32),
        ),
        in_specs=[hbm] * 3,
        out_specs=(hbm, hbm, hbm),
        scratch_shapes=[
            pltpu.VMEM(blocks, BF),
            pltpu.VMEM(blocks, BF),
            pltpu.VMEM((2, 16, 128, 128), BF),
            pltpu.VMEM((27, 128, 128), F32),
            dma((10,)),
        ],
        compiler_params=pltpu.CompilerParams(vmem_limit_bytes=62 * 1024 * 1024),
    )(conv, igrad, kg)
    return conv.reshape(2048, 128), igrad.reshape(2048, 128), kgrad


def solution(mesh):
    in_specs = (
        P(("gx", "gy"), None),
        P(("gx", "gy"), None),
        P(),
        P(("gx", "gy")),
        P(("gx", "gy"), None),
        P(("gx", "gy"), None, None),
        P(("gx", "gy"), None, None),
    )
    out_specs = (P(("gx", "gy"), None), P(("gx", "gy"), None), P())
    return jax.shard_map(
        per_device, mesh=mesh, in_specs=in_specs, out_specs=out_specs, check_vma=False
    )
```

```python
import math

import jax
import jax.numpy as jnp
from jax import lax
from jax.experimental import pallas as pl
from jax.experimental.pallas import tpu as pltpu
from jax.sharding import PartitionSpec as P

MESH = pl.DeviceIdType.MESH
BF = jnp.bfloat16
F32 = jnp.float32

NX, NY, NZ = 4, 4, 8
FACE_WAYS = ((-1, 0), (1, 0), (0, -1), (0, 1))
CORNER_WAYS = ((-1, -1), (-1, 1), (1, -1), (1, 1))
WAYS = FACE_WAYS + CORNER_WAYS


RUNS = (
    ((0, 0, 5), (5, 0, 4)),
    ((9, 5, 4), (13, 4, 5)),
    ((18, 9, 5), (23, 9, 4)),
)


def opposite(channel):
    return channel ^ 1 if channel < 4 else 11 - channel


def side(stride):
    return 0 if stride < 0 else 3


def places(local):
    if local == 0:
        return ((1, 0), (5, 1))
    if local == 3:
        return ((4, 0), (0, -1))
    return ((local + 1, 0),)


def kind(local):
    return 0 if local == 0 else (2 if local == 3 else 1)


def readers(ux, uy, uz):
    found = []
    for px, ox in places(ux):
        for py, oy in places(uy):
            for pz, oz in places(uz):
                found.append((px, py, pz, (ox + 1) * 9 + (oy + 1) * 3 + oz + 1))
    return found


def nn(a, b):
    return lax.dot_general(a, b, (((1,), (0,)), ((), ())), preferred_element_type=F32)


def nt(a, b):
    return lax.dot_general(a, b, (((1,), (1,)), ((), ())), preferred_element_type=F32)


def onehot(mask):
    return jnp.where(mask, 1.0, 0.0).astype(BF)


def iota(shape, dim):
    return lax.broadcasted_iota(jnp.int32, shape, dim)


def encode(rows):
    largest = jnp.max(jnp.abs(rows.reshape(-1, 8, 128)), axis=0)
    for step in (4, 2, 1):
        largest = jnp.maximum(largest, pltpu.roll(largest, step, 0))
    largest = jnp.maximum(largest, 1e-33)
    scale = largest * (1.0 / 32000.0)
    inverse = 32000.0 / largest
    coded = jnp.round(rows.reshape(-1, 8, 128) * inverse[None]).reshape(-1, 128)
    return coded.astype(jnp.int32).astype(jnp.int16), scale


def decode(coded, scale):
    rows = coded.astype(jnp.int32).astype(F32).reshape(-1, 8, 128)
    return (rows * scale[None]).reshape(-1, 128)


def body(
    face_in, corner_in, feat_in, cot_in, ker_in, near_in,
    conv, igrad, kg,
    face, corner, feat, cot, ker, near, live,
    et, pz, gz, gt, gty, wt, di, dp, de, oh, oht, bd, bdt, co, perm, pair_perm, part_perm,
    hs, hr, rs, rr,
    wd, rcore, hh, q1, r1, s1, q2, r2, qs, rscale, s2, q3, qs3, r3, rscale3, g2,
    isem, osem, hsem, hrem, brem, csem, crem, asem, arem,
):
    loads = [
        pltpu.make_async_copy(src, dst, isem.at[n])
        for n, (src, dst) in enumerate(
            (
                (face_in, face),
                (corner_in, corner),
                (feat_in, feat),
                (near_in, near),
                (cot_in, cot),
                (ker_in, ker),
            )
        )
    ]
    for copy in loads:
        copy.start()
    gx = lax.axis_index("gx")
    gy = lax.axis_index("gy")
    cy = gx // 16
    cz = (gx // 2) % 8
    cx = (gy // 2) * 2 + gx % 2
    core = gy % 2

    def at(x, y, z, c):
        return ((y * 8 + z) * 2 + x % 2, (x // 2) * 2 + c)

    sibling = (gx, gy // 2 * 2 + (1 - core))
    along_x = [at((cx + d) % NX, cy, cz, core) for d in range(1, NX)]
    along_y = [at(cx, (cy + d) % NY, cz, core) for d in range(1, NY)]
    along_z = [at(cx, cy, (cz + d) % NZ, core) for d in range(1, NZ)]
    halo = [(gx + wx, gy + wy) for wx, wy in WAYS]
    there = [
        (gx + wx >= 0) & (gx + wx < 64) & (gy + wy >= 0) & (gy + wy < 4) for wx, wy in WAYS
    ]

    barrier = pltpu.get_barrier_semaphore()
    greet = [along_z[n] for n in (3, 2, 4, 1, 5, 0, 6)] + along_x + along_y + [sibling]
    expected = len(greet)
    for other in greet:
        pl.semaphore_signal(barrier, inc=1, device_id=other, device_id_type=MESH)
    for ch in (4, 5, 6, 7, 0, 1, 2, 3):
        expected = expected + there[ch].astype(jnp.int32)

        @pl.when(there[ch])
        def _():
            pl.semaphore_signal(barrier, inc=1, device_id=halo[ch], device_id_type=MESH)

    r256, c256 = iota((256, 256), 0), iota((256, 256), 1)
    perm[...] = onehot(((r256 >> 4) == (c256 & 15)) & ((r256 & 15) == (c256 >> 4)))
    pair_perm[...] = onehot(c256 == (r256 & 15) * 16 + ((r256 >> 4) & 7) * 2 + (r256 >> 7))
    part_perm[...] = onehot(c256 == (r256 & 1) * 128 + ((r256 & 15) >> 1) * 16 + (r256 >> 4))
    eye = onehot(iota((128, 128), 0) == iota((128, 128), 1))
    eye256 = onehot(r256 == c256)

    def swap16(v):
        return nn(perm[...], v.reshape(256, 128)).reshape(16, 16, 128)

    r32, c32 = iota((32, 128), 0), iota((32, 128), 1)
    same_z = (r32 >> 3) == (c32 >> 5)
    loads[0].wait()
    loads[1].wait()
    for ch in range(8):
        index = jnp.full((32, 128), -1, jnp.int32)
        for n in range(8 if ch < 4 else 2):
            slot = n if ch < 4 else 2 * (opposite(ch) - 4) + n
            block = face[0, ch, n] if ch < 4 else corner[0, n, ch - 4]
            index = jnp.where((r32 & 7) == slot, block, index)
        pick = onehot(same_z & (index == (c32 & 31)))
        bd[ch] = pick
        bdt[ch] = nt(eye, pick).astype(BF)

    loads[2].wait()
    for hb in range(2):
        for ug in range(4):
            rows = swap16(feat[pl.ds(16 * hb, 16), pl.ds(16 * ug, 16), :])
            et[pl.ds(16 * ug, 16), pl.ds(16 * hb, 16), :] = rows.astype(BF)

    def rim_base(ch, chunk):
        wx, wy = WAYS[ch]
        ux = side(wx) if wx != 0 else chunk
        uy = side(wy) if wy != 0 else chunk
        return ux * 16 + uy * 4

    def chunks(ch):
        return 4 if ch < 4 else 1

    for ch in range(8):
        for chunk in range(chunks(ch)):
            source = et[pl.ds(rim_base(ch, chunk), 4), pl.ds(0, 32), :].reshape(128, 128)
            hs[ch, chunk] = nn(bd[ch], source).astype(BF)

    pl.semaphore_wait(barrier, expected)

    def part(buf, ch):
        return buf.at[ch] if ch < 4 else buf.at[ch, pl.ds(0, 1)]

    def halo_copy(src, dst, ss, rs_, ch):
        return pltpu.make_async_remote_copy(
            src_ref=part(src, ch),
            dst_ref=part(dst, opposite(ch)),
            send_sem=ss.at[ch],
            recv_sem=rs_.at[opposite(ch)],
            device_id=halo[ch],
            device_id_type=MESH,
        )

    def halo_arrived(src, dst, ss, rs_, ch):
        return pltpu.make_async_remote_copy(
            src_ref=part(src, ch),
            dst_ref=part(dst, ch),
            send_sem=ss.at[ch],
            recv_sem=rs_.at[ch],
            device_id=halo[ch],
            device_id_type=MESH,
        )

    for ch in (4, 5, 6, 7, 0, 1, 2, 3):
        @pl.when(there[ch])
        def _():
            halo_copy(hs, hr, hsem, hrem, ch).start()

    loads[3].wait()
    live[...] = jnp.where(near[:, 13:14] == r32, 1.0, 0.0)
    lives = [live[pl.ds(16 * hb, 16), :] for hb in range(2)]
    loads[4].wait()
    for x in range(4):
        for hb in range(2):
            rows = cot[pl.ds(16 * hb, 16), pl.ds(16 * x, 16), :].reshape(256, 128)
            rows = nn(pair_perm[...], rows).reshape(2, 4, 2, 16, 128) * lives[hb]
            for n in range(2):
                gz[x, :, :, pl.ds(16 * hb, 16), pl.ds(128 * n, 128)] = rows[n].astype(BF)
    for x in range(4):
        turned = nt(eye256, gz[x].reshape(256, 256))
        place = pl.ds(256 * x, 256)
        gt[:, place] = turned.astype(BF)
    for n, y in enumerate((0, 3)):
        turned = nt(eye256, gz[:, y].reshape(256, 256))
        gty[n, 0] = jnp.where(c256 < 64, 0.0, turned).astype(BF)
        gty[n, 1] = turned.astype(BF)
        gty[n, 2] = jnp.where(c256 < 192, turned, 0.0).astype(BF)

    for u in range(64):
        et[u, pl.ds(32, 48), :] = jnp.zeros((48, 128), BF)

    columns = c32 + jnp.where(c32 >= 32, 1, 0)
    for o in range(27):
        oh[o] = onehot(near[:, o : o + 1] == columns)

    def offsets_of(tx, ty, tz):
        pick = (0, 1, 3)
        return [r[3] for r in readers(pick[tx], pick[ty], pick[tz])]

    def stacked(offsets):
        if len(offsets) == 1:
            return oh[offsets[0]]
        return jnp.concatenate([oh[o] for o in offsets], axis=0)

    def inner(found):
        return [r for r in found if 1 <= r[0] <= 4 and 1 <= r[1] <= 4]

    def outer(found):
        return [r for r in found if not (1 <= r[0] <= 4 and 1 <= r[1] <= 4)]

    def keep(rows, found):
        for n, (px, py, p, _) in enumerate(found):
            pz[px, py, p // 2, :, pl.ds(128 * (p % 2), 128)] = rows[32 * n : 32 * n + 32]

    for py in (0, 5):
        pz[pl.ds(1, 4), py] = jnp.zeros((4, 3, 32, 256), BF)
    for ux in range(4):
        for uy in range(4):
            for uz in range(4):
                found = inner(readers(ux, uy, uz))
                picks = stacked([r[3] for r in found])[:, :32]
                keep(nn(picks, et[ux * 16 + uy * 4 + uz, pl.ds(0, 32)]).astype(BF), found)

    mine = pl.multiple_of(64 * core, 64)
    other = pl.multiple_of(64 - 64 * core, 64)

    def core_copy(s):
        return pltpu.make_async_remote_copy(
            src_ref=wd.at[pl.ds(9 * s, 9), pl.ds(other, 64), :],
            dst_ref=rcore.at[pl.ds(9 * s, 9)],
            send_sem=csem.at[s],
            recv_sem=crem.at[s],
            device_id=sibling,
            device_id_type=MESH,
        )

    def blocks_of(d0, d1):
        return (
            d0[:128, :128] + d0[128:, 128:],
            d0[:128, 128:] + d1[128:, :128],
            d1[:128, :128] + d1[128:, 128:],
        )

    for kx in range(3):
        x0, x1 = ((1, 4), (0, 4), (0, 3))[kx]
        for ky in range(3):
            left = gt[:, pl.ds(256 * x0, 256 * (x1 - x0))]
            sums = [
                nn(
                    left,
                    pz[pl.ds(x0 + kx, x1 - x0), pl.ds(ky, 4), pl.ds(w, 2)].reshape(-1, 256),
                )
                for w in range(2)
            ]
            for n, value in enumerate(blocks_of(*sums)):
                if kx == 1 and ky == 1:
                    wd[9 * kx + 3 * ky + n] = value
                else:
                    di[9 * kx + 3 * ky + n] = value

    for ch in range(8):
        @pl.when(there[ch])
        def _():
            halo_arrived(hs, hr, hsem, hrem, ch).wait_recv()
            wx, wy = WAYS[ch]
            for chunk in range(chunks(ch)):
                ux = side(-wx) if wx != 0 else chunk
                uy = side(-wy) if wy != 0 else chunk
                got = hr[ch, chunk].astype(F32).reshape(4, 8, 128)
                none = jnp.zeros((4, 8, 128), F32)
                pair = (got, none) if ch >= 4 or ch % 2 == 0 else (none, got)
                start = 64 if ch >= 4 else 32 + 16 * (ch // 2)
                et[pl.ds(ux * 16 + uy * 4, 4), pl.ds(start, 16), :] = jnp.concatenate(
                    pair, axis=1
                ).astype(BF)

    for ux in range(4):
        for uy in range(4):
            for uz in range(4):
                found = outer(readers(ux, uy, uz))
                if found:
                    picks = stacked([r[3] for r in found])
                    keep(nn(picks[:, :80], et[ux * 16 + uy * 4 + uz]).astype(BF), found)

    def send(src, dst, ns, nr, device):
        pltpu.make_async_remote_copy(
            src_ref=src,
            dst_ref=dst,
            send_sem=asem.at[ns],
            recv_sem=arem.at[nr],
            device_id=device,
            device_id_type=MESH,
        ).start()

    def counted(ref, ns, nr):
        return pltpu.make_async_remote_copy(
            src_ref=ref,
            dst_ref=ref,
            send_sem=asem.at[ns],
            recv_sem=arem.at[nr],
            device_id=sibling,
            device_id_type=MESH,
        )

    def arrived(ref, nr):
        counted(ref, 0, nr).wait_recv()

    def sent(ref, ns):
        counted(ref, ns, 0).wait_send()

    def sixteen(first, index):
        return pl.ds(pl.multiple_of(first + 16 * index, 16), 16)

    def quarter(index):
        return pl.ds(4 * index, 4)

    def core_sum(s):
        core_copy(s).wait()
        for n, (matrix, slot, count) in enumerate(RUNS[s]):
            kept = wd[pl.ds(matrix, count), pl.ds(mine, 64), :]
            hh[n, pl.ds(slot, count)] = kept + rcore[pl.ds(matrix, count)]

    def outer_sums(kx, ky, w):
        total = None
        if ky != 1:
            rows = pz[pl.ds(kx, 4), (0, None, 5)[ky], pl.ds(w, 2)].reshape(256, 256)
            total = nn(gty[ky // 2, kx], rows)
        if kx != 1:
            x, px = ((0, 0), None, (3, 5))[kx]
            rows = pz[px, pl.ds(ky, 4), pl.ds(w, 2)].reshape(256, 256)
            term = nn(gt[:, pl.ds(256 * x, 256)], rows)
            total = term if total is None else total + term
        return total

    for s in (1, 0, 2):
        for ky in range(3):
            if s == 1 and ky == 1:
                continue
            value = blocks_of(outer_sums(s, ky, 0), outer_sums(s, ky, 1))
            for n in range(3):
                j = 9 * s + 3 * ky + n
                wd[j] = di[j] + value[n]
        core_copy(s).start()
    for s in (1, 0, 2):
        core_sum(s)

    far_first = (2, 1, 3)
    for n in range(2):
        size = (14, 13)[n]
        for d in far_first:
            rows = sixteen(0, ((cx, cy)[n] + d) % 4)
            coded, scale = encode(hh[n, pl.ds(0, size), rows, :].reshape(-1, 128))
            q1[n, d - 1, pl.ds(0, size)] = coded.reshape(size, 16, 128)
            qs[0, n, d - 1] = scale
            device = (along_x, along_y)[n][d - 1]
            send(
                q1.at[n, d - 1, pl.ds(0, size)],
                r1.at[n, d - 1, pl.ds(0, size)],
                n,
                n,
                (along_x, along_y)[n][d - 1],
            )
            send(qs.at[0, n, d - 1], rscale.at[0, n, d - 1], 2, 2, (along_x, along_y)[n][d - 1])

    def weights(j, carry):
        low, mid, high = ker[3 * j], ker[3 * j + 1], ker[3 * j + 2]
        none = jnp.zeros((128, 128), BF)
        wt[j, 0, pl.ds(0, 128), pl.ds(0, 128)] = low
        wt[j, 0, pl.ds(0, 128), pl.ds(128, 128)] = none
        wt[j, 0, pl.ds(128, 128), pl.ds(0, 128)] = mid
        wt[j, 0, pl.ds(128, 128), pl.ds(128, 128)] = low
        wt[j, 1, pl.ds(0, 128), pl.ds(0, 128)] = high
        wt[j, 1, pl.ds(0, 128), pl.ds(128, 128)] = mid
        wt[j, 1, pl.ds(128, 128), pl.ds(0, 128)] = none
        wt[j, 1, pl.ds(128, 128), pl.ds(128, 128)] = high
        return carry

    loads[5].wait()
    lax.fori_loop(0, 9, weights, 0)

    for tx in range(3):
        for ty in range(3):
            for tz in range(3):
                offs = offsets_of(tx, ty, tz)
                flipped = nt(eye[:80], stacked(offs)).astype(BF)
                oht[tx * 9 + ty * 3 + tz, :, pl.ds(0, 32 * len(offs))] = flipped

    def clear_dp(x, carry):
        dp[x] = jnp.zeros((6, 3, 32, 256), F32)
        return carry

    lax.fori_loop(0, 6, clear_dp, 0)

    for px in range(6):
        for ky in range(3):
            for w in range(2):
                term = None
                for kx in range(3):
                    if 0 <= px - kx < 4:
                        one = nt(gz[px - kx].reshape(256, 256), wt[3 * kx + ky, w])
                        term = one if term is None else term + one
                dp[px, pl.ds(ky, 4), pl.ds(w, 2)] += term.reshape(4, 2, 32, 256)

    arrived(r1.at[0], 0)
    arrived(r1.at[1, :, pl.ds(0, 13)], 1)
    arrived(rscale.at[0], 2)
    for n in range(2):
        size = (14, 13)[n]
        total = hh[n, pl.ds(0, size), sixteen(0, (cx, cy)[n]), :]
        for d in range(3):
            got = decode(r1[n, d, pl.ds(0, size)].reshape(-1, 128), rscale[0, n, d])
            total = total + got.reshape(size, 16, 128)
        s1[n, pl.ds(0, size)] = total
        s1[n, pl.ds(size, 16 - size)] = jnp.zeros((16 - size, 16, 128), F32)

    for n in range(2):
        for d in far_first:
            coded, scale = encode(s1[n, quarter(((cy, cx)[n] + d) % 4)].reshape(64, 128))
            q2[n, d - 1] = coded.reshape(4, 16, 128)
            qs[1, n, d - 1] = scale
            device = (along_y, along_x)[n][d - 1]
            send(q2.at[n, d - 1], r2.at[n, d - 1], 3, 3, device)
            send(qs.at[1, n, d - 1], rscale.at[1, n, d - 1], 4, 4, device)

    for ux in range(4):
        for uy in range(4):
            pieces = []
            for uz in range(4):
                found = readers(ux, uy, uz)
                high, low = [], []
                for px, py, p, _ in found:
                    value = dp[px, py, p // 2, :, pl.ds(128 * (p % 2), 128)]
                    top = value.astype(BF)
                    high.append(top)
                    low.append((value - top.astype(F32)).astype(BF))
                high = jnp.concatenate(high, axis=0) if len(high) > 1 else high[0]
                low = jnp.concatenate(low, axis=0) if len(low) > 1 else low[0]
                group = kind(ux) * 9 + kind(uy) * 3 + kind(uz)
                res = nn(
                    oht[group, :, pl.ds(0, 32 * len(found))],
                    jnp.concatenate([high, low], axis=1),
                )
                res = res[:, :128] + res[:, 128:]
                de[ux * 16 + uy * 4 + uz] = res[:32]
                pieces.append(res)

            def give(slot, chunk, row):
                rs[slot, chunk] = jnp.concatenate(
                    [piece[row : row + 8] for piece in pieces], axis=0
                ).astype(BF)

            for slot in range(8):
                wx, wy = WAYS[slot]
                if (wx != 0 and ux != side(-wx)) or (wy != 0 and uy != side(-wy)):
                    continue
                chunk = 0 if slot >= 4 else (uy if wx != 0 else ux)
                give(slot, chunk, 64 if slot >= 4 else 32 + 8 * slot)

    for ch in range(8):
        @pl.when(there[ch])
        def _():
            halo_copy(hs, hr, hsem, hrem, ch).wait_send()
            halo_copy(rs, rr, hsem, brem, ch).start()

        @pl.when(jnp.logical_not(there[ch]))
        def _():
            rr[ch] = jnp.zeros((4, 32, 128), BF)

    def convolve(x):
        total = jnp.zeros((256, 256), F32)
        for kx in range(3):
            for ky in range(3):
                for w in range(2):
                    rows = pz[x + kx, pl.ds(ky, 4), pl.ds(w, 2)].reshape(256, 256)
                    total = total + nn(rows, wt[3 * kx + ky, w])
        alive = jnp.concatenate([live[...], live[...]], axis=1)
        co[x] = (total.reshape(4, 2, 32, 256) * alive).astype(BF)
    convolve(0)
    convolve(1)

    arrived(r2, 3)
    arrived(rscale.at[1], 4)
    for n in range(2):
        total = s1[n, quarter((cy, cx)[n])].reshape(64, 128)
        for d in range(3):
            total = total + decode(r2[n, d].reshape(64, 128), rscale[1, n, d])
        s2[n] = total

    coded, scale = encode(s2[...].reshape(128, 128))
    q3[...] = coded
    qs3[...] = scale
    r3[pl.ds(cz, 1)] = coded[None]
    rscale3[pl.ds(cz, 1)] = scale[None]
    for d in (4, 3, 5, 2, 6, 1, 7):
        send(q3, r3.at[cz], 5, 5, along_z[d - 1])
        send(qs3, rscale3.at[cz], 6, 6, along_z[d - 1])

    convolve(2)
    convolve(3)
    for x in range(4):
        for hb in range(2):
            parts = [
                co[x, :, :, pl.ds(16 * hb, 16), pl.ds(128 * n, 128)].reshape(128, 128)
                for n in range(2)
            ]
            rows = nn(part_perm[...], jnp.concatenate(parts, axis=0)).reshape(16, 16, 128)
            conv[pl.ds(16 * hb, 16), pl.ds(16 * x, 16), :] = rows.astype(BF)

    for ch in range(8):
        @pl.when(there[ch])
        def _():
            halo_arrived(rs, rr, hsem, brem, ch).wait_recv()

    for ux in range(4):
        parts = []
        for uy in range(4):
            rows = de[pl.ds(ux * 16 + uy * 4, 4)].reshape(128, 128)
            for ch in range(8):
                wx, wy = WAYS[ch]
                if (wx != 0 and ux != side(wx)) or (wy != 0 and uy != side(wy)):
                    continue
                chunk = 0 if ch >= 4 else (uy if wx != 0 else ux)
                rows = rows + nn(bdt[ch], rr[ch, chunk])
            parts.append(rows.astype(BF).reshape(4, 32, 128))
        parts = jnp.concatenate(parts, axis=0)
        for hb in range(2):
            swapped = swap16(parts[:, 16 * hb : 16 * hb + 16])
            igrad[pl.ds(16 * hb, 16), pl.ds(16 * ux, 16), :] = swapped.astype(BF)

    arrived(r3.at[pl.ds(0, 7)], 5)
    arrived(rscale3.at[pl.ds(0, 7)], 6)
    whole = decode(r3[0], rscale3[0])
    for z in range(1, 8):
        whole = whole + decode(r3[z], rscale3[z])
    whole = (whole * (1.0 / math.sqrt(256 * 32 * 64))).reshape(2, 4, 16, 128).astype(BF)
    g2[0, quarter(cy)] = whole[0]
    g2[1, quarter(cx)] = whole[1]

    def across(n, away):
        index = ((cy, cx)[n] + 4 - away) % 4
        rows = sixteen(64 * core, (cx, cy)[n])

        def go(slots):
            for d in far_first:
                send(
                    g2.at[n, slots],
                    kg.at[n, slots, rows, :],
                    9 + n,
                    11 + 2 * d + n,
                    (along_x, along_y)[n][d - 1],
                )

        @pl.when(index < 3)
        def _():
            go(quarter(index))

        @pl.when(index == 3)
        def _():
            go(pl.ds(12, (2, 1)[n]))

    for d in far_first:
        for n in range(2):
            piece = g2.at[n, quarter((cy, cx)[n])]
            send(piece, piece, 7 + n, 5 + 2 * d + n, (along_y, along_x)[n][d - 1])
    for n in range(2):
        across(n, 0)
    for d in (1, 3, 2):
        for n in range(2):
            arrived(g2.at[n, quarter(((cy, cx)[n] + 4 - d) % 4)], 5 + 2 * d + n)
            across(n, d)

    own = []
    slots = (pl.ds(0, 14), pl.ds(0, 13))
    for n in range(2):
        rows = kg.at[n, slots[n], sixteen(64 * core, (cx, cy)[n]), :]
        own.append(pltpu.make_async_copy(g2.at[n, slots[n]], rows, osem.at[n]))
        own[n].start()
        send(g2.at[n, slots[n]], rows, 11 + n, 19 + n, sibling)
    for d in (1, 3, 2):
        for n in range(2):
            rows = kg.at[n, slots[n], sixteen(64 * core, ((cx, cy)[n] + 4 - d) % 4), :]
            arrived(rows, 11 + 2 * d + n)
            send(rows, rows, 11 + n, 19 + n, sibling)

    sent(q1.at[0], 0)
    sent(q1.at[1, :, pl.ds(0, 13)], 1)
    sent(qs.at[0], 2)
    sent(q2, 3)
    sent(qs.at[1], 4)
    sent(r3.at[pl.ds(0, 7)], 5)
    sent(rscale3.at[pl.ds(0, 7)], 6)
    for ch in range(8):
        @pl.when(there[ch])
        def _():
            halo_copy(rs, rr, hsem, brem, ch).wait_send()
    for copy in own:
        copy.wait()
    for n in range(2):
        sent(g2.at[n, pl.ds(0, 12)], 7 + n)
        sent(kg.at[n, slots[n], pl.ds(0, 48), :], 9 + n)
        sent(kg.at[n, slots[n], pl.ds(0, 64), :], 11 + n)
        arrived(kg.at[n, slots[n], pl.ds(other, 64), :], 19 + n)


def finish(conv, igrad, kg, conv_out, igrad_out, kgrad_out, wide, sem):
    stores = []

    def store(src, dst):
        stores.append(pltpu.make_async_copy(src, dst, sem.at[len(stores)]))
        stores[-1].start()

    for s in range(3):
        for n, (matrix, slot, count) in enumerate(RUNS[s]):
            for m in range(count):
                wide[matrix + m] = kg[n, slot + m].T.astype(F32)
        part = pl.ds(9 * s, 9)
        store(wide.at[part], kgrad_out.at[part])
        if s == 0:
            store(conv, conv_out)
            store(igrad, igrad_out)
    for copy in stores:
        copy.wait()


def per_device(features, cotangent, kernel, block_count, neighbours, send_face, send_corner):
    vmem = pl.BlockSpec(memory_space=pltpu.VMEM)
    hbm = pl.BlockSpec(memory_space=pltpu.HBM)
    dma = pltpu.SemaphoreType.DMA
    blocks = (32, 64, 128)
    conv, igrad, kg = pl.pallas_call(
        body,
        out_shape=(
            pltpu.VMEM(blocks, BF),
            pltpu.VMEM(blocks, BF),
            pltpu.VMEM((2, 16, 128, 128), BF),
        ),
        in_specs=[hbm] * 6,
        out_specs=(vmem,) * 3,
        scratch_shapes=[
            pltpu.SMEM((1, 4, 8), jnp.int32),
            pltpu.SMEM((1, 2, 4), jnp.int32),
            pltpu.VMEM(blocks, BF),
            pltpu.VMEM(blocks, BF),
            pltpu.VMEM((27, 128, 128), BF),
            pltpu.VMEM((32, 27), jnp.int32),
            pltpu.VMEM((32, 128), F32),
            pltpu.VMEM((64, 80, 128), BF),
            pltpu.VMEM((6, 6, 3, 32, 256), BF),
            pltpu.VMEM((4, 4, 2, 32, 256), BF),
            pltpu.VMEM((256, 1024), BF),
            pltpu.VMEM((2, 3, 256, 256), BF),
            pltpu.VMEM((9, 2, 256, 256), BF),
            pltpu.VMEM((27, 128, 128), F32),
            pltpu.VMEM((6, 6, 3, 32, 256), F32),
            pltpu.VMEM((64, 32, 128), F32),
            pltpu.VMEM((27, 32, 128), BF),
            pltpu.VMEM((27, 80, 256), BF),
            pltpu.VMEM((8, 32, 128), BF),
            pltpu.VMEM((8, 128, 32), BF),
            pltpu.VMEM((4, 4, 2, 32, 256), BF),
            pltpu.VMEM((256, 256), BF),
            pltpu.VMEM((256, 256), BF),
            pltpu.VMEM((256, 256), BF),
            pltpu.VMEM((8, 4, 32, 128), BF),
            pltpu.VMEM((8, 4, 32, 128), BF),
            pltpu.VMEM((8, 4, 32, 128), BF),
            pltpu.VMEM((8, 4, 32, 128), BF),
            pltpu.VMEM((27, 128, 128), F32),
            pltpu.VMEM((27, 64, 128), F32),
            pltpu.VMEM((2, 14, 64, 128), F32),
            pltpu.VMEM((2, 3, 14, 16, 128), jnp.int16),
            pltpu.VMEM((2, 3, 14, 16, 128), jnp.int16),
            pltpu.VMEM((2, 16, 16, 128), F32),
            pltpu.VMEM((2, 3, 4, 16, 128), jnp.int16),
            pltpu.VMEM((2, 3, 4, 16, 128), jnp.int16),
            pltpu.VMEM((2, 2, 3, 8, 128), F32),
            pltpu.VMEM((2, 2, 3, 8, 128), F32),
            pltpu.VMEM((2, 64, 128), F32),
            pltpu.VMEM((128, 128), jnp.int16),
            pltpu.VMEM((8, 128), F32),
            pltpu.VMEM((8, 128, 128), jnp.int16),
            pltpu.VMEM((8, 8, 128), F32),
            pltpu.VMEM((2, 16, 16, 128), BF),
            dma((6,)), dma((2,)), dma((8,)), dma((8,)), dma((8,)),
            dma((3,)), dma((3,)), dma((13,)), dma((21,)),
        ],
        compiler_params=pltpu.CompilerParams(
            collective_id=0, has_side_effects=True, vmem_limit_bytes=52 * 1024 * 1024
        ),
        cost_estimate=pl.CostEstimate(
            flops=7_000_000_000, bytes_accessed=6_000_000, transcendentals=0
        ),
    )(
        send_face,
        jnp.swapaxes(send_corner, 1, 2),
        features.reshape(blocks),
        cotangent.reshape(blocks),
        kernel,
        neighbours,
    )
    conv, igrad, kgrad = pl.pallas_call(
        finish,
        out_shape=(
            jax.ShapeDtypeStruct(blocks, BF),
            jax.ShapeDtypeStruct(blocks, BF),
            jax.ShapeDtypeStruct((27, 128, 128), F32),
        ),
        in_specs=[vmem] * 3,
        out_specs=(hbm, hbm, hbm),
        scratch_shapes=[
            pltpu.VMEM((27, 128, 128), F32),
            dma((5,)),
        ],
        compiler_params=pltpu.CompilerParams(vmem_limit_bytes=32 * 1024 * 1024),
    )(conv, igrad, kg)
    return conv.reshape(2048, 128), igrad.reshape(2048, 128), kgrad


def solution(mesh):
    in_specs = (
        P(("gx", "gy"), None),
        P(("gx", "gy"), None),
        P(),
        P(("gx", "gy")),
        P(("gx", "gy"), None),
        P(("gx", "gy"), None, None),
        P(("gx", "gy"), None, None),
    )
    out_specs = (P(("gx", "gy"), None), P(("gx", "gy"), None), P())
    return jax.shard_map(
        per_device, mesh=mesh, in_specs=in_specs, out_specs=out_specs, check_vma=False
    )
```

```python
import math

import jax
import jax.numpy as jnp
from jax import lax
from jax.experimental import pallas as pl
from jax.experimental.pallas import tpu as pltpu
from jax.sharding import PartitionSpec as P

MESH = pl.DeviceIdType.MESH
BF = jnp.bfloat16
F32 = jnp.float32

NX, NY, NZ = 4, 4, 8
FACE_WAYS = ((-1, 0), (1, 0), (0, -1), (0, 1))
CORNER_WAYS = ((-1, -1), (-1, 1), (1, -1), (1, 1))
WAYS = FACE_WAYS + CORNER_WAYS


RUNS = (
    ((0, 0, 5), (5, 0, 4)),
    ((9, 5, 4), (13, 4, 5)),
    ((18, 9, 5), (23, 9, 4)),
)


def opposite(channel):
    return channel ^ 1 if channel < 4 else 11 - channel


def side(stride):
    return 0 if stride < 0 else 3


def places(local):
    if local == 0:
        return ((1, 0), (5, 1))
    if local == 3:
        return ((4, 0), (0, -1))
    return ((local + 1, 0),)


def kind(local):
    return 0 if local == 0 else (2 if local == 3 else 1)


def readers(ux, uy, uz):
    found = []
    for px, ox in places(ux):
        for py, oy in places(uy):
            for pz, oz in places(uz):
                found.append((px, py, pz, (ox + 1) * 9 + (oy + 1) * 3 + oz + 1))
    return found


def nn(a, b):
    return lax.dot_general(a, b, (((1,), (0,)), ((), ())), preferred_element_type=F32)


def nt(a, b):
    return lax.dot_general(a, b, (((1,), (1,)), ((), ())), preferred_element_type=F32)


def onehot(mask):
    return jnp.where(mask, 1.0, 0.0).astype(BF)


def iota(shape, dim):
    return lax.broadcasted_iota(jnp.int32, shape, dim)


def encode(rows):
    largest = jnp.max(jnp.abs(rows.reshape(-1, 8, 128)), axis=0)
    for step in (4, 2, 1):
        largest = jnp.maximum(largest, pltpu.roll(largest, step, 0))
    largest = jnp.maximum(largest, 1e-33)
    scale = largest * (1.0 / 32000.0)
    inverse = 32000.0 / largest
    coded = jnp.round(rows.reshape(-1, 8, 128) * inverse[None]).reshape(-1, 128)
    return coded.astype(jnp.int32).astype(jnp.int16), scale


def decode(coded, scale):
    rows = coded.astype(jnp.int32).astype(F32).reshape(-1, 8, 128)
    return (rows * scale[None]).reshape(-1, 128)


def body(
    face_in, corner_in, feat_in, cot_in, ker_in, near_in,
    conv, igrad, kg,
    face, corner, feat, cot, ker, near, live,
    et, pz, gz, gt, gty, wt, di, dp, de, oh, oht, bd, bdt, co, perm, pair_perm, part_perm,
    hs, hr, rs, rr,
    wd, rcore, hh, q1, r1, s1, q2, r2, qs, rscale, s2, q3, qs3, r3, rscale3, g2,
    isem, osem, hsem, hrem, brem, csem, crem, asem, arem,
):
    loads = [
        pltpu.make_async_copy(src, dst, isem.at[n])
        for n, (src, dst) in enumerate(
            (
                (face_in, face),
                (corner_in, corner),
                (feat_in, feat),
                (near_in, near),
                (cot_in, cot),
                (ker_in, ker),
            )
        )
    ]
    for copy in loads:
        copy.start()
    gx = lax.axis_index("gx")
    gy = lax.axis_index("gy")
    cy = gx // 16
    cz = (gx // 2) % 8
    cx = (gy // 2) * 2 + gx % 2
    core = gy % 2

    def at(x, y, z, c):
        return ((y * 8 + z) * 2 + x % 2, (x // 2) * 2 + c)

    sibling = (gx, gy // 2 * 2 + (1 - core))
    along_x = [at((cx + d) % NX, cy, cz, core) for d in range(1, NX)]
    along_y = [at(cx, (cy + d) % NY, cz, core) for d in range(1, NY)]
    along_z = [at(cx, cy, (cz + d) % NZ, core) for d in range(1, NZ)]
    halo = [(gx + wx, gy + wy) for wx, wy in WAYS]
    there = [
        (gx + wx >= 0) & (gx + wx < 64) & (gy + wy >= 0) & (gy + wy < 4) for wx, wy in WAYS
    ]

    barrier = pltpu.get_barrier_semaphore()
    greet = [along_z[n] for n in (3, 2, 4, 1, 5, 0, 6)] + along_x + along_y + [sibling]
    expected = len(greet)
    for other in greet:
        pl.semaphore_signal(barrier, inc=1, device_id=other, device_id_type=MESH)
    for ch in (4, 5, 6, 7, 0, 1, 2, 3):
        expected = expected + there[ch].astype(jnp.int32)

        @pl.when(there[ch])
        def _():
            pl.semaphore_signal(barrier, inc=1, device_id=halo[ch], device_id_type=MESH)

    r256, c256 = iota((256, 256), 0), iota((256, 256), 1)
    perm[...] = onehot(((r256 >> 4) == (c256 & 15)) & ((r256 & 15) == (c256 >> 4)))
    pair_perm[...] = onehot(c256 == (r256 & 15) * 16 + ((r256 >> 4) & 7) * 2 + (r256 >> 7))
    part_perm[...] = onehot(c256 == (r256 & 1) * 128 + ((r256 & 15) >> 1) * 16 + (r256 >> 4))
    eye = onehot(iota((128, 128), 0) == iota((128, 128), 1))
    eye256 = onehot(r256 == c256)

    def swap16(v):
        return nn(perm[...], v.reshape(256, 128)).reshape(16, 16, 128)

    r32, c32 = iota((32, 128), 0), iota((32, 128), 1)
    same_z = (r32 >> 3) == (c32 >> 5)
    loads[0].wait()
    loads[1].wait()
    for ch in range(8):
        index = jnp.full((32, 128), -1, jnp.int32)
        for n in range(8 if ch < 4 else 2):
            slot = n if ch < 4 else 2 * (opposite(ch) - 4) + n
            block = face[0, ch, n] if ch < 4 else corner[0, n, ch - 4]
            index = jnp.where((r32 & 7) == slot, block, index)
        pick = onehot(same_z & (index == (c32 & 31)))
        bd[ch] = pick
        bdt[ch] = nt(eye, pick).astype(BF)

    loads[2].wait()
    for hb in range(2):
        for ug in range(4):
            rows = swap16(feat[pl.ds(16 * hb, 16), pl.ds(16 * ug, 16), :])
            et[pl.ds(16 * ug, 16), pl.ds(16 * hb, 16), :] = rows.astype(BF)

    def rim_base(ch, chunk):
        wx, wy = WAYS[ch]
        ux = side(wx) if wx != 0 else chunk
        uy = side(wy) if wy != 0 else chunk
        return ux * 16 + uy * 4

    def chunks(ch):
        return 4 if ch < 4 else 1

    for ch in range(8):
        for chunk in range(chunks(ch)):
            source = et[pl.ds(rim_base(ch, chunk), 4), pl.ds(0, 32), :].reshape(128, 128)
            hs[ch, chunk] = nn(bd[ch], source).astype(BF)

    pl.semaphore_wait(barrier, expected)

    def part(buf, ch):
        return buf.at[ch] if ch < 4 else buf.at[ch, pl.ds(0, 1)]

    def halo_copy(src, dst, ss, rs_, ch):
        return pltpu.make_async_remote_copy(
            src_ref=part(src, ch),
            dst_ref=part(dst, opposite(ch)),
            send_sem=ss.at[ch],
            recv_sem=rs_.at[opposite(ch)],
            device_id=halo[ch],
            device_id_type=MESH,
        )

    def halo_arrived(src, dst, ss, rs_, ch):
        return pltpu.make_async_remote_copy(
            src_ref=part(src, ch),
            dst_ref=part(dst, ch),
            send_sem=ss.at[ch],
            recv_sem=rs_.at[ch],
            device_id=halo[ch],
            device_id_type=MESH,
        )

    for ch in (2, 3, 4, 5, 6, 7, 0, 1):
        @pl.when(there[ch])
        def _():
            halo_copy(hs, hr, hsem, hrem, ch).start()

    loads[3].wait()
    live[...] = jnp.where(near[:, 13:14] == r32, 1.0, 0.0)
    lives = [live[pl.ds(16 * hb, 16), :] for hb in range(2)]
    loads[4].wait()
    for x in range(4):
        for hb in range(2):
            rows = cot[pl.ds(16 * hb, 16), pl.ds(16 * x, 16), :].reshape(256, 128)
            rows = nn(pair_perm[...], rows).reshape(2, 4, 2, 16, 128) * lives[hb]
            for n in range(2):
                gz[x, :, :, pl.ds(16 * hb, 16), pl.ds(128 * n, 128)] = rows[n].astype(BF)
    for x in range(4):
        turned = nt(eye256, gz[x].reshape(256, 256))
        place = pl.ds(256 * x, 256)
        gt[:, place] = turned.astype(BF)
    for n, y in enumerate((0, 3)):
        turned = nt(eye256, gz[:, y].reshape(256, 256))
        gty[n, 0] = jnp.where(c256 < 64, 0.0, turned).astype(BF)
        gty[n, 1] = turned.astype(BF)
        gty[n, 2] = jnp.where(c256 < 192, turned, 0.0).astype(BF)

    for u in range(64):
        et[u, pl.ds(32, 48), :] = jnp.zeros((48, 128), BF)

    columns = c32 + jnp.where(c32 >= 32, 1, 0)
    for o in range(27):
        oh[o] = onehot(near[:, o : o + 1] == columns)

    def offsets_of(tx, ty, tz):
        pick = (0, 1, 3)
        return [r[3] for r in readers(pick[tx], pick[ty], pick[tz])]

    def stacked(offsets):
        if len(offsets) == 1:
            return oh[offsets[0]]
        return jnp.concatenate([oh[o] for o in offsets], axis=0)

    def inner(found):
        return [r for r in found if 1 <= r[0] <= 4 and 1 <= r[1] <= 4]

    def outer_y(found):
        return [r for r in found if 1 <= r[0] <= 4 and not 1 <= r[1] <= 4]

    def outer_x(found):
        return [r for r in found if not 1 <= r[0] <= 4]

    def gather(which):
        for ux in range(4):
            for uy in range(4):
                for uz in range(4):
                    found = which(readers(ux, uy, uz))
                    if found:
                        picks = stacked([r[3] for r in found])[:, :80]
                        keep(nn(picks, et[ux * 16 + uy * 4 + uz]).astype(BF), found)

    def keep(rows, found):
        for n, (px, py, p, _) in enumerate(found):
            pz[px, py, p // 2, :, pl.ds(128 * (p % 2), 128)] = rows[32 * n : 32 * n + 32]

    for py in (0, 5):
        pz[pl.ds(1, 4), py] = jnp.zeros((4, 3, 32, 256), BF)
    for ux in range(4):
        for uy in range(4):
            for uz in range(4):
                found = inner(readers(ux, uy, uz))
                picks = stacked([r[3] for r in found])[:, :32]
                keep(nn(picks, et[ux * 16 + uy * 4 + uz, pl.ds(0, 32)]).astype(BF), found)

    mine = pl.multiple_of(64 * core, 64)
    other = pl.multiple_of(64 - 64 * core, 64)

    def core_copy(s):
        return pltpu.make_async_remote_copy(
            src_ref=wd.at[pl.ds(9 * s, 9), pl.ds(other, 64), :],
            dst_ref=rcore.at[pl.ds(9 * s, 9)],
            send_sem=csem.at[s],
            recv_sem=crem.at[s],
            device_id=sibling,
            device_id_type=MESH,
        )

    def blocks_of(d0, d1):
        return (
            d0[:128, :128] + d0[128:, 128:],
            d0[:128, 128:] + d1[128:, :128],
            d1[:128, :128] + d1[128:, 128:],
        )

    for kx in range(3):
        x0, x1 = ((1, 4), (0, 4), (0, 3))[kx]
        for ky in range(3):
            left = gt[:, pl.ds(256 * x0, 256 * (x1 - x0))]
            sums = [
                nn(
                    left,
                    pz[pl.ds(x0 + kx, x1 - x0), pl.ds(ky, 4), pl.ds(w, 2)].reshape(-1, 256),
                )
                for w in range(2)
            ]
            for n, value in enumerate(blocks_of(*sums)):
                if kx == 1 and ky == 1:
                    wd[9 * kx + 3 * ky + n] = value
                else:
                    di[9 * kx + 3 * ky + n] = value

    def unpack(ch):
        @pl.when(there[ch])
        def _():
            halo_arrived(hs, hr, hsem, hrem, ch).wait_recv()
            wx, wy = WAYS[ch]
            for chunk in range(chunks(ch)):
                ux = side(-wx) if wx != 0 else chunk
                uy = side(-wy) if wy != 0 else chunk
                got = hr[ch, chunk].astype(F32).reshape(4, 8, 128)
                none = jnp.zeros((4, 8, 128), F32)
                pair = (got, none) if ch >= 4 or ch % 2 == 0 else (none, got)
                start = 64 if ch >= 4 else 32 + 16 * (ch // 2)
                et[pl.ds(ux * 16 + uy * 4, 4), pl.ds(start, 16), :] = jnp.concatenate(
                    pair, axis=1
                ).astype(BF)

    def send(src, dst, ns, nr, device):
        pltpu.make_async_remote_copy(
            src_ref=src,
            dst_ref=dst,
            send_sem=asem.at[ns],
            recv_sem=arem.at[nr],
            device_id=device,
            device_id_type=MESH,
        ).start()

    def counted(ref, ns, nr):
        return pltpu.make_async_remote_copy(
            src_ref=ref,
            dst_ref=ref,
            send_sem=asem.at[ns],
            recv_sem=arem.at[nr],
            device_id=sibling,
            device_id_type=MESH,
        )

    def arrived(ref, nr):
        counted(ref, 0, nr).wait_recv()

    def sent(ref, ns):
        counted(ref, ns, 0).wait_send()

    def sixteen(first, index):
        return pl.ds(pl.multiple_of(first + 16 * index, 16), 16)

    def quarter(index):
        return pl.ds(4 * index, 4)

    def core_sum(s):
        core_copy(s).wait()
        for n, (matrix, slot, count) in enumerate(RUNS[s]):
            kept = wd[pl.ds(matrix, count), pl.ds(mine, 64), :]
            hh[n, pl.ds(slot, count)] = kept + rcore[pl.ds(matrix, count)]

    def outer_sums(kx, ky, w):
        total = None
        if ky != 1:
            rows = pz[pl.ds(kx, 4), (0, None, 5)[ky], pl.ds(w, 2)].reshape(256, 256)
            total = nn(gty[ky // 2, kx], rows)
        if kx != 1:
            x, px = ((0, 0), None, (3, 5))[kx]
            rows = pz[px, pl.ds(ky, 4), pl.ds(w, 2)].reshape(256, 256)
            term = nn(gt[:, pl.ds(256 * x, 256)], rows)
            total = term if total is None else total + term
        return total

    def outer_wgrad(s):
        for ky in range(3):
            if s == 1 and ky == 1:
                continue
            value = blocks_of(outer_sums(s, ky, 0), outer_sums(s, ky, 1))
            for n in range(3):
                j = 9 * s + 3 * ky + n
                wd[j] = di[j] + value[n]
        core_copy(s).start()

    for ch in (2, 3):
        unpack(ch)
    gather(outer_y)
    outer_wgrad(1)
    for ch in (4, 5, 6, 7, 0, 1):
        unpack(ch)
    gather(outer_x)
    outer_wgrad(0)
    outer_wgrad(2)
    for s in (1, 0, 2):
        core_sum(s)

    far_first = (2, 1, 3)
    for n in range(2):
        size = (14, 13)[n]
        for d in far_first:
            rows = sixteen(0, ((cx, cy)[n] + d) % 4)
            coded, scale = encode(hh[n, pl.ds(0, size), rows, :].reshape(-1, 128))
            q1[n, d - 1, pl.ds(0, size)] = coded.reshape(size, 16, 128)
            qs[0, n, d - 1] = scale
            device = (along_x, along_y)[n][d - 1]
            send(
                q1.at[n, d - 1, pl.ds(0, size)],
                r1.at[n, d - 1, pl.ds(0, size)],
                n,
                n,
                (along_x, along_y)[n][d - 1],
            )
            send(qs.at[0, n, d - 1], rscale.at[0, n, d - 1], 2, 2, (along_x, along_y)[n][d - 1])

    def weights(j, carry):
        low, mid, high = ker[3 * j], ker[3 * j + 1], ker[3 * j + 2]
        none = jnp.zeros((128, 128), BF)
        wt[j, 0, pl.ds(0, 128), pl.ds(0, 128)] = low
        wt[j, 0, pl.ds(0, 128), pl.ds(128, 128)] = none
        wt[j, 0, pl.ds(128, 128), pl.ds(0, 128)] = mid
        wt[j, 0, pl.ds(128, 128), pl.ds(128, 128)] = low
        wt[j, 1, pl.ds(0, 128), pl.ds(0, 128)] = high
        wt[j, 1, pl.ds(0, 128), pl.ds(128, 128)] = mid
        wt[j, 1, pl.ds(128, 128), pl.ds(0, 128)] = none
        wt[j, 1, pl.ds(128, 128), pl.ds(128, 128)] = high
        return carry

    loads[5].wait()
    lax.fori_loop(0, 9, weights, 0)

    for tx in range(3):
        for ty in range(3):
            for tz in range(3):
                offs = offsets_of(tx, ty, tz)
                flipped = nt(eye[:80], stacked(offs)).astype(BF)
                oht[tx * 9 + ty * 3 + tz, :, pl.ds(0, 32 * len(offs))] = flipped

    def clear_dp(x, carry):
        dp[x] = jnp.zeros((6, 3, 32, 256), F32)
        return carry

    lax.fori_loop(0, 6, clear_dp, 0)

    for px in range(6):
        for ky in range(3):
            for w in range(2):
                term = None
                for kx in range(3):
                    if 0 <= px - kx < 4:
                        one = nt(gz[px - kx].reshape(256, 256), wt[3 * kx + ky, w])
                        term = one if term is None else term + one
                dp[px, pl.ds(ky, 4), pl.ds(w, 2)] += term.reshape(4, 2, 32, 256)

    arrived(r1.at[0], 0)
    arrived(r1.at[1, :, pl.ds(0, 13)], 1)
    arrived(rscale.at[0], 2)
    for n in range(2):
        size = (14, 13)[n]
        total = hh[n, pl.ds(0, size), sixteen(0, (cx, cy)[n]), :]
        for d in range(3):
            got = decode(r1[n, d, pl.ds(0, size)].reshape(-1, 128), rscale[0, n, d])
            total = total + got.reshape(size, 16, 128)
        s1[n, pl.ds(0, size)] = total
        s1[n, pl.ds(size, 16 - size)] = jnp.zeros((16 - size, 16, 128), F32)

    for n in range(2):
        for d in far_first:
            coded, scale = encode(s1[n, quarter(((cy, cx)[n] + d) % 4)].reshape(64, 128))
            q2[n, d - 1] = coded.reshape(4, 16, 128)
            qs[1, n, d - 1] = scale
            device = (along_y, along_x)[n][d - 1]
            send(q2.at[n, d - 1], r2.at[n, d - 1], 3, 3, device)
            send(qs.at[1, n, d - 1], rscale.at[1, n, d - 1], 4, 4, device)

    for ux in range(4):
        for uy in range(4):
            pieces = []
            for uz in range(4):
                found = readers(ux, uy, uz)
                high, low = [], []
                for px, py, p, _ in found:
                    value = dp[px, py, p // 2, :, pl.ds(128 * (p % 2), 128)]
                    top = value.astype(BF)
                    high.append(top)
                    low.append((value - top.astype(F32)).astype(BF))
                high = jnp.concatenate(high, axis=0) if len(high) > 1 else high[0]
                low = jnp.concatenate(low, axis=0) if len(low) > 1 else low[0]
                group = kind(ux) * 9 + kind(uy) * 3 + kind(uz)
                res = nn(
                    oht[group, :, pl.ds(0, 32 * len(found))],
                    jnp.concatenate([high, low], axis=1),
                )
                res = res[:, :128] + res[:, 128:]
                de[ux * 16 + uy * 4 + uz] = res[:32]
                pieces.append(res)

            def give(slot, chunk, row):
                rs[slot, chunk] = jnp.concatenate(
                    [piece[row : row + 8] for piece in pieces], axis=0
                ).astype(BF)

            for slot in range(8):
                wx, wy = WAYS[slot]
                if (wx != 0 and ux != side(-wx)) or (wy != 0 and uy != side(-wy)):
                    continue
                chunk = 0 if slot >= 4 else (uy if wx != 0 else ux)
                give(slot, chunk, 64 if slot >= 4 else 32 + 8 * slot)

    for ch in range(8):
        @pl.when(there[ch])
        def _():
            halo_copy(hs, hr, hsem, hrem, ch).wait_send()
            halo_copy(rs, rr, hsem, brem, ch).start()

        @pl.when(jnp.logical_not(there[ch]))
        def _():
            rr[ch] = jnp.zeros((4, 32, 128), BF)

    def convolve(x):
        total = jnp.zeros((256, 256), F32)
        for kx in range(3):
            for ky in range(3):
                for w in range(2):
                    rows = pz[x + kx, pl.ds(ky, 4), pl.ds(w, 2)].reshape(256, 256)
                    total = total + nn(rows, wt[3 * kx + ky, w])
        alive = jnp.concatenate([live[...], live[...]], axis=1)
        co[x] = (total.reshape(4, 2, 32, 256) * alive).astype(BF)
    convolve(0)
    convolve(1)

    arrived(r2, 3)
    arrived(rscale.at[1], 4)
    for n in range(2):
        total = s1[n, quarter((cy, cx)[n])].reshape(64, 128)
        for d in range(3):
            total = total + decode(r2[n, d].reshape(64, 128), rscale[1, n, d])
        s2[n] = total

    coded, scale = encode(s2[...].reshape(128, 128))
    q3[...] = coded
    qs3[...] = scale
    r3[pl.ds(cz, 1)] = coded[None]
    rscale3[pl.ds(cz, 1)] = scale[None]
    for d in (4, 3, 5, 2, 6, 1, 7):
        send(q3, r3.at[cz], 5, 5, along_z[d - 1])
        send(qs3, rscale3.at[cz], 6, 6, along_z[d - 1])

    convolve(2)
    convolve(3)
    for x in range(4):
        for hb in range(2):
            parts = [
                co[x, :, :, pl.ds(16 * hb, 16), pl.ds(128 * n, 128)].reshape(128, 128)
                for n in range(2)
            ]
            rows = nn(part_perm[...], jnp.concatenate(parts, axis=0)).reshape(16, 16, 128)
            conv[pl.ds(16 * hb, 16), pl.ds(16 * x, 16), :] = rows.astype(BF)

    for ch in range(8):
        @pl.when(there[ch])
        def _():
            halo_arrived(rs, rr, hsem, brem, ch).wait_recv()

    for ux in range(4):
        parts = []
        for uy in range(4):
            rows = de[pl.ds(ux * 16 + uy * 4, 4)].reshape(128, 128)
            for ch in range(8):
                wx, wy = WAYS[ch]
                if (wx != 0 and ux != side(wx)) or (wy != 0 and uy != side(wy)):
                    continue
                chunk = 0 if ch >= 4 else (uy if wx != 0 else ux)
                rows = rows + nn(bdt[ch], rr[ch, chunk])
            parts.append(rows.astype(BF).reshape(4, 32, 128))
        parts = jnp.concatenate(parts, axis=0)
        for hb in range(2):
            swapped = swap16(parts[:, 16 * hb : 16 * hb + 16])
            igrad[pl.ds(16 * hb, 16), pl.ds(16 * ux, 16), :] = swapped.astype(BF)

    arrived(r3.at[pl.ds(0, 7)], 5)
    arrived(rscale3.at[pl.ds(0, 7)], 6)
    whole = decode(r3[0], rscale3[0])
    for z in range(1, 8):
        whole = whole + decode(r3[z], rscale3[z])
    whole = (whole * (1.0 / math.sqrt(256 * 32 * 64))).reshape(2, 4, 16, 128).astype(BF)
    g2[0, quarter(cy)] = whole[0]
    g2[1, quarter(cx)] = whole[1]

    def across(n, away):
        index = ((cy, cx)[n] + 4 - away) % 4
        rows = sixteen(64 * core, (cx, cy)[n])

        def go(slots):
            for d in far_first:
                send(
                    g2.at[n, slots],
                    kg.at[n, slots, rows, :],
                    9 + n,
                    11 + 2 * d + n,
                    (along_x, along_y)[n][d - 1],
                )

        @pl.when(index < 3)
        def _():
            go(quarter(index))

        @pl.when(index == 3)
        def _():
            go(pl.ds(12, (2, 1)[n]))

    for d in far_first:
        for n in range(2):
            piece = g2.at[n, quarter((cy, cx)[n])]
            send(piece, piece, 7 + n, 5 + 2 * d + n, (along_y, along_x)[n][d - 1])
    for n in range(2):
        across(n, 0)
    for d in (1, 3, 2):
        for n in range(2):
            arrived(g2.at[n, quarter(((cy, cx)[n] + 4 - d) % 4)], 5 + 2 * d + n)
            across(n, d)

    own = []
    slots = (pl.ds(0, 14), pl.ds(0, 13))
    for n in range(2):
        rows = kg.at[n, slots[n], sixteen(64 * core, (cx, cy)[n]), :]
        own.append(pltpu.make_async_copy(g2.at[n, slots[n]], rows, osem.at[n]))
        own[n].start()
        send(g2.at[n, slots[n]], rows, 11 + n, 19 + n, sibling)
    for d in (1, 3, 2):
        for n in range(2):
            rows = kg.at[n, slots[n], sixteen(64 * core, ((cx, cy)[n] + 4 - d) % 4), :]
            arrived(rows, 11 + 2 * d + n)
            send(rows, rows, 11 + n, 19 + n, sibling)

    sent(q1.at[0], 0)
    sent(q1.at[1, :, pl.ds(0, 13)], 1)
    sent(qs.at[0], 2)
    sent(q2, 3)
    sent(qs.at[1], 4)
    sent(r3.at[pl.ds(0, 7)], 5)
    sent(rscale3.at[pl.ds(0, 7)], 6)
    for ch in range(8):
        @pl.when(there[ch])
        def _():
            halo_copy(rs, rr, hsem, brem, ch).wait_send()
    for copy in own:
        copy.wait()
    for n in range(2):
        sent(g2.at[n, pl.ds(0, 12)], 7 + n)
        sent(kg.at[n, slots[n], pl.ds(0, 48), :], 9 + n)
        sent(kg.at[n, slots[n], pl.ds(0, 64), :], 11 + n)
        arrived(kg.at[n, slots[n], pl.ds(other, 64), :], 19 + n)


def finish(conv, igrad, kg, conv_out, igrad_out, kgrad_out, wide, sem):
    stores = []

    def store(src, dst):
        stores.append(pltpu.make_async_copy(src, dst, sem.at[len(stores)]))
        stores[-1].start()

    store(conv, conv_out)
    store(igrad, igrad_out)
    for s in range(3):
        for n, (matrix, slot, count) in enumerate(RUNS[s]):
            for m in range(count):
                wide[matrix + m] = kg[n, slot + m].T.astype(F32)
        part = pl.ds(9 * s, 9)
        store(wide.at[part], kgrad_out.at[part])
    for copy in stores:
        copy.wait()


def per_device(features, cotangent, kernel, block_count, neighbours, send_face, send_corner):
    vmem = pl.BlockSpec(memory_space=pltpu.VMEM)
    hbm = pl.BlockSpec(memory_space=pltpu.HBM)
    dma = pltpu.SemaphoreType.DMA
    blocks = (32, 64, 128)
    conv, igrad, kg = pl.pallas_call(
        body,
        out_shape=(
            pltpu.VMEM(blocks, BF),
            pltpu.VMEM(blocks, BF),
            pltpu.VMEM((2, 16, 128, 128), BF),
        ),
        in_specs=[hbm] * 6,
        out_specs=(vmem,) * 3,
        scratch_shapes=[
            pltpu.SMEM((1, 4, 8), jnp.int32),
            pltpu.SMEM((1, 2, 4), jnp.int32),
            pltpu.VMEM(blocks, BF),
            pltpu.VMEM(blocks, BF),
            pltpu.VMEM((27, 128, 128), BF),
            pltpu.VMEM((32, 27), jnp.int32),
            pltpu.VMEM((32, 128), F32),
            pltpu.VMEM((64, 80, 128), BF),
            pltpu.VMEM((6, 6, 3, 32, 256), BF),
            pltpu.VMEM((4, 4, 2, 32, 256), BF),
            pltpu.VMEM((256, 1024), BF),
            pltpu.VMEM((2, 3, 256, 256), BF),
            pltpu.VMEM((9, 2, 256, 256), BF),
            pltpu.VMEM((27, 128, 128), F32),
            pltpu.VMEM((6, 6, 3, 32, 256), F32),
            pltpu.VMEM((64, 32, 128), F32),
            pltpu.VMEM((27, 32, 128), BF),
            pltpu.VMEM((27, 80, 256), BF),
            pltpu.VMEM((8, 32, 128), BF),
            pltpu.VMEM((8, 128, 32), BF),
            pltpu.VMEM((4, 4, 2, 32, 256), BF),
            pltpu.VMEM((256, 256), BF),
            pltpu.VMEM((256, 256), BF),
            pltpu.VMEM((256, 256), BF),
            pltpu.VMEM((8, 4, 32, 128), BF),
            pltpu.VMEM((8, 4, 32, 128), BF),
            pltpu.VMEM((8, 4, 32, 128), BF),
            pltpu.VMEM((8, 4, 32, 128), BF),
            pltpu.VMEM((27, 128, 128), F32),
            pltpu.VMEM((27, 64, 128), F32),
            pltpu.VMEM((2, 14, 64, 128), F32),
            pltpu.VMEM((2, 3, 14, 16, 128), jnp.int16),
            pltpu.VMEM((2, 3, 14, 16, 128), jnp.int16),
            pltpu.VMEM((2, 16, 16, 128), F32),
            pltpu.VMEM((2, 3, 4, 16, 128), jnp.int16),
            pltpu.VMEM((2, 3, 4, 16, 128), jnp.int16),
            pltpu.VMEM((2, 2, 3, 8, 128), F32),
            pltpu.VMEM((2, 2, 3, 8, 128), F32),
            pltpu.VMEM((2, 64, 128), F32),
            pltpu.VMEM((128, 128), jnp.int16),
            pltpu.VMEM((8, 128), F32),
            pltpu.VMEM((8, 128, 128), jnp.int16),
            pltpu.VMEM((8, 8, 128), F32),
            pltpu.VMEM((2, 16, 16, 128), BF),
            dma((6,)), dma((2,)), dma((8,)), dma((8,)), dma((8,)),
            dma((3,)), dma((3,)), dma((13,)), dma((21,)),
        ],
        compiler_params=pltpu.CompilerParams(
            collective_id=0, has_side_effects=True, vmem_limit_bytes=52 * 1024 * 1024
        ),
        cost_estimate=pl.CostEstimate(
            flops=7_000_000_000, bytes_accessed=6_000_000, transcendentals=0
        ),
    )(
        send_face,
        jnp.swapaxes(send_corner, 1, 2),
        features.reshape(blocks),
        cotangent.reshape(blocks),
        kernel,
        neighbours,
    )
    conv, igrad, kgrad = pl.pallas_call(
        finish,
        out_shape=(
            jax.ShapeDtypeStruct(blocks, BF),
            jax.ShapeDtypeStruct(blocks, BF),
            jax.ShapeDtypeStruct((27, 128, 128), F32),
        ),
        in_specs=[vmem] * 3,
        out_specs=(hbm, hbm, hbm),
        scratch_shapes=[
            pltpu.VMEM((27, 128, 128), F32),
            dma((5,)),
        ],
        compiler_params=pltpu.CompilerParams(vmem_limit_bytes=32 * 1024 * 1024),
    )(conv, igrad, kg)
    return conv.reshape(2048, 128), igrad.reshape(2048, 128), kgrad


def solution(mesh):
    in_specs = (
        P(("gx", "gy"), None),
        P(("gx", "gy"), None),
        P(),
        P(("gx", "gy")),
        P(("gx", "gy"), None),
        P(("gx", "gy"), None, None),
        P(("gx", "gy"), None, None),
    )
    out_specs = (P(("gx", "gy"), None), P(("gx", "gy"), None), P())
    return jax.shard_map(
        per_device, mesh=mesh, in_specs=in_specs, out_specs=out_specs, check_vma=False
    )
```

```python
import math

import jax
import jax.numpy as jnp
from jax import lax
from jax.experimental import pallas as pl
from jax.experimental.pallas import tpu as pltpu
from jax.sharding import PartitionSpec as P

MESH = pl.DeviceIdType.MESH
BF = jnp.bfloat16
F32 = jnp.float32

NX, NY, NZ = 4, 4, 8
FACE_WAYS = ((-1, 0), (1, 0), (0, -1), (0, 1))
CORNER_WAYS = ((-1, -1), (-1, 1), (1, -1), (1, 1))
WAYS = FACE_WAYS + CORNER_WAYS


RUNS = (
    ((0, 0, 5), (5, 0, 4)),
    ((9, 5, 4), (13, 4, 5)),
    ((18, 9, 5), (23, 9, 4)),
)


def opposite(channel):
    return channel ^ 1 if channel < 4 else 11 - channel


def side(stride):
    return 0 if stride < 0 else 3


def places(local):
    if local == 0:
        return ((1, 0), (5, 1))
    if local == 3:
        return ((4, 0), (0, -1))
    return ((local + 1, 0),)


def kind(local):
    return 0 if local == 0 else (2 if local == 3 else 1)


def readers(ux, uy, uz):
    found = []
    for px, ox in places(ux):
        for py, oy in places(uy):
            for pz, oz in places(uz):
                found.append((px, py, pz, (ox + 1) * 9 + (oy + 1) * 3 + oz + 1))
    return found


def nn(a, b):
    return lax.dot_general(a, b, (((1,), (0,)), ((), ())), preferred_element_type=F32)


def nt(a, b):
    return lax.dot_general(a, b, (((1,), (1,)), ((), ())), preferred_element_type=F32)


def onehot(mask):
    return jnp.where(mask, 1.0, 0.0).astype(BF)


def iota(shape, dim):
    return lax.broadcasted_iota(jnp.int32, shape, dim)


def encode(rows):
    largest = jnp.max(jnp.abs(rows.reshape(-1, 8, 128)), axis=0)
    for step in (4, 2, 1):
        largest = jnp.maximum(largest, pltpu.roll(largest, step, 0))
    largest = jnp.maximum(largest, 1e-33)
    scale = largest * (1.0 / 32000.0)
    inverse = 32000.0 / largest
    coded = jnp.round(rows.reshape(-1, 8, 128) * inverse[None]).reshape(-1, 128)
    return coded.astype(jnp.int32).astype(jnp.int16), scale


def decode(coded, scale):
    rows = coded.astype(jnp.int32).astype(F32).reshape(-1, 8, 128)
    return (rows * scale[None]).reshape(-1, 128)


def body(
    face_in, corner_in, feat_in, cot_in, ker_in, near_in,
    conv, igrad, kg,
    face, corner, feat, cot, ker, near, live,
    et, pz, gz, gt, gty, wt, di, dp, de, oh, oht, bd, bdt, co, perm, pair_perm, part_perm,
    hs, hr, rs, rr,
    wd, rcore, hh, q1, r1, s1, q2, r2, qs, rscale, s2, q3, qs3, r3, rscale3, g2,
    isem, osem, hsem, hrem, brem, csem, crem, asem, arem,
):
    loads = [
        pltpu.make_async_copy(src, dst, isem.at[n])
        for n, (src, dst) in enumerate(
            (
                (face_in, face),
                (corner_in, corner),
                (feat_in, feat),
                (near_in, near),
                (cot_in, cot),
                (ker_in, ker),
            )
        )
    ]
    for copy in loads:
        copy.start()
    gx = lax.axis_index("gx")
    gy = lax.axis_index("gy")
    cy = gx // 16
    cz = (gx // 2) % 8
    cx = (gy // 2) * 2 + gx % 2
    core = gy % 2

    def at(x, y, z, c):
        return ((y * 8 + z) * 2 + x % 2, (x // 2) * 2 + c)

    sibling = (gx, gy // 2 * 2 + (1 - core))
    along_x = [at((cx + d) % NX, cy, cz, core) for d in range(1, NX)]
    along_y = [at(cx, (cy + d) % NY, cz, core) for d in range(1, NY)]
    along_z = [at(cx, cy, (cz + d) % NZ, core) for d in range(1, NZ)]
    halo = [(gx + wx, gy + wy) for wx, wy in WAYS]
    there = [
        (gx + wx >= 0) & (gx + wx < 64) & (gy + wy >= 0) & (gy + wy < 4) for wx, wy in WAYS
    ]

    barrier = pltpu.get_barrier_semaphore()
    greet = [along_z[n] for n in (3, 2, 4, 1, 5, 0, 6)] + along_x + along_y + [sibling]
    expected = len(greet)
    for other in greet:
        pl.semaphore_signal(barrier, inc=1, device_id=other, device_id_type=MESH)
    for ch in (4, 5, 6, 7, 0, 1, 2, 3):
        expected = expected + there[ch].astype(jnp.int32)

        @pl.when(there[ch])
        def _():
            pl.semaphore_signal(barrier, inc=1, device_id=halo[ch], device_id_type=MESH)

    r256, c256 = iota((256, 256), 0), iota((256, 256), 1)
    perm[...] = onehot(((r256 >> 4) == (c256 & 15)) & ((r256 & 15) == (c256 >> 4)))
    pair_perm[...] = onehot(c256 == (r256 & 15) * 16 + ((r256 >> 4) & 7) * 2 + (r256 >> 7))
    part_perm[...] = onehot(c256 == (r256 & 1) * 128 + ((r256 & 15) >> 1) * 16 + (r256 >> 4))
    eye = onehot(iota((128, 128), 0) == iota((128, 128), 1))
    eye256 = onehot(r256 == c256)

    def swap16(v):
        return nn(perm[...], v.reshape(256, 128)).reshape(16, 16, 128)

    r32, c32 = iota((32, 128), 0), iota((32, 128), 1)
    same_z = (r32 >> 3) == (c32 >> 5)
    loads[0].wait()
    loads[1].wait()
    for ch in range(8):
        index = jnp.full((32, 128), -1, jnp.int32)
        for n in range(8 if ch < 4 else 2):
            slot = n if ch < 4 else 2 * (opposite(ch) - 4) + n
            block = face[0, ch, n] if ch < 4 else corner[0, n, ch - 4]
            index = jnp.where((r32 & 7) == slot, block, index)
        pick = onehot(same_z & (index == (c32 & 31)))
        bd[ch] = pick
        bdt[ch] = nt(eye, pick).astype(BF)

    loads[2].wait()
    for hb in range(2):
        for ug in range(4):
            rows = swap16(feat[pl.ds(16 * hb, 16), pl.ds(16 * ug, 16), :])
            et[pl.ds(16 * ug, 16), pl.ds(16 * hb, 16), :] = rows.astype(BF)

    def rim_base(ch, chunk):
        wx, wy = WAYS[ch]
        ux = side(wx) if wx != 0 else chunk
        uy = side(wy) if wy != 0 else chunk
        return ux * 16 + uy * 4

    def chunks(ch):
        return 4 if ch < 4 else 1

    for ch in range(8):
        for chunk in range(chunks(ch)):
            source = et[pl.ds(rim_base(ch, chunk), 4), pl.ds(0, 32), :].reshape(128, 128)
            hs[ch, chunk] = nn(bd[ch], source).astype(BF)

    pl.semaphore_wait(barrier, expected)

    def part(buf, ch):
        return buf.at[ch] if ch < 4 else buf.at[ch, pl.ds(0, 1)]

    def halo_copy(src, dst, ss, rs_, ch):
        return pltpu.make_async_remote_copy(
            src_ref=part(src, ch),
            dst_ref=part(dst, opposite(ch)),
            send_sem=ss.at[ch],
            recv_sem=rs_.at[opposite(ch)],
            device_id=halo[ch],
            device_id_type=MESH,
        )

    def halo_arrived(src, dst, ss, rs_, ch):
        return pltpu.make_async_remote_copy(
            src_ref=part(src, ch),
            dst_ref=part(dst, ch),
            send_sem=ss.at[ch],
            recv_sem=rs_.at[ch],
            device_id=halo[ch],
            device_id_type=MESH,
        )

    for ch in (2, 3, 4, 5, 6, 7, 0, 1):
        @pl.when(there[ch])
        def _():
            halo_copy(hs, hr, hsem, hrem, ch).start()

    loads[3].wait()
    live[...] = jnp.where(near[:, 13:14] == r32, 1.0, 0.0)
    lives = [live[pl.ds(16 * hb, 16), :] for hb in range(2)]
    loads[4].wait()
    for x in range(4):
        for hb in range(2):
            rows = cot[pl.ds(16 * hb, 16), pl.ds(16 * x, 16), :].reshape(256, 128)
            rows = nn(pair_perm[...], rows).reshape(2, 4, 2, 16, 128) * lives[hb]
            for n in range(2):
                gz[x, :, :, pl.ds(16 * hb, 16), pl.ds(128 * n, 128)] = rows[n].astype(BF)
    for x in range(4):
        turned = nt(eye256, gz[x].reshape(256, 256))
        place = pl.ds(256 * x, 256)
        gt[:, place] = turned.astype(BF)
    for n, y in enumerate((0, 3)):
        turned = nt(eye256, gz[:, y].reshape(256, 256))
        gty[n, 0] = jnp.where(c256 < 64, 0.0, turned).astype(BF)
        gty[n, 1] = turned.astype(BF)
        gty[n, 2] = jnp.where(c256 < 192, turned, 0.0).astype(BF)

    for u in range(64):
        et[u, pl.ds(32, 48), :] = jnp.zeros((48, 128), BF)

    columns = c32 + jnp.where(c32 >= 32, 1, 0)
    for o in range(27):
        oh[o] = onehot(near[:, o : o + 1] == columns)

    def offsets_of(tx, ty, tz):
        pick = (0, 1, 3)
        return [r[3] for r in readers(pick[tx], pick[ty], pick[tz])]

    def stacked(offsets):
        if len(offsets) == 1:
            return oh[offsets[0]]
        return jnp.concatenate([oh[o] for o in offsets], axis=0)

    def inner(found):
        return [r for r in found if 1 <= r[0] <= 4 and 1 <= r[1] <= 4]

    def outer_y(found):
        return [r for r in found if 1 <= r[0] <= 4 and not 1 <= r[1] <= 4]

    def outer_x(found):
        return [r for r in found if not 1 <= r[0] <= 4]

    def gather(which):
        for ux in range(4):
            for uy in range(4):
                for uz in range(4):
                    found = which(readers(ux, uy, uz))
                    if found:
                        picks = stacked([r[3] for r in found])[:, :80]
                        keep(nn(picks, et[ux * 16 + uy * 4 + uz]).astype(BF), found)

    def keep(rows, found):
        for n, (px, py, p, _) in enumerate(found):
            pz[px, py, p // 2, :, pl.ds(128 * (p % 2), 128)] = rows[32 * n : 32 * n + 32]

    for py in (0, 5):
        pz[pl.ds(1, 4), py] = jnp.zeros((4, 3, 32, 256), BF)
    for ux in range(4):
        for uy in range(4):
            for uz in range(4):
                found = inner(readers(ux, uy, uz))
                picks = stacked([r[3] for r in found])[:, :32]
                keep(nn(picks, et[ux * 16 + uy * 4 + uz, pl.ds(0, 32)]).astype(BF), found)

    mine = pl.multiple_of(64 * core, 64)
    other = pl.multiple_of(64 - 64 * core, 64)

    def core_copy(s):
        return pltpu.make_async_remote_copy(
            src_ref=wd.at[pl.ds(9 * s, 9), pl.ds(other, 64), :],
            dst_ref=rcore.at[pl.ds(9 * s, 9)],
            send_sem=csem.at[s],
            recv_sem=crem.at[s],
            device_id=sibling,
            device_id_type=MESH,
        )

    def blocks_of(d0, d1):
        return (
            d0[:128, :128] + d0[128:, 128:],
            d0[:128, 128:] + d1[128:, :128],
            d1[:128, :128] + d1[128:, 128:],
        )

    for kx in range(3):
        x0, x1 = ((1, 4), (0, 4), (0, 3))[kx]
        for ky in range(3):
            left = gt[:, pl.ds(256 * x0, 256 * (x1 - x0))]
            sums = [
                nn(
                    left,
                    pz[pl.ds(x0 + kx, x1 - x0), pl.ds(ky, 4), pl.ds(w, 2)].reshape(-1, 256),
                )
                for w in range(2)
            ]
            for n, value in enumerate(blocks_of(*sums)):
                if kx == 1 and ky == 1:
                    wd[9 * kx + 3 * ky + n] = value
                else:
                    di[9 * kx + 3 * ky + n] = value

    def unpack(ch):
        @pl.when(there[ch])
        def _():
            halo_arrived(hs, hr, hsem, hrem, ch).wait_recv()
            wx, wy = WAYS[ch]
            for chunk in range(chunks(ch)):
                ux = side(-wx) if wx != 0 else chunk
                uy = side(-wy) if wy != 0 else chunk
                got = hr[ch, chunk].astype(F32).reshape(4, 8, 128)
                none = jnp.zeros((4, 8, 128), F32)
                pair = (got, none) if ch >= 4 or ch % 2 == 0 else (none, got)
                start = 64 if ch >= 4 else 32 + 16 * (ch // 2)
                et[pl.ds(ux * 16 + uy * 4, 4), pl.ds(start, 16), :] = jnp.concatenate(
                    pair, axis=1
                ).astype(BF)

    def send(src, dst, ns, nr, device):
        pltpu.make_async_remote_copy(
            src_ref=src,
            dst_ref=dst,
            send_sem=asem.at[ns],
            recv_sem=arem.at[nr],
            device_id=device,
            device_id_type=MESH,
        ).start()

    def counted(ref, ns, nr):
        return pltpu.make_async_remote_copy(
            src_ref=ref,
            dst_ref=ref,
            send_sem=asem.at[ns],
            recv_sem=arem.at[nr],
            device_id=sibling,
            device_id_type=MESH,
        )

    def arrived(ref, nr):
        counted(ref, 0, nr).wait_recv()

    def sent(ref, ns):
        counted(ref, ns, 0).wait_send()

    def sixteen(first, index):
        return pl.ds(pl.multiple_of(first + 16 * index, 16), 16)

    def quarter(index):
        return pl.ds(4 * index, 4)

    def core_sum(s):
        core_copy(s).wait()
        for n, (matrix, slot, count) in enumerate(RUNS[s]):
            kept = wd[pl.ds(matrix, count), pl.ds(mine, 64), :]
            hh[n, pl.ds(slot, count)] = kept + rcore[pl.ds(matrix, count)]

    def outer_sums(kx, ky, w):
        total = None
        if ky != 1:
            rows = pz[pl.ds(kx, 4), (0, None, 5)[ky], pl.ds(w, 2)].reshape(256, 256)
            total = nn(gty[ky // 2, kx], rows)
        if kx != 1:
            x, px = ((0, 0), None, (3, 5))[kx]
            rows = pz[px, pl.ds(ky, 4), pl.ds(w, 2)].reshape(256, 256)
            term = nn(gt[:, pl.ds(256 * x, 256)], rows)
            total = term if total is None else total + term
        return total

    def outer_wgrad(s):
        for ky in range(3):
            if s == 1 and ky == 1:
                continue
            value = blocks_of(outer_sums(s, ky, 0), outer_sums(s, ky, 1))
            for n in range(3):
                j = 9 * s + 3 * ky + n
                wd[j] = di[j] + value[n]
        core_copy(s).start()

    for ch in (2, 3):
        unpack(ch)
    gather(outer_y)
    outer_wgrad(1)
    for ch in (4, 5, 6, 7, 0, 1):
        unpack(ch)
    gather(outer_x)
    outer_wgrad(0)
    outer_wgrad(2)
    for s in (1, 0, 2):
        core_sum(s)

    far_first = (2, 1, 3)
    for n in range(2):
        size = (14, 13)[n]
        for d in far_first:
            rows = sixteen(0, ((cx, cy)[n] + d) % 4)
            coded, scale = encode(hh[n, pl.ds(0, size), rows, :].reshape(-1, 128))
            q1[n, d - 1, pl.ds(0, size)] = coded.reshape(size, 16, 128)
            qs[0, n, d - 1] = scale
            device = (along_x, along_y)[n][d - 1]
            send(
                q1.at[n, d - 1, pl.ds(0, size)],
                r1.at[n, d - 1, pl.ds(0, size)],
                n,
                n,
                (along_x, along_y)[n][d - 1],
            )
            send(qs.at[0, n, d - 1], rscale.at[0, n, d - 1], 2, (2, 21)[n], (along_x, along_y)[n][d - 1])

    def weights(j, carry):
        low, mid, high = ker[3 * j], ker[3 * j + 1], ker[3 * j + 2]
        none = jnp.zeros((128, 128), BF)
        wt[j, 0, pl.ds(0, 128), pl.ds(0, 128)] = low
        wt[j, 0, pl.ds(0, 128), pl.ds(128, 128)] = none
        wt[j, 0, pl.ds(128, 128), pl.ds(0, 128)] = mid
        wt[j, 0, pl.ds(128, 128), pl.ds(128, 128)] = low
        wt[j, 1, pl.ds(0, 128), pl.ds(0, 128)] = high
        wt[j, 1, pl.ds(0, 128), pl.ds(128, 128)] = mid
        wt[j, 1, pl.ds(128, 128), pl.ds(0, 128)] = none
        wt[j, 1, pl.ds(128, 128), pl.ds(128, 128)] = high
        return carry

    loads[5].wait()
    lax.fori_loop(0, 9, weights, 0)

    for tx in range(3):
        for ty in range(3):
            for tz in range(3):
                offs = offsets_of(tx, ty, tz)
                flipped = nt(eye[:80], stacked(offs)).astype(BF)
                oht[tx * 9 + ty * 3 + tz, :, pl.ds(0, 32 * len(offs))] = flipped

    def clear_dp(x, carry):
        dp[x] = jnp.zeros((6, 3, 32, 256), F32)
        return carry

    lax.fori_loop(0, 6, clear_dp, 0)

    for px in range(6):
        for ky in range(3):
            for w in range(2):
                term = None
                for kx in range(3):
                    if 0 <= px - kx < 4:
                        one = nt(gz[px - kx].reshape(256, 256), wt[3 * kx + ky, w])
                        term = one if term is None else term + one
                dp[px, pl.ds(ky, 4), pl.ds(w, 2)] += term.reshape(4, 2, 32, 256)

    for n in range(2):
        size = (14, 13)[n]
        arrived(r1.at[n, :, pl.ds(0, size)], n)
        arrived(rscale.at[0, n], (2, 21)[n])
        total = hh[n, pl.ds(0, size), sixteen(0, (cx, cy)[n]), :]
        for d in range(3):
            got = decode(r1[n, d, pl.ds(0, size)].reshape(-1, 128), rscale[0, n, d])
            total = total + got.reshape(size, 16, 128)
        s1[n, pl.ds(0, size)] = total
        s1[n, pl.ds(size, 16 - size)] = jnp.zeros((16 - size, 16, 128), F32)
        for d in far_first:
            coded, scale = encode(s1[n, quarter(((cy, cx)[n] + d) % 4)].reshape(64, 128))
            q2[n, d - 1] = coded.reshape(4, 16, 128)
            qs[1, n, d - 1] = scale
            device = (along_y, along_x)[n][d - 1]
            send(q2.at[n, d - 1], r2.at[n, d - 1], 3, 3, device)
            send(qs.at[1, n, d - 1], rscale.at[1, n, d - 1], 4, 4, device)

    for ux in range(4):
        for uy in range(4):
            pieces = []
            for uz in range(4):
                found = readers(ux, uy, uz)
                high, low = [], []
                for px, py, p, _ in found:
                    value = dp[px, py, p // 2, :, pl.ds(128 * (p % 2), 128)]
                    top = value.astype(BF)
                    high.append(top)
                    low.append((value - top.astype(F32)).astype(BF))
                high = jnp.concatenate(high, axis=0) if len(high) > 1 else high[0]
                low = jnp.concatenate(low, axis=0) if len(low) > 1 else low[0]
                group = kind(ux) * 9 + kind(uy) * 3 + kind(uz)
                res = nn(
                    oht[group, :, pl.ds(0, 32 * len(found))],
                    jnp.concatenate([high, low], axis=1),
                )
                res = res[:, :128] + res[:, 128:]
                de[ux * 16 + uy * 4 + uz] = res[:32]
                pieces.append(res)

            def give(slot, chunk, row):
                rs[slot, chunk] = jnp.concatenate(
                    [piece[row : row + 8] for piece in pieces], axis=0
                ).astype(BF)

            for slot in range(8):
                wx, wy = WAYS[slot]
                if (wx != 0 and ux != side(-wx)) or (wy != 0 and uy != side(-wy)):
                    continue
                chunk = 0 if slot >= 4 else (uy if wx != 0 else ux)
                give(slot, chunk, 64 if slot >= 4 else 32 + 8 * slot)

    for ch in range(8):
        @pl.when(there[ch])
        def _():
            halo_copy(hs, hr, hsem, hrem, ch).wait_send()
            halo_copy(rs, rr, hsem, brem, ch).start()

        @pl.when(jnp.logical_not(there[ch]))
        def _():
            rr[ch] = jnp.zeros((4, 32, 128), BF)

    def convolve(x):
        total = jnp.zeros((256, 256), F32)
        for kx in range(3):
            for ky in range(3):
                for w in range(2):
                    rows = pz[x + kx, pl.ds(ky, 4), pl.ds(w, 2)].reshape(256, 256)
                    total = total + nn(rows, wt[3 * kx + ky, w])
        alive = jnp.concatenate([live[...], live[...]], axis=1)
        co[x] = (total.reshape(4, 2, 32, 256) * alive).astype(BF)
    convolve(0)
    convolve(1)

    arrived(r2, 3)
    arrived(rscale.at[1], 4)
    for n in range(2):
        total = s1[n, quarter((cy, cx)[n])].reshape(64, 128)
        for d in range(3):
            total = total + decode(r2[n, d].reshape(64, 128), rscale[1, n, d])
        s2[n] = total

    coded, scale = encode(s2[...].reshape(128, 128))
    q3[...] = coded
    qs3[...] = scale
    r3[pl.ds(cz, 1)] = coded[None]
    rscale3[pl.ds(cz, 1)] = scale[None]
    for d in (4, 3, 5, 2, 6, 1, 7):
        send(q3, r3.at[cz], 5, 5, along_z[d - 1])
        send(qs3, rscale3.at[cz], 6, 6, along_z[d - 1])

    convolve(2)
    convolve(3)
    for x in range(4):
        for hb in range(2):
            parts = [
                co[x, :, :, pl.ds(16 * hb, 16), pl.ds(128 * n, 128)].reshape(128, 128)
                for n in range(2)
            ]
            rows = nn(part_perm[...], jnp.concatenate(parts, axis=0)).reshape(16, 16, 128)
            conv[pl.ds(16 * hb, 16), pl.ds(16 * x, 16), :] = rows.astype(BF)

    for ch in range(8):
        @pl.when(there[ch])
        def _():
            halo_arrived(rs, rr, hsem, brem, ch).wait_recv()

    for ux in range(4):
        parts = []
        for uy in range(4):
            rows = de[pl.ds(ux * 16 + uy * 4, 4)].reshape(128, 128)
            for ch in range(8):
                wx, wy = WAYS[ch]
                if (wx != 0 and ux != side(wx)) or (wy != 0 and uy != side(wy)):
                    continue
                chunk = 0 if ch >= 4 else (uy if wx != 0 else ux)
                rows = rows + nn(bdt[ch], rr[ch, chunk])
            parts.append(rows.astype(BF).reshape(4, 32, 128))
        parts = jnp.concatenate(parts, axis=0)
        for hb in range(2):
            swapped = swap16(parts[:, 16 * hb : 16 * hb + 16])
            igrad[pl.ds(16 * hb, 16), pl.ds(16 * ux, 16), :] = swapped.astype(BF)

    arrived(r3.at[pl.ds(0, 7)], 5)
    arrived(rscale3.at[pl.ds(0, 7)], 6)
    whole = decode(r3[0], rscale3[0])
    for z in range(1, 8):
        whole = whole + decode(r3[z], rscale3[z])
    whole = (whole * (1.0 / math.sqrt(256 * 32 * 64))).reshape(2, 4, 16, 128).astype(BF)
    g2[0, quarter(cy)] = whole[0]
    g2[1, quarter(cx)] = whole[1]

    def across(n, away):
        index = ((cy, cx)[n] + 4 - away) % 4
        rows = sixteen(64 * core, (cx, cy)[n])

        def go(slots):
            for d in far_first:
                send(
                    g2.at[n, slots],
                    kg.at[n, slots, rows, :],
                    9 + n,
                    11 + 2 * d + n,
                    (along_x, along_y)[n][d - 1],
                )

        @pl.when(index < 3)
        def _():
            go(quarter(index))

        @pl.when(index == 3)
        def _():
            go(pl.ds(12, (2, 1)[n]))

    for d in far_first:
        for n in range(2):
            piece = g2.at[n, quarter((cy, cx)[n])]
            send(piece, piece, 7 + n, 5 + 2 * d + n, (along_y, along_x)[n][d - 1])
    for n in range(2):
        across(n, 0)
    for d in (1, 3, 2):
        for n in range(2):
            arrived(g2.at[n, quarter(((cy, cx)[n] + 4 - d) % 4)], 5 + 2 * d + n)
            across(n, d)

    own = []
    slots = (pl.ds(0, 14), pl.ds(0, 13))
    for n in range(2):
        rows = kg.at[n, slots[n], sixteen(64 * core, (cx, cy)[n]), :]
        own.append(pltpu.make_async_copy(g2.at[n, slots[n]], rows, osem.at[n]))
        own[n].start()
        send(g2.at[n, slots[n]], rows, 11 + n, 19 + n, sibling)
    for d in (1, 3, 2):
        for n in range(2):
            rows = kg.at[n, slots[n], sixteen(64 * core, ((cx, cy)[n] + 4 - d) % 4), :]
            arrived(rows, 11 + 2 * d + n)
            send(rows, rows, 11 + n, 19 + n, sibling)

    sent(q1.at[0], 0)
    sent(q1.at[1, :, pl.ds(0, 13)], 1)
    sent(qs.at[0], 2)
    sent(q2, 3)
    sent(qs.at[1], 4)
    sent(r3.at[pl.ds(0, 7)], 5)
    sent(rscale3.at[pl.ds(0, 7)], 6)
    for ch in range(8):
        @pl.when(there[ch])
        def _():
            halo_copy(rs, rr, hsem, brem, ch).wait_send()
    for copy in own:
        copy.wait()
    for n in range(2):
        sent(g2.at[n, pl.ds(0, 12)], 7 + n)
        sent(kg.at[n, slots[n], pl.ds(0, 48), :], 9 + n)
        sent(kg.at[n, slots[n], pl.ds(0, 64), :], 11 + n)
        arrived(kg.at[n, slots[n], pl.ds(other, 64), :], 19 + n)


def finish(conv, igrad, kg, conv_out, igrad_out, kgrad_out, wide, sem):
    stores = []

    def store(src, dst):
        stores.append(pltpu.make_async_copy(src, dst, sem.at[len(stores)]))
        stores[-1].start()

    store(conv, conv_out)
    store(igrad, igrad_out)
    for s in range(3):
        for n, (matrix, slot, count) in enumerate(RUNS[s]):
            for m in range(count):
                wide[matrix + m] = kg[n, slot + m].T.astype(F32)
        part = pl.ds(9 * s, 9)
        store(wide.at[part], kgrad_out.at[part])
    for copy in stores:
        copy.wait()


def per_device(features, cotangent, kernel, block_count, neighbours, send_face, send_corner):
    vmem = pl.BlockSpec(memory_space=pltpu.VMEM)
    hbm = pl.BlockSpec(memory_space=pltpu.HBM)
    dma = pltpu.SemaphoreType.DMA
    blocks = (32, 64, 128)
    conv, igrad, kg = pl.pallas_call(
        body,
        out_shape=(
            pltpu.VMEM(blocks, BF),
            pltpu.VMEM(blocks, BF),
            pltpu.VMEM((2, 16, 128, 128), BF),
        ),
        in_specs=[hbm] * 6,
        out_specs=(vmem,) * 3,
        scratch_shapes=[
            pltpu.SMEM((1, 4, 8), jnp.int32),
            pltpu.SMEM((1, 2, 4), jnp.int32),
            pltpu.VMEM(blocks, BF),
            pltpu.VMEM(blocks, BF),
            pltpu.VMEM((27, 128, 128), BF),
            pltpu.VMEM((32, 27), jnp.int32),
            pltpu.VMEM((32, 128), F32),
            pltpu.VMEM((64, 80, 128), BF),
            pltpu.VMEM((6, 6, 3, 32, 256), BF),
            pltpu.VMEM((4, 4, 2, 32, 256), BF),
            pltpu.VMEM((256, 1024), BF),
            pltpu.VMEM((2, 3, 256, 256), BF),
            pltpu.VMEM((9, 2, 256, 256), BF),
            pltpu.VMEM((27, 128, 128), F32),
            pltpu.VMEM((6, 6, 3, 32, 256), F32),
            pltpu.VMEM((64, 32, 128), F32),
            pltpu.VMEM((27, 32, 128), BF),
            pltpu.VMEM((27, 80, 256), BF),
            pltpu.VMEM((8, 32, 128), BF),
            pltpu.VMEM((8, 128, 32), BF),
            pltpu.VMEM((4, 4, 2, 32, 256), BF),
            pltpu.VMEM((256, 256), BF),
            pltpu.VMEM((256, 256), BF),
            pltpu.VMEM((256, 256), BF),
            pltpu.VMEM((8, 4, 32, 128), BF),
            pltpu.VMEM((8, 4, 32, 128), BF),
            pltpu.VMEM((8, 4, 32, 128), BF),
            pltpu.VMEM((8, 4, 32, 128), BF),
            pltpu.VMEM((27, 128, 128), F32),
            pltpu.VMEM((27, 64, 128), F32),
            pltpu.VMEM((2, 14, 64, 128), F32),
            pltpu.VMEM((2, 3, 14, 16, 128), jnp.int16),
            pltpu.VMEM((2, 3, 14, 16, 128), jnp.int16),
            pltpu.VMEM((2, 16, 16, 128), F32),
            pltpu.VMEM((2, 3, 4, 16, 128), jnp.int16),
            pltpu.VMEM((2, 3, 4, 16, 128), jnp.int16),
            pltpu.VMEM((2, 2, 3, 8, 128), F32),
            pltpu.VMEM((2, 2, 3, 8, 128), F32),
            pltpu.VMEM((2, 64, 128), F32),
            pltpu.VMEM((128, 128), jnp.int16),
            pltpu.VMEM((8, 128), F32),
            pltpu.VMEM((8, 128, 128), jnp.int16),
            pltpu.VMEM((8, 8, 128), F32),
            pltpu.VMEM((2, 16, 16, 128), BF),
            dma((6,)), dma((2,)), dma((8,)), dma((8,)), dma((8,)),
            dma((3,)), dma((3,)), dma((13,)), dma((22,)),
        ],
        compiler_params=pltpu.CompilerParams(
            collective_id=0, has_side_effects=True, vmem_limit_bytes=52 * 1024 * 1024
        ),
        cost_estimate=pl.CostEstimate(
            flops=7_000_000_000, bytes_accessed=6_000_000, transcendentals=0
        ),
    )(
        send_face,
        jnp.swapaxes(send_corner, 1, 2),
        features.reshape(blocks),
        cotangent.reshape(blocks),
        kernel,
        neighbours,
    )
    conv, igrad, kgrad = pl.pallas_call(
        finish,
        out_shape=(
            jax.ShapeDtypeStruct(blocks, BF),
            jax.ShapeDtypeStruct(blocks, BF),
            jax.ShapeDtypeStruct((27, 128, 128), F32),
        ),
        in_specs=[vmem] * 3,
        out_specs=(hbm, hbm, hbm),
        scratch_shapes=[
            pltpu.VMEM((27, 128, 128), F32),
            dma((5,)),
        ],
        compiler_params=pltpu.CompilerParams(vmem_limit_bytes=32 * 1024 * 1024),
    )(conv, igrad, kg)
    return conv.reshape(2048, 128), igrad.reshape(2048, 128), kgrad


def solution(mesh):
    in_specs = (
        P(("gx", "gy"), None),
        P(("gx", "gy"), None),
        P(),
        P(("gx", "gy")),
        P(("gx", "gy"), None),
        P(("gx", "gy"), None, None),
        P(("gx", "gy"), None, None),
    )
    out_specs = (P(("gx", "gy"), None), P(("gx", "gy"), None), P())
    return jax.shard_map(
        per_device, mesh=mesh, in_specs=in_specs, out_specs=out_specs, check_vma=False
    )
```
